32 devices in a mesh: dp: 8 (over y, x, core), fsdp: 4 (over z).
Axes of the slice: x: 2, y: 2, z: 4, core: 2. Of those that a mesh axis runs over, the one named last changes fastest.
Arguments:
- tokens: bfloat16 [128, 256, 384], P(('dp', 'fsdp')), may hold values from -4 to 4, as said below
- cond: bfloat16 [128, 384], P(('dp', 'fsdp')), may hold values from -4 to 4, as said below
- cotangent: bfloat16 [128, 256, 384], P(('dp', 'fsdp')), may hold values from -4 to 4, as said below
- keep_mask: int32 [128], P(('dp', 'fsdp')), may hold values 0 or 1
- w_ada: bfloat16 [2, 384, 2304], P(None, 'fsdp'), may hold values from -0.20412415 to 0.20412415, as said below
- w_qkv: bfloat16 [2, 384, 1152], P(None, 'fsdp'), may hold values from -0.20412415 to 0.20412415, as said below
- w_proj: bfloat16 [2, 384, 384], P(None, 'fsdp'), may hold values from -1.6329932 to 1.6329932, as said below
- w_up: bfloat16 [2, 384, 1536], P(None, 'fsdp'), may hold values from -0.20412415 to 0.20412415, as said below
- w_down: bfloat16 [2, 1536, 384], P(None, 'fsdp'), may hold values from -0.102062073 to 0.102062073, as said below
Outputs:
- output: bfloat16 [128, 256, 384], P(('dp', 'fsdp'))
- grad_tokens: float32 [128, 256, 384], P(('dp', 'fsdp'))
- grad_cond: float32 [128, 384], P(('dp', 'fsdp'))
- grad_ada: float32 [2, 384, 2304], P(None, 'fsdp')
- grad_qkv: float32 [2, 384, 1152], P(None, 'fsdp')
- grad_proj: float32 [2, 384, 384], P(None, 'fsdp')
- grad_up: float32 [2, 384, 1536], P(None, 'fsdp')
- grad_down: float32 [2, 1536, 384], P(None, 'fsdp')
The draws below stay inside these ranges and needn't reach their ends.
Inputs may be any that keep to these rules, and one draw needn't show every extreme that they name: `tokens`: independent entries of mean zero and deviation one. `cond`: independent entries of mean zero and deviation one. `cotangent`: independent entries of mean zero and deviation one. `w_ada`: independent entries of mean zero and deviation 384^-0.5. `w_qkv`: independent entries of mean zero and deviation 384^-0.5. `w_proj`: independent entries of mean zero. `w_up`: independent entries of mean zero and deviation 384^-0.5. `w_down`: independent entries of mean zero and deviation 1536^-0.5.
All inputs are finite; a program needn't handle non-finite values. No bound on the sum of `keep_mask` on one device may be relied on, other than what follows from the above.
Results may differ from the reference program's by a relative error of at most 0.014.
Values may be sent and summed in bfloat16 or wider, within the bound.
A program may use at most 192 MiB of HBM per device.

```python
import math
import jax
import jax.numpy as jnp
from jax import lax

D = 384
HEADS = 6
FF = 1536
SEQ = 256
BLOCKS = 2
IMG_DEV = 4
IMAGES = 128
N_DP = 8
N_FSDP = 4


def normal_part(key, shape, deviation):
    return jax.random.truncated_normal(key, -4.0, 4.0, shape, jnp.float32) * deviation


def draw_tokens(key, part):
    key = jax.random.fold_in(key, 11)
    shape = (IMG_DEV * N_DP * N_FSDP, SEQ, D)
    return normal_part(key, shape, 1.0).astype(jnp.bfloat16)


def draw_cond(key, part):
    key = jax.random.fold_in(key, 12)
    shape = (IMG_DEV * N_DP * N_FSDP, D)
    return normal_part(key, shape, 1.0).astype(jnp.bfloat16)


def draw_cotangent(key, part):
    key = jax.random.fold_in(key, 13)
    shape = (IMG_DEV * N_DP * N_FSDP, SEQ, D)
    return normal_part(key, shape, 1.0).astype(jnp.bfloat16)


def draw_w_ada(key, part):
    key = jax.random.fold_in(key, 14)
    shape = (BLOCKS, D, 6 * D)
    return normal_part(key, shape, D ** (-0.5)).astype(jnp.bfloat16)


def draw_w_qkv(key, part):
    key = jax.random.fold_in(key, 15)
    shape = (BLOCKS, D, 3 * D)
    return normal_part(key, shape, D ** (-0.5)).astype(jnp.bfloat16)


def draw_w_proj(key, part):
    key = jax.random.fold_in(key, 16)
    shape = (BLOCKS, D, D)
    deviation = max(D // 64, 1) ** (-0.5)
    return normal_part(key, shape, deviation).astype(jnp.bfloat16)


def draw_w_up(key, part):
    key = jax.random.fold_in(key, 17)
    shape = (BLOCKS, D, FF)
    return normal_part(key, shape, D ** (-0.5)).astype(jnp.bfloat16)


def draw_w_down(key, part):
    key = jax.random.fold_in(key, 18)
    shape = (BLOCKS, FF, D)
    return normal_part(key, shape, FF ** (-0.5)).astype(jnp.bfloat16)


def touch_ends(entries, own_key, smallest, top_value):
    longest = entries.shape.index(max(entries.shape))
    spots = []
    for shift in (0, 1):
        where = [jax.random.randint(jax.random.fold_in(own_key, axis), (), 0, length) for axis, length in enumerate(entries.shape)]
        where[longest] = (where[longest] + shift) % entries.shape[longest]
        spots.append(tuple(where))
    return entries.at[spots[0]].set(smallest).at[spots[1]].set(top_value)


def setup_inputs(seed: int = 0) -> dict:
    key_of = jax.random.split(jax.random.key(seed), 10)
    tokens = draw_tokens(jax.random.fold_in(key_of[9], 71), 0)
    cond = draw_cond(jax.random.fold_in(key_of[9], 71), 0)
    cotangent = draw_cotangent(jax.random.fold_in(key_of[9], 71), 0)
    keep_mask = touch_ends((jax.random.randint(key_of[3], (IMAGES,), 0, 4) < 3).astype(jnp.int32), jax.random.fold_in(key_of[3], 1), 0, 1)
    w_ada = draw_w_ada(jax.random.fold_in(key_of[9], 71), 0)
    w_qkv = draw_w_qkv(jax.random.fold_in(key_of[9], 71), 0)
    w_proj = draw_w_proj(jax.random.fold_in(key_of[9], 71), 0)
    w_up = draw_w_up(jax.random.fold_in(key_of[9], 71), 0)
    w_down = draw_w_down(jax.random.fold_in(key_of[9], 71), 0)
    return {"tokens": tokens, "cond": cond, "cotangent": cotangent, "keep_mask": keep_mask, "w_ada": w_ada, "w_qkv": w_qkv, "w_proj": w_proj, "w_up": w_up, "w_down": w_down}


@jax.custom_vjp
def low(v):
    return lax.optimization_barrier(v.astype(jnp.bfloat16)).astype(jnp.float32)

@jax.custom_vjp
def low_back(v):
    return v

def low_keep(v):
    return (low(v), None)

def low_pass(kept, grad):
    return (grad,)

def back_keep(v):
    return (v, None)

def back_low(kept, grad):
    return (low(grad),)
low.defvjp(low_keep, low_pass)
low_back.defvjp(back_keep, back_low)

def modulate(values, shift, scale):
    center = lax.optimization_barrier(jnp.mean(values, axis=-1, keepdims=True))
    centered = values - center
    spread = lax.optimization_barrier(jnp.mean(centered * centered, axis=-1, keepdims=True))
    return centered * lax.rsqrt(spread + 1e-06) * (1.0 + scale[:, None, :]) + shift[:, None, :]

def block(state, cond, w_ada, w_qkv, w_proj, w_up, w_down):
    group, length, width = state.shape
    head_size = width // HEADS
    highest = lax.Precision.HIGHEST
    cond_act = low(jax.nn.silu(cond))
    modulation = low_back(jnp.einsum('gd,de->ge', cond_act, w_ada, precision=highest))
    pieces = jnp.split(modulation, 6, axis=1)
    first_in = low(modulate(state, pieces[0], pieces[1]))
    qkv = low(low_back(jnp.einsum('gld,de->gle', first_in, w_qkv, precision=highest)))
    qkv = qkv.reshape(group, length, 3, HEADS, head_size)
    queries = qkv[:, :, 0]
    key_rows = qkv[:, :, 1]
    values = qkv[:, :, 2]
    scores = low_back(jnp.einsum('gqhe,gkhe->ghqk', queries, key_rows, precision=highest) * head_size ** (-0.5))
    probs = low(jax.nn.softmax(scores, axis=-1))
    mixed = jnp.einsum('ghqk,gkhe->gqhe', probs, values, precision=highest)
    mixed = low(low_back(mixed)).reshape(group, length, width)
    attended = low_back(jnp.einsum('gld,de->gle', mixed, w_proj, precision=highest))
    middle = state + pieces[2][:, None, :] * attended
    second_in = low(modulate(middle, pieces[3], pieces[4]))
    hidden_pre = low_back(jnp.einsum('gld,df->glf', second_in, w_up, precision=highest))
    activated = low(jax.nn.gelu(hidden_pre, approximate=True))
    branch_out = low_back(jnp.einsum('glf,fd->gld', activated, w_down, precision=highest))
    return middle + pieces[5][:, None, :] * branch_out

def forward(state, cond, weights):
    for index in range(BLOCKS):
        state = block(state, cond, *(w[index] for w in weights))
    return state

def reference(tokens, cond, cotangent, keep_mask, w_ada, w_qkv, w_proj, w_up, w_down):
    images = tokens.shape[0]
    group = math.gcd(images, max(1, 4096 // SEQ))
    rounds = images // group
    weights = tuple((w.astype(jnp.float32) for w in (w_ada, w_qkv, w_proj, w_up, w_down)))
    tok_groups = tokens.astype(jnp.float32).reshape(rounds, group, SEQ, D)
    cond_groups = cond.astype(jnp.float32).reshape(rounds, group, D)
    cot_groups = cotangent.astype(jnp.float32).reshape(rounds, group, SEQ, D)
    mask_groups = keep_mask.astype(jnp.float32).reshape(rounds, group)

    def step(totals, item):
        tok_g, cond_g, cot_g, mask_g = item
        result, pull = jax.vjp(forward, tok_g, cond_g, weights)
        d_tok, d_cond, d_weights = pull(cot_g * mask_g[:, None, None])
        totals = jax.tree.map(lambda left, right: left + right, totals, d_weights)
        return (totals, (result.astype(jnp.bfloat16), d_tok, d_cond))
    zeros = tuple((jnp.zeros(w.shape, jnp.float32) for w in weights))
    totals, (result, d_tok, d_cond) = lax.scan(step, zeros, (tok_groups, cond_groups, cot_groups, mask_groups))
    return (result.reshape(images, SEQ, D), d_tok.reshape(images, SEQ, D), d_cond.reshape(images, D), totals[0], totals[1], totals[2], totals[3], totals[4])
```

```python
import functools

import jax
import jax.numpy as jnp
from jax import lax
from jax.experimental import pallas as pl
from jax.experimental.pallas import tpu as pltpu
from jax.sharding import PartitionSpec as P

MESH = pl.DeviceIdType.MESH
bf, f32 = jnp.bfloat16, jnp.float32
HEADS = 6
GROUP = 8
NN = (((1,), (0,)), ((), ()))
NT = (((1,), (1,)), ((), ()))
TN = (((0,), (0,)), ((), ()))
GELU_A = 0.7978845608028654
GELU_B = GELU_A * 0.044715


def dot(a, b, dims=NN):
    return lax.dot_general(a, b, dims, preferred_element_type=f32)


def exact_dot(a, b, dims=NN):
    return lax.dot_general(a, b, dims, precision=lax.Precision.HIGHEST, preferred_element_type=f32)


def one_hot(shape, hit):
    r = lax.broadcasted_iota(jnp.int32, shape, 0)
    c = lax.broadcasted_iota(jnp.int32, shape, 1)
    return jnp.where(hit(r, c), 1.0, 0.0)


def norm_hat(v):
    c = v - jnp.mean(v, -1, keepdims=True)
    r = lax.rsqrt(jnp.mean(c * c, -1, keepdims=True) + 1e-6)
    return c * r, r


def norm_back(dx, hat, r):
    return r * (dx - jnp.mean(dx, -1, keepdims=True) - hat * jnp.mean(dx * hat, -1, keepdims=True))


class Refs:
    pass


def scratch(F, I, L, D, FF, B):
    T = I * L
    R = D // F // 2
    return dict(
        wq=((B, F, 2, R, FF), bf),
        wu=((B, F, 2, R, FF), bf),
        wd=((B, F, 4, 2, R, D), bf),
        wa=((B, D // F, 6 * D), bf),
        tk=((T, D), bf),
        x1=((T, D), f32),
        fi=((B, T, D), bf),
        qkv=((B, T, 3 * D), bf),
        pt=((B, I * HEADS, L, L), bf),
        mt=((B, D, T), bf),
        att=((B, T, D), bf),
        mid=((B, T, D), f32),
        si=((B, T, D), bf),
        hid=((B, T, FF), bf),
        br=((B, T, D), bf),
        g=((T, D), f32),
        db=((T, D), bf),
        act=((T, FF), bf),
        da=((T, D), bf),
        os=((T, D), bf),
        mod=((B, 6 * I, D), f32),
        dm=((B, 32, D), f32),
        cd=((I, D), bf),
        gc=((8, D), f32),
        ms=((B, F, 24, D), f32),
        mr=((B, F, 24, D), f32),
        cg=((4, 2, F, 16, D), bf),
        dg=((B, 2, 4, 2, F, 16, D), bf),
        cs=((F, 8, D), f32),
        cr=((F, 8, D), f32),
        gq=((F, 2, R, FF), bf),
        gu=((F, 2, R, FF), bf),
        gd=((F, 4, 2, R, D), bf),
        hq=((B, F, R, FF), bf),
        hu=((B, F, R, FF), bf),
        hd=((B, F, 4, R, D), bf),
        qr=((B, 3, 3, F, R, D), bf),
        qs=((B, 3, F, R, D), bf),
        zr=((B, 3, F, R, D), bf),
        oq=((B, 2, R, FF), bf),
        ou=((B, 2, R, FF), bf),
        od=((B, 4, 2, R, D), bf),
    )


INPUTS = ("tokens", "cond", "cotangent", "mask", "ada", "qkv_w", "proj_w", "up_w", "down_w")
OUTPUTS = ("output", "grad_tokens", "grad_cond", "grad_ada", "grad_q", "grad_u", "grad_d")
N_SEMS = 256


def kernel(names, F, I, L, D, FF, B, *refs):
    n_in, n_out = len(INPUTS), len(OUTPUTS)
    inp, out, k = Refs(), Refs(), Refs()
    for name, ref in zip(INPUTS, refs[:n_in]):
        setattr(inp, name, ref)
    for name, ref in zip(OUTPUTS, refs[n_in : n_in + n_out]):
        setattr(out, name, ref)
    for name, ref in zip(names, refs[n_in + n_out :]):
        setattr(k, name, ref)
    sems, local_sems = refs[-2], refs[-1]
    R = D // F // 2
    HS = D // HEADS
    KINDS = ("q", "u", "d")

    me, f = lax.axis_index("dp"), lax.axis_index("fsdp")
    e = me % GROUP
    base = me - e
    c, q = e % 2, e // 2
    other = 1 - c
    z_peer = [(f + r) % F for r in range(F)]
    q_peer = [(q + j) % 4 for j in range(4)]

    def at_z(r):
        return (me, z_peer[r])

    def at_q(j):
        return (base + 2 * q_peer[j] + c, f)

    at_c = (base + 2 * q + other, f)

    def rows(i, n=L):
        return pl.ds(pl.multiple_of(i * n, n), n)

    def quarter(j):
        return pl.ds(pl.multiple_of(q_peer[j] * D, D), D)

    index = {}

    def sem(key):
        return sems.at[index.setdefault(key, len(index))]

    pending = []

    def send(key, src, dst, to):
        pltpu.make_async_remote_copy(
            src_ref=src,
            dst_ref=dst,
            send_sem=sem(("send",) + key),
            recv_sem=sem(("recv",) + key),
            device_id=to,
            device_id_type=MESH,
        ).start()

    def wait(kind, key, like):
        pltpu.make_async_copy(like, like, sem((kind,) + key)).wait()

    local_index = {}

    def local(key, src, dst):
        copy = pltpu.make_async_copy(
            src, dst, local_sems.at[local_index.setdefault(key, len(local_index))]
        )
        return copy

    whole = {"q": k.wq, "u": k.wu, "d": k.wd}

    def w_piece(b, w, fz, qi, ci):
        if w == "d":
            return k.wd.at[b, fz, qi, ci]
        return whole[w].at[b, fz, ci, :, pl.ds(pl.multiple_of(qi * D, D), D)]

    def w_half(b, w, fz, ci):
        if w == "d":
            return k.wd.at[b, fz, :, ci]
        return whole[w].at[b, fz, ci]

    def w_like(b, w, n):
        if w == "d":
            return k.wd.at[b, pl.ds(0, n // 3), pl.ds(0, 3), 0] if n % 3 == 0 else k.wd.at[b, 0, pl.ds(0, n), 0]
        return whole[w].at[b, pl.ds(0, n // 3), 0, :, pl.ds(0, 3 * D)] if n % 3 == 0 else whole[w].at[b, 0, 0, :, pl.ds(0, n * D)]

    def w_z(b, w):
        for r in range(1, F):
            send(("wz", b, w), w_piece(b, w, f, q, c), w_piece(b, w, f, q, c), at_z(r))

    def w_zq(b, w):
        wait("recv", ("wz", b, w), w_like(b, w, F - 1))
        for j in range(1, 4):
            for r in range(1, F):
                p = w_piece(b, w, z_peer[r], q, c)
                send(("wq", b, w), p, p, at_q(j))

    def w_qc(b, w):
        wait("recv", ("wq", b, w), w_like(b, w, 3 * (F - 1)))
        for r in range(1, F):
            p = w_half(b, w, z_peer[r], c)
            send(("wc", b, w), p, p, at_c)

    def w_ready(b, w):
        wait("recv", ("wc", b, w), w_like_halves(b, w))

    def w_like_halves(b, w):
        return k.wd.at[b, pl.ds(0, F - 1), :, 0] if w == "d" else whole[w].at[b, pl.ds(0, F - 1), 0]

    def w_sent():
        for b in range(B):
            for w in KINDS:
                wait("send", ("wz", b, w), w_like(b, w, F - 1))
                wait("send", ("wq", b, w), w_like(b, w, 3 * (F - 1)))
                wait("send", ("wc", b, w), w_like_halves(b, w))

    def cols():
        return one_hot((D, D // F), lambda r, s: r == f * (D // F) + s)

    def cond_start():
        v = k.cd[...].astype(f32)
        a = v / (1.0 + jnp.exp(-v))
        k.cg[q, c, f] = jnp.concatenate([a] * 4, axis=0).astype(bf)
        for r in range(1, F):
            send(("cz",), k.cg.at[q, c, f], k.cg.at[q, c, f], at_z(r))

    def cond_zq():
        for j in range(1, 4):
            send(("cq",), k.cg.at[q, c], k.cg.at[q, c], at_q(j))

    def cond_qc():
        wait("recv", ("cq",), k.cg.at[pl.ds(0, 3), 0])
        send(("cc",), k.cg.at[:, c], k.cg.at[:, c], at_c)

    def cond_ready():
        wait("recv", ("cc",), k.cg.at[:, 0])

    def tile_mask(n, p):
        r = lax.broadcasted_iota(jnp.int32, (n, 1), 0)
        return jnp.where((r // 4) % 4 == p, 1.0, 0.0)

    def mod_partial(b):
        a = dot(k.cg[q, c].reshape(F * 16, D), cols().astype(bf))
        lo, hi = (a * tile_mask(F * 16, 0)).astype(bf), (a * tile_mask(F * 16, 1)).astype(bf)
        for s in range(3):
            t = dot(lo, k.wa[b, :, 2 * s * D : (2 * s + 1) * D]) + dot(hi, k.wa[b, :, (2 * s + 1) * D : (2 * s + 2) * D])
            k.ms[b, :, 8 * s : 8 * s + 8, :] = t.reshape(F, 16, D)[:, :8]
        for r in range(1, F):
            send(("mz", b), k.ms.at[b, z_peer[r]], k.mr.at[b, f], at_z(r))

    def mod_ready(b):
        wait("recv", ("mz", b), k.mr.at[b, pl.ds(0, F - 1)])
        total = k.ms[b, f]
        for r in range(1, F):
            total = total + k.mr[b, z_peer[r]]
        k.mod[b] = total

    def piece(b, i, p):
        return k.mod[b, pl.ds(p * I + i, 1), :]

    def dm_row(b, i, p, v):
        at = (p - 2) * I if p >= 2 else 16 + p * I
        k.dm[b, pl.ds(at + i, 1), :] = v

    def dm_start(b, late):
        k.dg[b, late, q, c, f] = k.dm[b, 16 * late : 16 * late + 16].astype(bf)
        for r in range(1, F):
            p = k.dg.at[b, late, q, c, f]
            send(("dz", b, late), p, p, at_z(r))

    def dm_zq(b, late):
        wait("recv", ("dz", b, late), k.dg.at[b, late, 0, 0, pl.ds(0, F - 1)])
        for j in range(1, 4):
            p = k.dg.at[b, late, q, c]
            send(("dq", b, late), p, p, at_q(j))

    def dm_qc(b, late):
        wait("recv", ("dq", b, late), k.dg.at[b, late, pl.ds(0, 3), 0])
        p = k.dg.at[b, late, :, c]
        send(("dc", b, late), p, p, at_c)

    def dm_ready(b, late):
        wait("recv", ("dc", b, late), k.dg.at[b, late, :, 0])

    def dcond_part(b, late):
        t = k.dg[b, late, q, c].reshape(F * 16, D).astype(f32)
        acc = None
        for p in range(2 if late else 4):
            at = (p if late else p + 2) * D
            o = dot((t * tile_mask(F * 16, p)).astype(bf), k.wa[b, :, at : at + D], NT)
            acc = o if acc is None else acc + o
        return acc

    def dcond_send():
        acc = dcond_part(0, 0) + dcond_part(0, 1) + dcond_part(1, 0) + dcond_part(1, 1)
        fold = one_hot((F * 8, F * 16), lambda r, s: (r // 8 == s // 16) & (r % 8 == s % 4))
        t = exact_dot(exact_dot(fold, acc), cols(), NT)
        k.cs[...] = t.reshape(F, 8, D)
        for r in range(1, F):
            send(("gz",), k.cs.at[z_peer[r]], k.cr.at[f], at_z(r))

    def dcond_finish():
        wait("recv", ("gz",), k.cr.at[pl.ds(0, F - 1)])
        total = k.cs[f]
        for r in range(1, F):
            total = total + k.cr[z_peer[r]]
        v = k.cd[...].astype(f32)
        s = 1.0 / (1.0 + jnp.exp(-v))
        k.gc[:I] = total[:I] * (s * (1.0 + v * (1.0 - s)))
        local(("grad_cond",), k.gc.at[pl.ds(0, I)], out.grad_cond).start()

    def grad_ada(b, late):
        n = GROUP * F * 16
        a = dot(k.cg[...].reshape(n, D), cols().astype(bf))
        t = k.dg[b, late].reshape(n, D)
        stage = (k.mid.at[1], k.x1)[b]
        for p in range(2 if late else 4):
            m = p if late else p + 2
            at = pl.ds(m * (D // F), D // F)
            stage[at, :] = dot((a * tile_mask(n, p)).astype(bf), t, TN)
            local(("ada", b, m), stage.at[at], out.grad_ada.at[b, :, pl.ds(m * D, D)]).start()

    grads = {"q": k.gq, "u": k.gu, "d": k.gd}
    halves = {"q": k.hq, "u": k.hu, "d": k.hd}
    results = {"q": k.oq, "u": k.ou, "d": k.od}
    outs = {"q": out.grad_q, "u": out.grad_u, "d": out.grad_d}
    number = {"q": 0, "u": 1, "d": 2}

    def g_half(w, ci):
        return grads[w].at[:, :, ci] if w == "d" else grads[w].at[:, ci]

    def h_quarter(b, w, j):
        return k.hd.at[b, :, q_peer[j]] if w == "d" else halves[w].at[b, :, :, quarter(j)]

    def r_piece(b, w):
        return k.od.at[b, q, c] if w == "d" else results[w].at[b, c, :, quarter(0)]

    def r_half(b, w, ci):
        return k.od.at[b, :, ci] if w == "d" else results[w].at[b, ci]

    def g_c(b, w):
        send(("gc", b, w), g_half(w, other), halves[w].at[b], at_c)

    def g_cq(b, w):
        wait("recv", ("gc", b, w), halves[w].at[b])
        wait("send", ("gc", b, w), halves[w].at[b])

        def add(n, _):
            own = k.gd[n, :, c] if w == "d" else grads[w][n, c]
            halves[w][b, n] = (halves[w][b, n].astype(f32) + own.astype(f32)).astype(bf)
            return 0

        lax.fori_loop(0, F, add, 0)
        for j in range(1, 4):
            send(("gq", b, w), h_quarter(b, w, j), k.qr.at[b, number[w], j - 1], at_q(j))

    def g_qz(b, w):
        m = number[w]
        wait("recv", ("gq", b, w), k.qr.at[b, m])

        def add(n, _):
            own = k.hd[b, n, q] if w == "d" else halves[w][b, n, :, quarter(0)]
            total = own.astype(f32)
            for j in range(3):
                total = total + k.qr[b, m, j, n].astype(f32)
            k.qs[b, m, n] = total.astype(bf)
            return 0

        lax.fori_loop(0, F, add, 0)
        for r in range(1, F):
            send(("gz", b, w), k.qs.at[b, m, z_peer[r]], k.zr.at[b, m, f], at_z(r))

    def g_zq(b, w):
        m = number[w]
        wait("recv", ("gz", b, w), k.zr.at[b, m, pl.ds(0, F - 1)])
        total = k.qs[b, m, f].astype(f32)
        for r in range(1, F):
            total = total + k.zr[b, m, z_peer[r]].astype(f32)
        total = total.astype(bf)
        if w == "d":
            k.od[b, q, c] = total
        else:
            results[w][b, c, :, quarter(0)] = total
        for j in range(1, 4):
            send(("rq", b, w), r_piece(b, w), r_piece(b, w), at_q(j))

    def g_qc(b, w):
        wait("recv", ("rq", b, w), k.qr.at[b, number[w], 0, pl.ds(0, 3)])
        send(("rc", b, w), r_half(b, w, c), r_half(b, w, c), at_c)

    def g_done(b, w):
        wait("recv", ("rc", b, w), r_half(b, w, 0))
        local(("out", b, w), results[w].at[b], outs[w].at[b]).start()

    def rest_sent():
        wait("send", ("cz",), k.cg.at[0, 0, pl.ds(0, F - 1)])
        wait("send", ("cq",), k.cg.at[pl.ds(0, 3), 0])
        wait("send", ("cc",), k.cg.at[:, 0])
        wait("send", ("gz",), k.cs.at[pl.ds(0, F - 1)])
        for b in range(B):
            wait("send", ("mz", b), k.ms.at[b, pl.ds(0, F - 1)])
            for late in range(2):
                wait("send", ("dz", b, late), k.dg.at[b, late, 0, 0, pl.ds(0, F - 1)])
                wait("send", ("dq", b, late), k.dg.at[b, late, pl.ds(0, 3), 0])
                wait("send", ("dc", b, late), k.dg.at[b, late, :, 0])
            for w in KINDS:
                m = number[w]
                wait("send", ("gq", b, w), k.qr.at[b, m])
                wait("send", ("gz", b, w), k.zr.at[b, m, pl.ds(0, F - 1)])
                wait("send", ("rq", b, w), k.qr.at[b, m, 0, pl.ds(0, 3)])
                wait("send", ("rc", b, w), r_half(b, w, 0))

    def m_qkv(b):
        return k.wq[b, :, :, :, : 3 * D].reshape(D, 3 * D)

    def m_proj(b):
        return k.wq[b, :, :, :, 3 * D :].reshape(D, D)

    def m_up(b, at, n):
        return k.wu[b, :, :, :, at : at + n].reshape(D, n)

    def m_down(b):
        return k.wd[b].reshape(FF, D)

    def state(b, r):
        return k.tk[r, :].astype(f32) if b == 0 else k.x1[r, :]

    def lane_masks():
        lane = lax.broadcasted_iota(jnp.int32, (1, 2 * HS), 1)
        lo = jnp.where(lane < HS, 1.0, 0.0)
        return lo.astype(bf), (1.0 - lo).astype(bf)

    def fwd_attention(b, i):
        r = rows(i)
        x = state(b, r)
        hat, _ = norm_hat(x)
        first = (hat * (1.0 + piece(b, i, 1)) + piece(b, i, 0)).astype(bf)
        k.fi[b, r, :] = first
        qkv = dot(first, m_qkv(b))
        qs = (qkv[:, :D] * HS**-0.5).astype(bf)
        ks = qkv[:, D : 2 * D].astype(bf)
        vs = qkv[:, 2 * D :].astype(bf)
        k.qkv[b, r, :D] = qs
        k.qkv[b, r, D : 2 * D] = ks
        k.qkv[b, r, 2 * D :] = vs
        vt = vs.T
        masks = lane_masks()
        mixed = []
        for h in range(HEADS):
            s = slice((h // 2) * 2 * HS, (h // 2 + 1) * 2 * HS)
            scores = dot(ks[:, s] * masks[h % 2], qs[:, s], NT)
            ex = jnp.exp(scores - jnp.max(scores, axis=0, keepdims=True))
            probs = (ex * (1.0 / jnp.sum(ex, axis=0, keepdims=True))).astype(bf)
            k.pt[b, i * HEADS + h] = probs
            mixed.append(dot(vt[h * HS : (h + 1) * HS], probs))
        mt = jnp.concatenate(mixed, axis=0).astype(bf)
        k.mt[b, :, r] = mt
        att = dot(mt, m_proj(b), TN)
        k.att[b, r, :] = att.astype(bf)
        mid = x + piece(b, i, 2) * att
        k.mid[b, r, :] = mid
        hat, _ = norm_hat(mid)
        k.si[b, r, :] = (hat * (1.0 + piece(b, i, 4)) + piece(b, i, 3)).astype(bf)

    def fwd_mlp(b, i):
        r = rows(i)
        second = k.si[b, r, :]
        n = FF // 3
        acc = None
        for j in range(3):
            x = dot(second, m_up(b, j * n, n))
            k.hid[b, r, j * n : (j + 1) * n] = x.astype(bf)
            a = (x * (0.5 * jnp.tanh(x * (GELU_A + GELU_B * (x * x))) + 0.5)).astype(bf)
            o = dot(a, m_down(b)[j * n : (j + 1) * n])
            acc = o if acc is None else acc + o
        k.br[b, r, :] = acc.astype(bf)
        y = k.mid[b, r, :] + piece(b, i, 5) * acc
        if b < B - 1:
            k.x1[r, :] = y
        else:
            k.os[r, :] = y.astype(bf)
            k.g[r, :] = k.db[r, :].astype(f32) * inp.mask[i].astype(f32)

    def bwd_mlp(b, i):
        r = rows(i)
        g = k.g[r, :]
        dm_row(b, i, 5, jnp.sum(g * k.br[b, r, :].astype(f32), axis=0, keepdims=True))
        db = (g * piece(b, i, 5)).astype(bf)
        k.db[r, :] = db
        n = FF // 3
        acc = None
        for j in range(3):
            s = slice(j * n, (j + 1) * n)
            da = dot(db, m_down(b)[s], NT)
            x = k.hid[b, r, s].astype(f32)
            x2 = x * x
            t = jnp.tanh(x * (GELU_A + GELU_B * x2))
            h = 0.5 * t + 0.5
            a = x * h
            k.act[r, s] = a.astype(bf)
            dh = ((a * (1.0 - t) * (GELU_A + (3 * GELU_B) * x2) + h) * da).astype(bf)
            k.hid[b, r, s] = dh
            o = dot(dh, m_up(b, j * n, n), NT)
            acc = o if acc is None else acc + o
        hat, rs = norm_hat(k.mid[b, r, :])
        dm_row(b, i, 3, jnp.sum(acc, axis=0, keepdims=True))
        dm_row(b, i, 4, jnp.sum(acc * hat, axis=0, keepdims=True))
        d_mid = g + norm_back(acc * (1.0 + piece(b, i, 4)), hat, rs)
        k.g[r, :] = d_mid
        dm_row(b, i, 2, jnp.sum(d_mid * k.att[b, r, :].astype(f32), axis=0, keepdims=True))
        k.da[r, :] = (d_mid * piece(b, i, 2)).astype(bf)

    def grad_down(b):
        k.gd[...] = dot(k.act[...], k.db[...], TN).astype(bf).reshape(F, 4, 2, R, D)

    def grad_up(b):
        k.gu[...] = dot(k.si[b], k.hid[b], TN).astype(bf).reshape(F, 2, R, FF)

    def grad_proj(b):
        k.gq[:, :, :, 3 * D :] = dot(k.mt[b], k.da[...]).astype(bf).reshape(F, 2, R, D)

    def grad_qkv(b):
        k.gq[:, :, :, : 3 * D] = dot(k.fi[b], k.qkv[b], TN).astype(bf).reshape(F, 2, R, 3 * D)

    def bwd_attention(b, i):
        r = rows(i)
        do = dot(k.da[r, :], m_proj(b), NT).astype(bf)
        qs = k.qkv[b, r, :D]
        ks = k.qkv[b, r, D : 2 * D]
        vs = k.qkv[b, r, 2 * D :]
        kt = ks.T
        masks = lane_masks()
        dq = []
        for p in range(HEADS // 2):
            s = slice(p * 2 * HS, (p + 1) * 2 * HS)
            dv = dk = None
            for m in range(2):
                h = 2 * p + m
                probs = k.pt[b, i * HEADS + h]
                dp = dot(vs[:, s] * masks[m], do[:, s], NT)
                pf = probs.astype(f32)
                w = pf * dp
                ds = (w - pf * jnp.sum(w, axis=0, keepdims=True)).astype(bf)
                o = dot(probs, do[:, s] * masks[m])
                dv = o if dv is None else dv + o
                o = dot(ds, qs[:, s] * masks[m])
                dk = o if dk is None else dk + o
                dq.append(dot(kt[h * HS : (h + 1) * HS], ds))
            k.qkv[b, r, D + p * 2 * HS : D + (p + 1) * 2 * HS] = dk.astype(bf)
            k.qkv[b, r, 2 * D + p * 2 * HS : 2 * D + (p + 1) * 2 * HS] = dv.astype(bf)
        k.qkv[b, r, :D] = (jnp.concatenate(dq, axis=0) * HS**-0.5).astype(bf).T

    def bwd_first(b, i):
        r = rows(i)
        acc = dot(k.qkv[b, r, :], m_qkv(b), NT)
        hat, rs = norm_hat(state(b, r))
        dm_row(b, i, 0, jnp.sum(acc, axis=0, keepdims=True))
        dm_row(b, i, 1, jnp.sum(acc * hat, axis=0, keepdims=True))
        k.g[r, :] = k.g[r, :] + norm_back(acc * (1.0 + piece(b, i, 1)), hat, rs)

    def images(fn, b, tasks={}):
        def step(i, _):
            for at, todo in tasks.items():
                pl.when(i == at)(functools.partial(run, todo))
            fn(b, i)
            return 0

        lax.fori_loop(0, I, step, 0)

    def run(todo):
        for fn, *args in todo:
            fn(*args)

    loads = [
        local(("cd",), inp.cond, k.cd),
        local(("wa",), inp.ada, k.wa),
        local(("wq",), inp.qkv_w, k.wq.at[:, f, :, :, pl.ds(0, 3 * D)]),
        local(("wp",), inp.proj_w, k.wq.at[:, f, :, :, pl.ds(3 * D, D)]),
        local(("tk",), inp.tokens, k.tk),
        local(("wu",), inp.up_w, k.wu.at[:, f]),
        local(("wd",), inp.down_w, k.wd.at[:, f]),
        local(("db",), inp.cotangent, k.db),
    ]
    for copy in loads:
        copy.start()
    k.dm[...] = jnp.zeros_like(k.dm)

    barrier = pltpu.get_barrier_semaphore()
    everyone = [at_z(r) for r in range(1, F)] + [at_q(j) for j in range(1, 4)] + [at_c]
    for peer in everyone:
        pl.semaphore_signal(barrier, inc=1, device_id=peer, device_id_type=MESH)
    pl.semaphore_wait(barrier, len(everyone))

    for copy in loads:
        copy.wait()
    cond_start()
    w_z(0, "q")
    wait("recv", ("cz",), k.cg.at[0, 0, pl.ds(0, F - 1)])
    mod_partial(0)
    w_z(0, "u")
    w_z(0, "d")
    w_zq(0, "q")
    mod_partial(1)
    w_z(1, "q")
    mod_ready(0)
    w_zq(0, "u")
    w_qc(0, "q")
    w_zq(0, "d")
    w_ready(0, "q")
    images(
        fwd_attention,
        0,
        {
            0: [(w_z, 1, "u"), (w_z, 1, "d"), (cond_zq,)],
            1: [(w_qc, 0, "u"), (w_zq, 1, "q")],
            2: [(mod_ready, 1), (w_zq, 1, "u")],
            3: [(w_qc, 0, "d"), (cond_qc,), (w_zq, 1, "d")],
        },
    )
    run([(w_ready, 0, "u"), (w_ready, 0, "d")])
    images(fwd_mlp, 0, {0: [(w_qc, 1, "q")], 2: [(cond_ready,)]})
    w_ready(1, "q")
    images(fwd_attention, 1, {1: [(w_qc, 1, "u")], 3: [(w_qc, 1, "d")]})
    run([(w_ready, 1, "u"), (w_ready, 1, "d")])
    images(fwd_mlp, 1)
    local(("os",), k.os, out.output).start()

    images(bwd_mlp, 1)
    grad_down(1)
    g_c(1, "d")
    dm_start(1, 0)
    grad_up(1)
    g_c(1, "u")
    grad_proj(1)
    images(bwd_attention, 1, {0: [(g_cq, 1, "d")], 1: [(g_cq, 1, "u"), (dm_zq, 1, 0)]})
    grad_qkv(1)
    g_c(1, "q")
    images(bwd_first, 1, {1: [(g_qz, 1, "d")], 2: [(g_cq, 1, "q")], 3: [(dm_qc, 1, 0)]})
    dm_start(1, 1)
    images(
        bwd_mlp,
        0,
        {
            0: [(g_zq, 1, "d"), (dm_ready, 1, 0)],
            1: [(g_qz, 1, "u"), (dm_zq, 1, 1)],
            2: [(g_qc, 1, "d")],
            3: [(g_zq, 1, "u")],
        },
    )
    grad_down(0)
    g_c(0, "d")
    dm_start(0, 0)
    grad_up(0)
    g_c(0, "u")
    grad_proj(0)
    images(
        bwd_attention,
        0,
        {
            0: [(g_cq, 0, "d"), (g_qz, 1, "q"), (g_done, 1, "d"), (dm_qc, 1, 1)],
            1: [(g_cq, 0, "u"), (g_qc, 1, "u"), (dm_zq, 0, 0), (dm_ready, 1, 1), (grad_ada, 1, 0)],
            2: [(g_zq, 1, "q"), (g_done, 1, "u"), (grad_ada, 1, 1)],
            3: [(dm_qc, 0, 0)],
        },
    )
    grad_qkv(0)
    g_c(0, "q")
    images(
        bwd_first,
        0,
        {0: [(g_qc, 1, "q")], 1: [(g_qz, 0, "d")], 2: [(g_cq, 0, "q"), (dm_ready, 0, 0)], 3: [(g_done, 1, "q")]},
    )
    local(("g",), k.g, out.grad_tokens).start()
    dm_start(0, 1)
    run(
        [
            (grad_ada, 0, 0),
            (g_zq, 0, "d"),
            (dm_zq, 0, 1),
            (dcond_send,),
            (g_qz, 0, "u"),
            (g_qc, 0, "d"),
            (dm_qc, 0, 1),
            (dcond_finish,),
            (g_zq, 0, "u"),
            (g_done, 0, "d"),
            (dm_ready, 0, 1),
            (grad_ada, 0, 1),
            (g_qz, 0, "q"),
            (g_qc, 0, "u"),
            (g_done, 0, "u"),
            (g_zq, 0, "q"),
            (g_qc, 0, "q"),
            (g_done, 0, "q"),
        ]
    )
    w_sent()
    rest_sent()
    local(("os",), k.os, out.output).wait()
    local(("g",), k.g, out.grad_tokens).wait()
    local(("grad_cond",), k.gc.at[pl.ds(0, I)], out.grad_cond).wait()
    for b in range(B):
        stage = (k.mid.at[1], k.x1)[b]
        for m in range(6):
            at = pl.ds(m * (D // F), D // F)
            local(("ada", b, m), stage.at[at], out.grad_ada.at[b, :, pl.ds(m * D, D)]).wait()
        for w in KINDS:
            local(("out", b, w), results[w].at[b], outs[w].at[b]).wait()
    assert len(index) <= N_SEMS and len(local_index) <= 64


def body(F, tokens, cond, cotangent, keep_mask, w_ada, w_qkv, w_proj, w_up, w_down):
    I, L, D = tokens.shape
    B, _, FF = w_up.shape
    R = D // F // 2
    shapes = scratch(F, I, L, D, FF, B)
    names = tuple(shapes)
    anywhere = pl.BlockSpec(memory_space=pl.ANY)
    results = pl.pallas_call(
        functools.partial(kernel, names, F, I, L, D, FF, B),
        name="blocks",
        out_shape=[
            jax.ShapeDtypeStruct((I * L, D), bf),
            jax.ShapeDtypeStruct((I * L, D), f32),
            jax.ShapeDtypeStruct((I, D), f32),
            jax.ShapeDtypeStruct((B, D // F, 6 * D), f32),
            jax.ShapeDtypeStruct((B, 2, R, FF), bf),
            jax.ShapeDtypeStruct((B, 2, R, FF), bf),
            jax.ShapeDtypeStruct((B, 4, 2, R, D), bf),
        ],
        in_specs=[pl.BlockSpec(memory_space=pltpu.SMEM) if n == "mask" else anywhere for n in INPUTS],
        out_specs=[anywhere] * len(OUTPUTS),
        scratch_shapes=[pltpu.VMEM(*shapes[n]) for n in names]
        + [pltpu.SemaphoreType.DMA((N_SEMS,)), pltpu.SemaphoreType.DMA((64,))],
        compiler_params=pltpu.CompilerParams(
            collective_id=0, has_side_effects=True, vmem_limit_bytes=64 * 2**20 - 2**17
        ),
    )(
        tokens.reshape(I * L, D),
        cond,
        cotangent.reshape(I * L, D),
        keep_mask,
        w_ada,
        w_qkv.reshape(B, 2, R, 3 * D),
        w_proj.reshape(B, 2, R, D),
        w_up.reshape(B, 2, R, FF),
        w_down.reshape(B, 4, 2, R, D),
    )
    output, grad_tokens, grad_cond, grad_ada, grad_q, grad_u, grad_d = results
    grad_q = grad_q.reshape(B, 2 * R, FF)
    weights = (
        grad_ada,
        grad_q[:, :, : 3 * D].astype(f32),
        grad_q[:, :, 3 * D :].astype(f32),
        grad_u.reshape(B, 2 * R, FF).astype(f32),
        grad_d.reshape(B, 8 * R, D).astype(f32),
    )
    if lax.axis_size("dp") > GROUP:
        first = lax.axis_index("dp") % GROUP == 0
        weights = lax.psum(tuple(jnp.where(first, w, 0.0) for w in weights), "dp")
    return (output.reshape(I, L, D), grad_tokens.reshape(I, L, D), grad_cond, *weights)


def solution(mesh):
    slots = P(("dp", "fsdp"), None, None)
    weight = P(None, "fsdp", None)
    return jax.shard_map(
        functools.partial(body, mesh.shape["fsdp"]),
        mesh=mesh,
        in_specs=(slots, P(("dp", "fsdp"), None), slots, P(("dp", "fsdp"))) + (weight,) * 5,
        out_specs=(slots, slots, P(("dp", "fsdp"), None)) + (weight,) * 5,
        check_vma=False,
    )
```

```python
import functools

import jax
import jax.numpy as jnp
from jax import lax
from jax.experimental import pallas as pl
from jax.experimental.pallas import tpu as pltpu
from jax.sharding import PartitionSpec as P

MESH = pl.DeviceIdType.MESH
bf, f32 = jnp.bfloat16, jnp.float32
HEADS = 6
PAIRS = HEADS // 2
GROUP = 8
NN = (((1,), (0,)), ((), ()))
NT = (((1,), (1,)), ((), ()))
TN = (((0,), (0,)), ((), ()))
GELU_A = 0.7978845608028654
GELU_B = GELU_A * 0.044715
KINDS = ("u", "d", "q0", "q1", "q2")
SPLIT = ((1, "d"),)
DIRECT = ((0, "d"), (0, "q"), (1, "d"), (1, "q"), (1, "u"))
METHOD = (
    {"u": "ring", "d": "q", "q0": "q", "q1": "q", "q2": "q"},
    {"u": "ring", "d": "q", "q0": "q", "q1": "q", "q2": "q"},
)


def dot(a, b, dims=NN):
    return lax.dot_general(a, b, dims, preferred_element_type=f32)


def exact_dot(a, b, dims=NN):
    return lax.dot_general(a, b, dims, precision=lax.Precision.HIGHEST, preferred_element_type=f32)


def one_hot(shape, hit):
    r = lax.broadcasted_iota(jnp.int32, shape, 0)
    c = lax.broadcasted_iota(jnp.int32, shape, 1)
    return jnp.where(hit(r, c), 1.0, 0.0)


def norm_hat(v):
    c = v - jnp.mean(v, -1, keepdims=True)
    r = lax.rsqrt(jnp.mean(c * c, -1, keepdims=True) + 1e-6)
    return c * r, r


def norm_back(dx, hat, r):
    return r * (dx - jnp.mean(dx, -1, keepdims=True) - hat * jnp.mean(dx * hat, -1, keepdims=True))


class Refs:
    pass


def scratch(F, I, L, D, FF, B):
    T = I * L
    R = D // F // 2
    W = D // PAIRS
    shapes = dict(
        wq=((B, F, 2, R, FF), bf),
        wu=((B, F, 2, R, FF), bf),
        wd=((B, F, 4, 2, R, D), bf),
        wa=((B, D // F, 6 * D), bf),
        tk=((T, D), bf),
        x1=((T, D), f32),
        fi=((B, T, D), bf),
        qkv=((B, T, 3 * D), bf),
        pt=((B, I * HEADS, L, L), bf),
        mt=((B, D, T), bf),
        att=((B, T, D), bf),
        mid=((B, T, D), f32),
        si=((B, T, D), bf),
        hid=((B, T, FF), bf),
        br=((B, T, D), bf),
        g=((T, D), f32),
        db=((T, D), bf),
        act=((T, FF), bf),
        da=((T, D), bf),
        os=((T, D), bf),
        mod=((B, 6 * I, D), f32),
        dm=((B + 1, 16, D), f32),
        cd=((I, D), bf),
        gc=((8, D), f32),
        ms=((B, F, 6 * I, D), f32),
        mr=((B, F, 6 * I, D), f32),
        cg=((4, 2, F, 16, D), bf),
        dg=((B + 1, 4, 2, F, 16, D), bf),
        cs=((F, 8, D), f32),
        cr=((F, 8, D), f32),
        gq=((PAIRS, F, 2, R, 4 * W), bf),
        gu=((F, 2, R, FF), bf),
        gd=((F, 4, 2, R, D), bf),
        hq=((B, PAIRS, F, R, 4 * W), bf),
        hu=((B, F, R, FF), bf),
        hd=((B, F, 4, R, D), bf),
        oq=((B, PAIRS, 2, R, 4 * W), bf),
        ou=((B, 2, R, FF), bf),
        od=((B, 4, 2, R, D), bf),
    )
    for block in range(B):
        for w in KINDS:
            n = W if w[0] == "q" else D
            four = (4, R, n) if w == "d" else (R, 4 * n)
            at = f"{w}{block}"
            if METHOD[block][w] == "direct":
                shapes["a" + at] = ((4 * F, R, n), bf)
            elif METHOD[block][w] == "ring":
                shapes["t" + at] = (four, bf)
                shapes["a" + at] = ((2, *four), bf)
                shapes["s" + at] = (four, bf)
                shapes["b" + at] = ((3, R, n), bf)
            else:
                shapes["a" + at] = ((3, F, R, n), bf)
                shapes["s" + at] = ((F, R, n), bf)
                shapes["b" + at] = ((F, R, n), bf)
    return shapes


INPUTS = ("tokens", "cond", "cotangent", "mask", "ada", "qkv_w", "proj_w", "up_w", "down_w")
OUTPUTS = ("output", "grad_tokens", "grad_cond", "grad_ada", "grad_q", "grad_u", "grad_d")
N_SEMS = 256
N_LOCAL = 64


def kernel(names, F, I, L, D, FF, B, *refs):
    n_in, n_out = len(INPUTS), len(OUTPUTS)
    inp, out, k = Refs(), Refs(), Refs()
    for name, ref in zip(INPUTS, refs[:n_in]):
        setattr(inp, name, ref)
    for name, ref in zip(OUTPUTS, refs[n_in : n_in + n_out]):
        setattr(out, name, ref)
    for name, ref in zip(names, refs[n_in + n_out :]):
        setattr(k, name, ref)
    sems, local_sems = refs[-2], refs[-1]
    T = I * L
    R = D // F // 2
    W = D // PAIRS
    HS = D // HEADS
    images = range(I)

    me, f = lax.axis_index("dp"), lax.axis_index("fsdp")
    e = me % GROUP
    base = me - e
    c, q = e % 2, e // 2
    other = 1 - c
    z_peer = [(f + r) % F for r in range(F)]
    q_peer = [(q + j) % 4 for j in range(4)]

    def at_z(r):
        return (me, z_peer[r])

    def at_q(j, r=0):
        return (base + 2 * q_peer[j] + c, z_peer[r])

    def at_c(j=0):
        return (base + 2 * q_peer[j] + other, f)

    def rows(i):
        return slice(i * L, (i + 1) * L)

    def cut(j, n):
        return pl.ds(pl.multiple_of(j * n, n), n)

    index = {}

    def sem(key):
        return sems.at[index.setdefault(key, len(index))]

    def send(key, src, dst, to):
        pltpu.make_async_remote_copy(
            src_ref=src,
            dst_ref=dst,
            send_sem=sem(("send",) + key),
            recv_sem=sem(("recv",) + key),
            device_id=to,
            device_id_type=MESH,
        ).start()

    unsent = []

    def wait(kind, key, like):
        if kind == "recv" and key[0] != "gc":
            unsent.append((key, like))
        pltpu.make_async_copy(like, like, sem((kind,) + key)).wait()

    def all_sent():
        while unsent:
            key, like = unsent.pop(0)
            pltpu.make_async_copy(like, like, sem(("send",) + key)).wait()

    local_index = {}

    def local(key, src, dst):
        n = local_index.setdefault(key, len(local_index))
        return pltpu.make_async_copy(src, dst, local_sems.at[n])

    whole = {"q": k.wq, "u": k.wu, "d": k.wd}

    def main(b, w):
        return pl.ds(0, R * 2 // 3 if (b, w) in SPLIT else R)

    rest = pl.ds(R * 2 // 3, R // 3)

    def w_main(b, w, fz):
        some = main(b, w)
        return k.wd.at[b, fz, q, c, some] if w == "d" else whole[w].at[b, fz, c, some, cut(q, D)]

    def w_rest(b, w, fz):
        return k.wd.at[b, fz, :, c, rest] if w == "d" else whole[w].at[b, fz, c, rest]

    def w_half(b, w, fz):
        return k.wd.at[b, fz, :, c] if w == "d" else whole[w].at[b, fz, c]

    def like_main(b, w, n, m=1):
        some = main(b, w)
        return k.wd.at[b, pl.ds(0, n), pl.ds(0, m), 0, some] if w == "d" else whole[w].at[b, pl.ds(0, n), 0, some, pl.ds(0, m * D)]

    def like_rest(b, w, n):
        return k.wd.at[b, pl.ds(0, n), :, 0, rest] if w == "d" else whole[w].at[b, pl.ds(0, n), 0, rest]

    def w_z(b, w):
        for r in (1, 3, 2) if (b, w) in DIRECT else (1, 3):
            p = w_main(b, w, f)
            send(("wz", b, w), p, p, at_z(r))
        if (b, w) in SPLIT:
            for r in (1, 3):
                p = w_rest(b, w, f)
                send(("wr", b, w), p, p, at_z(r))

    def w_to_q(b, w, some):
        for r in some:
            for j in range(1, 4):
                p = w_main(b, w, z_peer[r])
                send(("wq", b, w), p, p, at_q(j))

    def w_zq(b, w):
        wait("recv", ("wz", b, w), like_main(b, w, 3))
        w_to_q(b, w, (1, 3, 2))

    def w_relay(b, w):
        if (b, w) not in DIRECT:
            wait("recv", ("wz", b, w), like_main(b, w, 2))
            p = w_main(b, w, z_peer[3])
            send(("wm", b, w), p, p, at_z(1))
        if (b, w) in SPLIT:
            wait("recv", ("wr", b, w), like_rest(b, w, 2))
            p = w_rest(b, w, z_peer[3])
            send(("wo", b, w), p, p, at_z(1))
        if (b, w) not in DIRECT:
            w_to_q(b, w, (1, 3))

    def w_opposite(b, w):
        wait("recv", ("wm", b, w), like_main(b, w, 1))
        w_to_q(b, w, (2,))

    def w_qc(b, w):
        if (b, w) in SPLIT:
            wait("recv", ("wo", b, w), like_rest(b, w, 1))
        wait("recv", ("wq", b, w), like_main(b, w, 3, 3))
        for r in range(1, F):
            p = w_half(b, w, z_peer[r])
            send(("wc", b, w), p, p, at_c())

    def w_ready(b, w):
        wait("recv", ("wc", b, w), k.wd.at[b, pl.ds(0, F - 1), :, 0] if w == "d" else whole[w].at[b, pl.ds(0, F - 1), 0])

    def cols():
        return one_hot((D, D // F), lambda r, s: r == f * (D // F) + s)

    def cond_tile():
        v = k.cd[...].astype(f32)
        a = v / (1.0 + jnp.exp(-v))
        k.cg[q, c, f] = jnp.concatenate([a] * 4, axis=0).astype(bf)

    def cond_z():
        for r in range(1, F):
            send(("cz",), k.cg.at[q, c, f], k.cg.at[q, c, f], at_z(r))

    def cond_zq():
        for j in range(1, 4):
            send(("cq",), k.cg.at[q, c], k.cg.at[q, c], at_q(j))

    def cond_qc():
        wait("recv", ("cq",), k.cg.at[pl.ds(0, 3), 0])
        send(("cc",), k.cg.at[:, c], k.cg.at[:, c], at_c())

    def cond_ready():
        wait("recv", ("cc",), k.cg.at[:, 0])

    def tile_mask(n, p):
        r = lax.broadcasted_iota(jnp.int32, (n, 1), 0)
        return jnp.where((r // 4) % 4 == p, 1.0, 0.0)

    def mod_partial(b, first, last):
        a = dot(k.cg[q, c].reshape(F * 16, D), cols().astype(bf))
        lo, hi = (a * tile_mask(F * 16, 0)).astype(bf), (a * tile_mask(F * 16, 1)).astype(bf)
        for s in range(first, last):
            t = dot(lo, k.wa[b, :, 2 * s * D : (2 * s + 1) * D]) + dot(hi, k.wa[b, :, (2 * s + 1) * D : (2 * s + 2) * D])
            k.ms[b, :, 8 * s : 8 * s + 8, :] = t.reshape(F, 16, D)[:, :8]
        some = pl.ds(8 * first, 8 * (last - first))
        for r in range(1, F):
            send(("mz", b, first), k.ms.at[b, z_peer[r], some], k.mr.at[b, f, some], at_z(r))

    def mod_ready(b, first, last):
        some = slice(8 * first, 8 * last)
        wait("recv", ("mz", b, first), k.mr.at[b, pl.ds(0, F - 1), pl.ds(8 * first, 8 * (last - first))])
        total = k.ms[b, f, some]
        for r in range(1, F):
            total = total + k.mr[b, z_peer[r], some]
        k.mod[b, some] = total

    def piece(b, i, p):
        return k.mod[b, p * I + i : p * I + i + 1, :]

    def dm_row(b, i, p, v):
        t, at = (b, p - 2) if p >= 2 else (B, 2 * b + p)
        k.dm[t, at * I + i : at * I + i + 1, :] = v

    def dm_pieces(t):
        return [(t, p + 2) for p in range(4)] if t < B else [(p // 2, p % 2) for p in range(4)]

    def dm_start(t):
        k.dg[t, q, c, f] = k.dm[t].astype(bf)
        for r in range(1, F):
            p = k.dg.at[t, q, c, f]
            send(("dz", t), p, p, at_z(r))

    def dm_direct(t):
        k.dg[t, q, c, f] = k.dm[t].astype(bf)
        p = k.dg.at[t, q, c, f]
        for r in range(1, F):
            send(("dz", t), p, p, at_z(r))
        for j in range(1, 4):
            for r in range(F):
                send(("dq", t), p, p, at_q(j, r))

    def dm_z(t):
        wait("recv", ("dz", t), k.dg.at[t, 0, 0, pl.ds(0, F - 1)])

    def dm_zq(t):
        wait("recv", ("dz", t), k.dg.at[t, 0, 0, pl.ds(0, F - 1)])
        for j in range(1, 4):
            p = k.dg.at[t, q, c]
            send(("dq", t), p, p, at_q(j))

    def dm_qc(t):
        wait("recv", ("dq", t), k.dg.at[t, pl.ds(0, 3), 0])
        p = k.dg.at[t, :, c]
        send(("dc", t), p, p, at_c())

    def dm_ready(t):
        wait("recv", ("dc", t), k.dg.at[t, :, 0])

    def dcond_part(t):
        tile = k.dg[t, q, c].reshape(F * 16, D).astype(f32)
        acc = None
        for p, (b, m) in enumerate(dm_pieces(t)):
            o = dot((tile * tile_mask(F * 16, p)).astype(bf), k.wa[b, :, m * D : (m + 1) * D], NT)
            acc = o if acc is None else acc + o
        return acc

    def dcond_send():
        acc = dcond_part(0) + dcond_part(1) + dcond_part(2)
        fold = one_hot((F * 8, F * 16), lambda r, s: (r // 8 == s // 16) & (r % 8 == s % 4))
        t = exact_dot(exact_dot(fold, acc), cols(), NT)
        k.cs[...] = t.reshape(F, 8, D)
        for r in range(1, F):
            send(("gz",), k.cs.at[z_peer[r]], k.cr.at[f], at_z(r))

    def dcond_finish():
        wait("recv", ("gz",), k.cr.at[pl.ds(0, F - 1)])
        total = k.cs[f]
        for r in range(1, F):
            total = total + k.cr[z_peer[r]]
        v = k.cd[...].astype(f32)
        s = 1.0 / (1.0 + jnp.exp(-v))
        k.gc[:I] = total[:I] * (s * (1.0 + v * (1.0 - s)))
        local(("grad_cond",), k.gc.at[pl.ds(0, I)], out.grad_cond).start()

    def ada_copy(b, m):
        stage = (k.x1, k.mid.at[1])[b]
        return local(("ada", b, m), stage.at[pl.ds(m * (D // F), D // F)], out.grad_ada.at[b, :, pl.ds(m * D, D)])

    def grad_ada(t):
        n = GROUP * F * 16
        a = dot(k.cg[...].reshape(n, D), cols().astype(bf))
        tile = k.dg[t].reshape(n, D)
        for p, (b, m) in enumerate(dm_pieces(t)):
            stage = (k.x1, k.mid.at[1])[b]
            stage[m * (D // F) : (m + 1) * (D // F), :] = dot((a * tile_mask(n, p)).astype(bf), tile, TN)
            ada_copy(b, m).start()

    def width(w):
        return W if w[0] == "q" else D

    def g_local(w):
        return k.gq.at[int(w[1])] if w[0] == "q" else {"u": k.gu, "d": k.gd}[w]

    def g_halves(b, w):
        return k.hq.at[b, int(w[1])] if w[0] == "q" else {"u": k.hu, "d": k.hd}[w].at[b]

    def g_result(b, w):
        return k.oq.at[b, int(w[1])] if w[0] == "q" else {"u": k.ou, "d": k.od}[w].at[b]

    def g_buf(b, w, kind):
        return getattr(k, f"{kind}{w}{b}")

    def one_of(w, ref, j):
        return ref.at[q_peer[j]] if w == "d" else ref.at[:, cut(q_peer[j], width(w))]

    def r_piece(b, w):
        return k.od.at[b, q, c] if w == "d" else g_result(b, w).at[c, :, cut(q, width(w))]

    def r_half(b, w):
        return k.od.at[b, :, c] if w == "d" else g_result(b, w).at[c]

    def g_c(b, w):
        half = k.gd.at[:, :, other] if w == "d" else g_local(w).at[:, other]
        send(("gc", b, w), half, g_halves(b, w), at_c())

    def g_1(b, w):
        h = g_halves(b, w)
        for kind in ("send", "recv"):
            wait(kind, ("gc", b, w), h)
        for n in range(F):
            own = k.gd[n, :, c] if w == "d" else g_local(w)[n, c]
            h[n] = h[n] + own
        how = METHOD[b][w]
        if how == "direct":
            for r, j in [(r, j) for r in range(F) for j in range(4)][1:]:
                send(("g1", b, w), h.at[z_peer[r], :, cut(q_peer[j], W)], g_buf(b, w, "a").at[r * 4 + j], at_q(j, r))
        elif how == "ring":
            send(("gt", b, w), h.at[z_peer[2]], g_buf(b, w, "t"), at_z(1))
        else:
            for j in range(1, 4):
                p = h.at[:, q_peer[j]] if w == "d" else h.at[:, :, cut(q_peer[j], width(w))]
                send(("g1", b, w), p, g_buf(b, w, "a").at[j - 1], at_q(j))

    def g_ring(b, w):
        h, t = g_halves(b, w), g_buf(b, w, "t")
        wait("recv", ("gt", b, w), t)
        h[z_peer[1]] = h[z_peer[1]] + t[...]
        for n, r in enumerate((1, 3)):
            send(("g1", b, w), h.at[z_peer[r]], g_buf(b, w, "a").at[n], at_z(r))

    def g_direct(b, w):
        h, a = g_halves(b, w), g_buf(b, w, "a")
        wait("recv", ("g1", b, w), a.at[pl.ds(0, 4 * F - 1)])
        total = h[f, :, cut(q, W)].astype(f32)
        for n in range(1, 4 * F):
            total = total + a[n].astype(f32)
        p = r_piece(b, w)
        p[...] = total.astype(bf)
        for j in range(1, 4):
            send(("g3", b, w), p, p, at_q(j))
        for j in range(4):
            send(("g3", b, w), p, p, at_c(j))

    def g_2(b, w):
        h, a, s = g_halves(b, w), g_buf(b, w, "a"), g_buf(b, w, "s")
        wait("recv", ("g1", b, w), a)
        if METHOD[b][w] == "ring":
            total = h[f].astype(f32) + a[0].astype(f32) + a[1].astype(f32)
            s[...] = total.astype(bf)
            for j in range(1, 4):
                send(("g2", b, w), one_of(w, s, j), g_buf(b, w, "b").at[j - 1], at_q(j))
        else:
            for n in range(F):
                own = h[n, q] if w == "d" else h[n, :, cut(q, width(w))]
                total = own.astype(f32)
                for j in range(3):
                    total = total + a[j, n].astype(f32)
                s[n] = total.astype(bf)
            for r in range(1, F):
                send(("g2", b, w), s.at[z_peer[r]], g_buf(b, w, "b").at[f], at_z(r))

    def g_3(b, w):
        s, a = g_buf(b, w, "s"), g_buf(b, w, "b")
        if METHOD[b][w] == "ring":
            wait("recv", ("g2", b, w), a)
            total = one_of(w, s, 0)[...].astype(f32)
            for j in range(3):
                total = total + a[j].astype(f32)
        else:
            wait("recv", ("g2", b, w), a.at[pl.ds(0, F - 1)])
            total = s[f].astype(f32)
            for r in range(1, F):
                total = total + a[z_peer[r]].astype(f32)
        r_piece(b, w)[...] = total.astype(bf)
        for j in range(1, 4):
            send(("g3", b, w), r_piece(b, w), r_piece(b, w), at_q(j))

    def g_4(b, w):
        wait("recv", ("g3", b, w), k.od.at[b, pl.ds(0, 3), 0] if w == "d" else g_result(b, w).at[0, :, pl.ds(0, 3 * width(w))])
        send(("g4", b, w), r_half(b, w), r_half(b, w), at_c())

    def out_copy(b, w):
        to = out.grad_q.at[b, int(w[1])] if w[0] == "q" else {"u": out.grad_u, "d": out.grad_d}[w].at[b]
        return local(("out", b, w), g_result(b, w), to)

    def g_5(b, w):
        if METHOD[b][w] == "direct":
            wait("recv", ("g3", b, w), g_buf(b, w, "a").at[pl.ds(0, 7)])
        else:
            wait("recv", ("g4", b, w), k.od.at[b, :, 0] if w == "d" else g_result(b, w).at[0])
        out_copy(b, w).start()

    def m_qkv(b):
        return k.wq[b, :, :, :, : 3 * D].reshape(D, 3 * D)

    def m_proj(b):
        return k.wq[b, :, :, :, 3 * D :].reshape(D, D)

    def m_up(b, at, n):
        return k.wu[b, :, :, :, at : at + n].reshape(D, n)

    def m_down(b):
        return k.wd[b].reshape(FF, D)

    def state(b, i):
        return k.tk[rows(i), :].astype(f32) if b == 0 else k.x1[rows(i), :]

    def lane_masks():
        lane = lax.broadcasted_iota(jnp.int32, (1, 2 * HS), 1)
        lo = jnp.where(lane < HS, 1.0, 0.0)
        return lo.astype(bf), (1.0 - lo).astype(bf)

    def head_cols(p, which):
        return slice(p * D + which * W, p * D + (which + 1) * W)

    def fwd_norm(b, i):
        hat, _ = norm_hat(state(b, i))
        k.fi[b, rows(i), :] = (hat * (1.0 + piece(b, i, 1)) + piece(b, i, 0)).astype(bf)

    def fwd_qkv(b, i):
        r = rows(i)
        y = dot(k.fi[b, r, :], m_qkv(b))
        for p in range(PAIRS):
            s = head_cols(p, 0)
            k.qkv[b, r, s] = (y[:, s] * HS**-0.5).astype(bf)
            s = slice(p * D + W, (p + 1) * D)
            k.qkv[b, r, s] = y[:, s].astype(bf)

    def fwd_probs(b, i):
        masks = lane_masks()
        for h in range(HEADS):
            qs = k.qkv[b, rows(i), head_cols(h // 2, 0)]
            ks = k.qkv[b, rows(i), head_cols(h // 2, 1)]
            scores = dot(ks * masks[h % 2], qs, NT)
            ex = jnp.exp(scores - jnp.max(scores, axis=0, keepdims=True))
            k.pt[b, i * HEADS + h] = (ex * (1.0 / jnp.sum(ex, axis=0, keepdims=True))).astype(bf)

    def fwd_mix(b, i):
        mixed = []
        for p in range(PAIRS):
            vt = k.qkv[b, rows(i), head_cols(p, 2)].T
            for m in range(2):
                mixed.append(dot(vt[m * HS : (m + 1) * HS], k.pt[b, i * HEADS + 2 * p + m]))
        k.mt[b, :, rows(i)] = jnp.concatenate(mixed, axis=0).astype(bf)

    def fwd_proj(b, i):
        r = rows(i)
        att = dot(k.mt[b, :, r], m_proj(b), TN)
        k.att[b, r, :] = att.astype(bf)
        mid = state(b, i) + piece(b, i, 2) * att
        k.mid[b, r, :] = mid
        hat, _ = norm_hat(mid)
        k.si[b, r, :] = (hat * (1.0 + piece(b, i, 4)) + piece(b, i, 3)).astype(bf)

    def fwd_up(b):
        n = FF // 3
        for j in range(3):
            x = dot(k.si[b], m_up(b, j * n, n))
            k.hid[b, :, j * n : (j + 1) * n] = x.astype(bf)
            k.act[:, j * n : (j + 1) * n] = (x * (0.5 * jnp.tanh(x * (GELU_A + GELU_B * (x * x))) + 0.5)).astype(bf)

    def fwd_down(b):
        acc = dot(k.act[...], m_down(b))
        k.br[b] = acc.astype(bf)
        for i in images:
            r = rows(i)
            y = k.mid[b, r, :] + piece(b, i, 5) * acc[r]
            if b < B - 1:
                k.x1[r, :] = y
            else:
                k.os[r, :] = y.astype(bf)
                k.g[r, :] = k.db[r, :].astype(f32) * inp.mask[i].astype(f32)

    def bwd_hidden(b):
        for i in images:
            r = rows(i)
            g = k.g[r, :]
            dm_row(b, i, 5, jnp.sum(g * k.br[b, r, :].astype(f32), axis=0, keepdims=True))
            k.db[r, :] = (g * piece(b, i, 5)).astype(bf)
        n = FF // 2
        for h in range(2):
            r = slice(h * T // 2, (h + 1) * T // 2)
            for j in range(2):
                s = slice(j * n, (j + 1) * n)
                da = dot(k.db[r, :], m_down(b)[s], NT)
                x = k.hid[b, r, s].astype(f32)
                x2 = x * x
                t = jnp.tanh(x * (GELU_A + GELU_B * x2))
                up = 0.5 * t + 0.5
                a = x * up
                k.act[r, s] = a.astype(bf)
                k.hid[b, r, s] = ((a * (1.0 - t) * (GELU_A + (3 * GELU_B) * x2) + up) * da).astype(bf)

    def bwd_second(b):
        acc = dot(k.hid[b], m_up(b, 0, FF), NT)
        for i in images:
            r = rows(i)
            d = acc[r]
            hat, rs = norm_hat(k.mid[b, r, :])
            dm_row(b, i, 3, jnp.sum(d, axis=0, keepdims=True))
            dm_row(b, i, 4, jnp.sum(d * hat, axis=0, keepdims=True))
            d_mid = k.g[r, :] + norm_back(d * (1.0 + piece(b, i, 4)), hat, rs)
            k.g[r, :] = d_mid
            dm_row(b, i, 2, jnp.sum(d_mid * k.att[b, r, :].astype(f32), axis=0, keepdims=True))
            k.da[r, :] = (d_mid * piece(b, i, 2)).astype(bf)

    def grad_down(b):
        n = FF // 2
        for h in range(2):
            x = dot(k.act[:, h * n : (h + 1) * n], k.db[...], TN)
            k.gd[h * F // 2 : (h + 1) * F // 2] = x.astype(bf).reshape(F // 2, 4, 2, R, D)

    def grad_up(b):
        n = FF // 2
        for h in range(2):
            s = slice(h * n, (h + 1) * n)
            k.gu[:, :, :, s] = dot(k.si[b], k.hid[b, :, s], TN).astype(bf).reshape(F, 2, R, n)

    def grad_proj(b):
        x = dot(k.mt[b], k.da[...]).astype(bf).reshape(F, 2, R, D)
        for p in range(PAIRS):
            k.gq[p, :, :, :, 3 * W :] = x[:, :, :, p * W : (p + 1) * W]

    def grad_qkv(b, p):
        x = dot(k.fi[b], k.qkv[b, :, p * D : (p + 1) * D], TN)
        k.gq[p, :, :, :, : 3 * W] = x.astype(bf).reshape(F, 2, R, 3 * W)

    def bwd_heads(b, p):
        masks = lane_masks()

        def ds_at(i, m):
            return slice(i * L, (i + 1) * L), slice(m * L, (m + 1) * L)

        wp = m_proj(b)[p * W : (p + 1) * W]
        for i in images:
            r = rows(i)
            do = dot(k.da[r, :], wp, NT).astype(bf)
            k.db[r, :W] = do
            vs = k.qkv[b, r, head_cols(p, 2)]
            for m in range(2):
                dp = dot(vs * masks[m], do, NT)
                pf = k.pt[b, i * HEADS + 2 * p + m].astype(f32)
                w = pf * dp
                k.act[ds_at(i, m)] = (w - pf * jnp.sum(w, axis=0, keepdims=True)).astype(bf)
        for i in images:
            r = rows(i)
            do = k.db[r, :W]
            qs = k.qkv[b, r, head_cols(p, 0)]
            ks = k.qkv[b, r, head_cols(p, 1)]
            kt = ks.T
            ds = [k.act[ds_at(i, m)] for m in range(2)]
            pt = [k.pt[b, i * HEADS + 2 * p + m] for m in range(2)]
            dk = dot(ds[0], qs * masks[0]) + dot(ds[1], qs * masks[1])
            dv = dot(pt[0], do * masks[0]) + dot(pt[1], do * masks[1])
            dq = jnp.concatenate([dot(kt[m * HS : (m + 1) * HS], ds[m]) for m in range(2)], axis=0)
            k.qkv[b, r, head_cols(p, 1)] = dk.astype(bf)
            k.qkv[b, r, head_cols(p, 2)] = dv.astype(bf)
            k.qkv[b, r, head_cols(p, 0)] = (dq * HS**-0.5).astype(bf).T

    def bwd_first(b, some):
        for i in some:
            r = rows(i)
            d = dot(k.qkv[b, r, :], m_qkv(b), NT)
            hat, rs = norm_hat(state(b, i))
            dm_row(b, i, 0, jnp.sum(d, axis=0, keepdims=True))
            dm_row(b, i, 1, jnp.sum(d * hat, axis=0, keepdims=True))
            k.g[r, :] = k.g[r, :] + norm_back(d * (1.0 + piece(b, i, 1)), hat, rs)

    def run(*todo):
        for fn, *args in todo:
            fn(*args)

    def each(fn, b):
        for i in images:
            fn(b, i)

    def phase(*todo):
        pl.when(me >= 0)(functools.partial(run, *todo))

    barrier = pltpu.get_barrier_semaphore()
    everyone = [at_q(j, r) for r in range(F) for j in range(4)][1:] + [at_c(j) for j in range(4)]
    for peer in everyone:
        pl.semaphore_signal(barrier, inc=1, device_id=peer, device_id_type=MESH)
    cond_load = local(("cd",), inp.cond, k.cd)
    cond_load.start()
    ada_load = local(("wa",), inp.ada, k.wa)
    w_loads = {"q": [], "u": [local(("wu",), inp.up_w, k.wu.at[:, f])], "d": [local(("wd",), inp.down_w, k.wd.at[:, f])]}
    for which in range(3):
        for p in range(PAIRS):
            w_loads["q"].append(
                local(
                    ("wq", which, p),
                    inp.qkv_w.at[:, :, :, pl.ds(which * D + p * W, W)],
                    k.wq.at[:, f, :, :, pl.ds(p * D + which * W, W)],
                )
            )
    w_loads["q"].append(local(("wp",), inp.proj_w, k.wq.at[:, f, :, :, pl.ds(3 * D, D)]))
    other_loads = [local(("tk",), inp.tokens, k.tk), local(("db",), inp.cotangent, k.db)]
    for copy in w_loads["q"] + [ada_load] + w_loads["u"] + w_loads["d"] + other_loads:
        copy.start()
    cond_load.wait()
    cond_tile()
    for copy in w_loads["q"] + [ada_load] + w_loads["u"] + w_loads["d"] + other_loads:
        copy.wait()
    pl.semaphore_wait(barrier, len(everyone))

    run((cond_z,), (w_z, 0, "u"), (w_z, 0, "q"), (wait, "recv", ("cz",), k.cg.at[0, 0, pl.ds(0, F - 1)]), (cond_zq,), (w_z, 0, "d"), (mod_partial, 1, 0, 3), (w_relay, 0, "u"), (w_zq, 0, "q"), (cond_qc,), (cond_ready,), (w_z, 1, "q"), (mod_partial, 0, 0, 1), (w_zq, 0, "d"), (mod_ready, 1, 0, 3), (w_z, 1, "u"), (mod_partial, 0, 1, 3), (w_qc, 0, "q"), (w_ready, 0, "q"), (w_opposite, 0, "u"), (w_zq, 1, "q"), (w_z, 1, "d"), (mod_ready, 0, 0, 1))
    phase((each, fwd_norm, 0))
    phase((each, fwd_qkv, 0))
    run((w_qc, 0, "d"),)
    phase((each, fwd_probs, 0), (each, fwd_mix, 0))
    run((w_qc, 0, "u"), (w_ready, 0, "d"), (w_zq, 1, "u"), (mod_ready, 0, 1, 3))
    phase((each, fwd_proj, 0))
    run((w_ready, 0, "u"),)
    phase((fwd_up, 0))
    run((w_qc, 1, "q"), (w_zq, 1, "d"))
    phase((fwd_down, 0))
    run((w_relay, 1, "d"), (w_ready, 1, "q"))
    phase((each, fwd_norm, 1), (each, fwd_qkv, 1))
    phase((each, fwd_probs, 1), (each, fwd_mix, 1))
    run((w_qc, 1, "u"),)
    phase((each, fwd_proj, 1))
    run((w_qc, 1, "d"), (w_ready, 1, "u"))
    phase((fwd_up, 1))
    run((w_ready, 1, "d"),)
    phase((fwd_down, 1))
    out_load = local(("os",), k.os, out.output)
    out_load.start()
    phase((bwd_hidden, 1))
    phase((grad_down, 1))
    run((g_c, 1, "d"),)
    phase((grad_up, 1))
    run((g_c, 1, "u"),)
    phase((bwd_second, 1))
    run((g_1, 1, "u"), (g_1, 1, "d"), (dm_start, 1))
    phase((grad_proj, 1))
    phase((bwd_heads, 1, 0))
    phase((grad_qkv, 1, 0))
    run((g_c, 1, "q0"),)
    phase((bwd_heads, 1, 1))
    run((g_1, 1, "q0"),)
    phase((grad_qkv, 1, 1))
    run((g_c, 1, "q1"), (g_ring, 1, "u"))
    phase((bwd_heads, 1, 2))
    run((g_1, 1, "q1"),)
    phase((grad_qkv, 1, 2))
    run((g_c, 1, "q2"), (g_2, 1, "d"))
    phase((bwd_first, 1, images))
    run((g_1, 1, "q2"), (g_2, 1, "q0"), (dm_zq, 1))
    phase((bwd_hidden, 0))
    run((g_2, 1, "u"), (g_2, 1, "q1"))
    phase((grad_up, 0))
    run((g_c, 0, "u"), (g_3, 1, "d"), (dm_qc, 1), (g_2, 1, "q2"))
    phase((grad_down, 0))
    run((g_c, 0, "d"), (g_3, 1, "q0"), (g_1, 0, "u"), (g_3, 1, "q1"), (g_3, 1, "u"), (dm_ready, 1))
    phase((bwd_second, 0))
    run((g_1, 0, "d"), (g_4, 1, "q0"), (g_4, 1, "d"), (dm_start, 0))
    phase((grad_proj, 0))
    phase((bwd_heads, 0, 0))
    run((g_5, 1, "d"), (g_5, 1, "q0"), (g_4, 1, "u"))
    phase((grad_qkv, 0, 0))
    run((g_c, 0, "q0"), (g_ring, 0, "u"))
    phase((bwd_heads, 0, 1))
    run((g_1, 0, "q0"), (dm_zq, 0), (g_5, 1, "u"))
    phase((grad_qkv, 0, 1))
    run((g_c, 0, "q1"),)
    phase((bwd_heads, 0, 2))
    run((g_1, 0, "q1"),)
    phase((grad_qkv, 0, 2))
    run((g_c, 0, "q2"), (g_2, 0, "d"))
    phase((bwd_first, 0, images[: I // 2]))
    run((g_1, 0, "q2"), (g_2, 0, "q0"))
    phase((bwd_first, 0, images[I // 2 :]))
    run((dm_start, 2),)
    g_load = local(("g",), k.g, out.grad_tokens)
    g_load.start()
    run((grad_ada, 1), (dm_qc, 0), (g_3, 1, "q2"), (g_4, 1, "q1"), (g_2, 0, "u"), (dm_ready, 0), (grad_ada, 0), (g_2, 0, "q1"), (g_5, 1, "q1"), (g_3, 0, "d"), (g_2, 0, "q2"), (g_3, 0, "q0"), (g_4, 1, "q2"), (dm_zq, 2), (dcond_send,), (g_5, 1, "q2"), (g_3, 0, "u"), (g_3, 0, "q1"), (g_4, 0, "d"), (g_4, 0, "q0"), (g_3, 0, "q2"), (g_5, 0, "d"), (g_5, 0, "q0"), (dm_qc, 2), (dcond_finish,), (dm_ready, 2), (grad_ada, 2), (g_4, 0, "u"), (g_4, 0, "q1"), (g_4, 0, "q2"), (g_5, 0, "u"), (g_5, 0, "q1"), (all_sent,), (g_5, 0, "q2"))
    run((all_sent,),)
    out_load.wait()
    g_load.wait()
    local(("grad_cond",), k.gc.at[pl.ds(0, I)], out.grad_cond).wait()
    for b in range(B):
        for m in range(6):
            ada_copy(b, m).wait()
        for w in KINDS:
            out_copy(b, w).wait()
    assert len(index) <= N_SEMS and len(local_index) <= N_LOCAL


def finish(*refs):
    n = len(OUTPUTS)
    src, dst, low, high, mid, sems = refs[:n], refs[n : 2 * n + 1], refs[2 * n + 1 : 2 * n + 4], refs[2 * n + 4 : -5], refs[-5:-1], refs[-1]
    B, pairs, _, R, four = src[4].shape
    W = four // 4
    D = W * pairs
    copies = []

    def copy(a, b):
        copies.append(pltpu.make_async_copy(a, b, sems.at[len(copies)]))
        copies[-1].start()
        return copies[-1]

    loads = [copy(src[4 + m], low[m]) for m in range(3)]
    through = [copy(src[m], mid[m]) for m in range(4)]
    qkv, proj, up, down = high
    loads[0].wait()
    for b in range(B):
        for p in range(pairs):
            x = low[0][b, p].reshape(2 * R, 4 * W).astype(f32)
            for j in range(3):
                qkv[b, :, j * D + p * W : j * D + (p + 1) * W] = x[:, j * W : (j + 1) * W]
            proj[b, :, p * W : (p + 1) * W] = x[:, 3 * W :]
    copy(qkv, dst[4])
    copy(proj, dst[5])
    loads[1].wait()
    up[...] = low[1][...].reshape(up.shape).astype(f32)
    copy(up, dst[6])
    loads[2].wait()
    down[...] = low[2][...].reshape(down.shape).astype(f32)
    copy(down, dst[7])
    for m in range(4):
        through[m].wait()
        copy(mid[m], dst[m])
    for c in copies[7:]:
        c.wait()


def body(F, tokens, cond, cotangent, keep_mask, w_ada, w_qkv, w_proj, w_up, w_down):
    I, L, D = tokens.shape
    B, _, FF = w_up.shape
    R = D // F // 2
    W = D // PAIRS
    T = I * L
    shapes = scratch(F, I, L, D, FF, B)
    names = tuple(shapes)
    anywhere = pl.BlockSpec(memory_space=pl.ANY)
    results = [
        jax.ShapeDtypeStruct((T, D), bf),
        jax.ShapeDtypeStruct((T, D), f32),
        jax.ShapeDtypeStruct((I, D), f32),
        jax.ShapeDtypeStruct((B, D // F, 6 * D), f32),
        jax.ShapeDtypeStruct((B, PAIRS, 2, R, 4 * W), bf),
        jax.ShapeDtypeStruct((B, 2, R, FF), bf),
        jax.ShapeDtypeStruct((B, 4, 2, R, D), bf),
    ]
    found = pl.pallas_call(
        functools.partial(kernel, names, F, I, L, D, FF, B),
        name="blocks",
        out_shape=results,
        in_specs=[pl.BlockSpec(memory_space=pltpu.SMEM) if n == "mask" else anywhere for n in INPUTS],
        out_specs=[anywhere] * len(OUTPUTS),
        scratch_shapes=[pltpu.VMEM(*shapes[n]) for n in names]
        + [pltpu.SemaphoreType.DMA((N_SEMS,)), pltpu.SemaphoreType.DMA((N_LOCAL,))],
        compiler_params=pltpu.CompilerParams(
            collective_id=0, has_side_effects=True, vmem_limit_bytes=64 * 2**20 - 2**17
        ),
    )(
        tokens.reshape(T, D),
        cond,
        cotangent.reshape(T, D),
        keep_mask,
        w_ada,
        w_qkv.reshape(B, 2, R, 3 * D),
        w_proj.reshape(B, 2, R, D),
        w_up.reshape(B, 2, R, FF),
        w_down.reshape(B, 4, 2, R, D),
    )
    grads = [(B, 2 * R, 3 * D), (B, 2 * R, D), (B, 2 * R, FF), (B, 8 * R, D)]
    output, grad_tokens, grad_cond, *weights = pl.pallas_call(
        finish,
        name="finish",
        out_shape=results[:4] + [jax.ShapeDtypeStruct(s, f32) for s in grads],
        in_specs=[anywhere] * len(OUTPUTS),
        out_specs=[anywhere] * 8,
        scratch_shapes=[pltpu.VMEM(r.shape, bf) for r in results[4:]]
        + [pltpu.VMEM(s, f32) for s in grads]
        + [pltpu.VMEM(r.shape, r.dtype) for r in results[:4]]
        + [pltpu.SemaphoreType.DMA((16,))],
        compiler_params=pltpu.CompilerParams(vmem_limit_bytes=64 * 2**20 - 2**17),
    )(*found)
    if lax.axis_size("dp") > GROUP:
        first = lax.axis_index("dp") % GROUP == 0
        weights = lax.psum(tuple(jnp.where(first, w, 0.0) for w in weights), "dp")
    return (output.reshape(I, L, D), grad_tokens.reshape(I, L, D), grad_cond, *weights)


def solution(mesh):
    slots = P(("dp", "fsdp"), None, None)
    weight = P(None, "fsdp", None)
    return jax.shard_map(
        functools.partial(body, mesh.shape["fsdp"]),
        mesh=mesh,
        in_specs=(slots, P(("dp", "fsdp"), None), slots, P(("dp", "fsdp"))) + (weight,) * 5,
        out_specs=(slots, slots, P(("dp", "fsdp"), None)) + (weight,) * 5,
        check_vma=False,
    )
```

```python
import functools

import jax
import jax.numpy as jnp
from jax import lax
from jax.experimental import pallas as pl
from jax.experimental.pallas import tpu as pltpu
from jax.sharding import PartitionSpec as P

MESH = pl.DeviceIdType.MESH
bf, f32 = jnp.bfloat16, jnp.float32
HEADS = 6
PAIRS = HEADS // 2
GROUP = 8
NN = (((1,), (0,)), ((), ()))
NT = (((1,), (1,)), ((), ()))
TN = (((0,), (0,)), ((), ()))
GELU_A = 0.7978845608028654
GELU_B = GELU_A * 0.044715
KINDS = ("u", "d", "q0", "q1", "q2")
SPLIT = ((0, "d"), (1, "d"))
DIRECT = ((0, "d"), (0, "q"), (0, "u"), (1, "d"))
STEPS = ()
ONE = ((0, "q1"),)
METHOD = (
    {"u": "q", "d": "steps", "q0": "ring", "q1": "steps", "q2": "q"},
    {"u": "q", "d": "q", "q0": "steps", "q1": "steps", "q2": "q"},
)


def dot(a, b, dims=NN):
    return lax.dot_general(a, b, dims, preferred_element_type=f32)


def exact_dot(a, b, dims=NN):
    return lax.dot_general(a, b, dims, precision=lax.Precision.HIGHEST, preferred_element_type=f32)


def one_hot(shape, hit):
    r = lax.broadcasted_iota(jnp.int32, shape, 0)
    c = lax.broadcasted_iota(jnp.int32, shape, 1)
    return jnp.where(hit(r, c), 1.0, 0.0)


def norm_hat(v):
    c = v - jnp.mean(v, -1, keepdims=True)
    r = lax.rsqrt(jnp.mean(c * c, -1, keepdims=True) + 1e-6)
    return c * r, r


def norm_back(dx, hat, r):
    return r * (dx - jnp.mean(dx, -1, keepdims=True) - hat * jnp.mean(dx * hat, -1, keepdims=True))


def gelu_parts(x):
    x2 = x * x
    t = jnp.tanh(x * (GELU_A + GELU_B * x2))
    up = 0.5 * t + 0.5
    a = x * up
    return a, a * (1.0 - t) * (GELU_A + (3 * GELU_B) * x2) + up


class Refs:
    pass


def scratch(F, I, L, D, FF, B):
    T = I * L
    R = D // F // 2
    W = D // PAIRS
    shapes = dict(
        wq=((B, F, 2, R, FF), bf),
        wu=((B, F, 2, R, FF), bf),
        wd=((B, F, 4, 2, R, D), bf),
        wa=((B, D // F, 6 * D), bf),
        xs=((B + 1, T, D), f32),
        fi=((B, T, D), bf),
        qkv=((B, T, 3 * D), bf),
        pt=((B, I * HEADS, L, L), bf),
        mt=((B, D, T), bf),
        att=((B, T, D), bf),
        mid=((B, T, D), f32),
        si=((B, T, D), bf),
        hid=((B, T, FF), bf),
        br=((B, T, D), bf),
        db=((T, D), bf),
        act=((T, FF), bf),
        da=((T, D), bf),
        mod=((B * 3, 2 * I, D), f32),
        dm=((B, 4 * I, D), f32),
        dl=((B, 2 * I, D), f32),
        cd=((I, D), bf),
        gc=((8, D), f32),
        ms=((F, B * 6 * I, D), bf),
        mr=((F, B * 6 * I, D), bf),
        cz=((F, 16, D), bf),
        cg=((4, 2, 16, D), bf),
        dg=((B + 1, 4, 2, F, 16, D), bf),
        cs=((F, 8, D), f32),
        cr=((F, 8, D), f32),
        gq=((PAIRS, F, 2, R, 4 * W), bf),
        gu=((F, 2, R, FF), bf),
        gd=((F, 4, 2, R, D), bf),
        hq=((B, PAIRS, F, R, 4 * W), bf),
        hu=((B, F, R, FF), bf),
        hd=((B, F, 4, R, D), bf),
        oq=((B, PAIRS, 2, R, 4 * W), bf),
        ou=((B, 2, R, FF), bf),
        od=((B, 4, 2, R, D), bf),
    )
    for block in range(B):
        for w in KINDS:
            n = W if w[0] == "q" else D
            four = (4, R, n) if w == "d" else (R, 4 * n)
            at = f"{w}{block}"
            if METHOD[block][w] == "direct":
                shapes["a" + at] = ((4 * F, R, n), bf)
            elif METHOD[block][w] == "ring":
                shapes["t" + at] = (four, bf)
                shapes["a" + at] = ((2, *four), bf)
                shapes["s" + at] = (four, bf)
                shapes["b" + at] = ((3, R, n), bf)
            else:
                if METHOD[block][w] == "steps":
                    shapes["t" + at] = ((2, F, R, n), bf)
                    shapes["a" + at] = ((F, R, n), bf)
                else:
                    shapes["a" + at] = ((3, F, R, n), bf)
                shapes["s" + at] = ((F, R, n), bf)
                shapes["b" + at] = ((F, R, n), bf)
    return shapes


INPUTS = ("tokens", "cond", "cotangent", "mask", "ada", "qkv_w", "proj_w", "up_w", "down_w")
OUTPUTS = ("output", "grad_tokens", "grad_cond", "grad_ada", "grad_q", "grad_u", "grad_d")
N_SEMS = 256
N_LOCAL = 64


def kernel(names, F, I, L, D, FF, B, *refs):
    n_in, n_out = len(INPUTS), len(OUTPUTS)
    inp, out, k = Refs(), Refs(), Refs()
    for name, ref in zip(INPUTS, refs[:n_in]):
        setattr(inp, name, ref)
    for name, ref in zip(OUTPUTS, refs[n_in : n_in + n_out]):
        setattr(out, name, ref)
    for name, ref in zip(names, refs[n_in + n_out :]):
        setattr(k, name, ref)
    sems, local_sems = refs[-2], refs[-1]
    T = I * L
    R = D // F // 2
    W = D // PAIRS
    HS = D // HEADS
    images = range(I)

    me, f = lax.axis_index("dp"), lax.axis_index("fsdp")
    e = me % GROUP
    base = me - e
    c, q = e % 2, e // 2
    other = 1 - c
    z_peer = [(f + r) % F for r in range(F)]
    q_peer = [(q + j) % 4 for j in range(4)]

    def at_z(r):
        return (me, z_peer[r])

    x_next, y_next = q + 1 - 2 * (q % 2), (q + 2) % 4
    first = x_next * other + y_next * c
    second = x_next * c + y_next * other
    across = 6 - q - first - second

    def at(qi):
        return (base + 2 * qi + c, f)

    def at_q(j, r=0):
        return (base + 2 * q_peer[j] + c, z_peer[r])

    def at_c(j=0):
        return (base + 2 * q_peer[j] + other, f)

    def rows(i):
        return slice(i * L, (i + 1) * L)

    def cut(j, n):
        return pl.ds(pl.multiple_of(j * n, n), n)

    index = {}

    def sem(key):
        return sems.at[index.setdefault(key, len(index))]

    def send(key, src, dst, to):
        pltpu.make_async_remote_copy(
            src_ref=src,
            dst_ref=dst,
            send_sem=sem(("send",) + key),
            recv_sem=sem(("recv",) + key),
            device_id=to,
            device_id_type=MESH,
        ).start()

    unsent = []

    def wait(kind, key, like):
        if kind == "recv" and key[0] != "gc":
            unsent.append((key, like))
        done(kind, key, like)

    def done(kind, key, like):
        ref = like() if callable(like) else like
        pltpu.make_async_copy(ref, ref, sem((kind,) + key)).wait()

    def all_sent():
        while unsent:
            done("send", *unsent.pop(0))

    local_index = {}

    def local(key, src, dst):
        n = local_index.setdefault(key, len(local_index))
        return pltpu.make_async_copy(src, dst, local_sems.at[n])

    whole = {"q": k.wq, "u": k.wu, "d": k.wd}

    def main(b, w):
        return pl.ds(0, R * 2 // 3 if (b, w) in SPLIT else R)

    rest = pl.ds(R * 2 // 3, R // 3)

    def w_main(b, w, fz, qi=q):
        some = main(b, w)
        return k.wd.at[b, fz, qi, c, some] if w == "d" else whole[w].at[b, fz, c, some, cut(qi, D)]

    def w_rest(b, w, fz):
        return k.wd.at[b, fz, :, c, rest] if w == "d" else whole[w].at[b, fz, c, rest]

    def w_half(b, w, fz):
        return k.wd.at[b, fz, :, c] if w == "d" else whole[w].at[b, fz, c]

    def like_main(b, w, n, m=1):
        some = main(b, w)
        return k.wd.at[b, pl.ds(0, n), pl.ds(0, m), 0, some] if w == "d" else whole[w].at[b, pl.ds(0, n), 0, some, pl.ds(0, m * D)]

    def like_rest(b, w, n):
        return k.wd.at[b, pl.ds(0, n), :, 0, rest] if w == "d" else whole[w].at[b, pl.ds(0, n), 0, rest]

    def w_z(b, w):
        for r in (1, 3, 2) if (b, w) in DIRECT else (1, 3):
            p = w_main(b, w, f)
            send(("wz", b, w), p, p, at_z(r))
        if (b, w) in SPLIT:
            for r in (1, 3):
                p = w_rest(b, w, f)
                send(("wr", b, w), p, p, at_z(r))

    def w_to_q(b, w, some):
        for r in some:
            for j in range(1, 4):
                p = w_main(b, w, z_peer[r])
                send(("wq", b, w), p, p, at_q(j))

    def w_zq(b, w):
        if (b, w) in DIRECT:
            wait("recv", ("wz", b, w), lambda: like_main(b, w, 3))
        else:
            wait("recv", ("wm", b, w), lambda: like_main(b, w, 1))
        if (b, w) in STEPS:
            for r in (1, 3, 2):
                p = w_main(b, w, z_peer[r])
                send(("w1", b, w), p, p, at(first))
        else:
            w_to_q(b, w, (1, 3, 2))

    def w_q2(b, w):
        wait("recv", ("w1", b, w), lambda: like_main(b, w, 3))
        for qi in (q, first):
            for r in (1, 3, 2):
                p = w_main(b, w, z_peer[r], qi)
                send(("wq", b, w), p, p, at(second))

    def w_relay(b, w):
        if (b, w) not in DIRECT:
            wait("recv", ("wz", b, w), lambda: like_main(b, w, 2))
            p = w_main(b, w, z_peer[3])
            send(("wm", b, w), p, p, at_z(1))
        if (b, w) in SPLIT:
            wait("recv", ("wr", b, w), lambda: like_rest(b, w, 2))
            p = w_rest(b, w, z_peer[3])
            send(("wo", b, w), p, p, at_z(1))
        if (b, w) not in DIRECT and (b, w) not in STEPS:
            w_to_q(b, w, (1, 3))

    def w_opposite(b, w):
        wait("recv", ("wm", b, w), lambda: like_main(b, w, 1))
        w_to_q(b, w, (2,))

    def w_qc(b, w):
        if (b, w) in SPLIT:
            wait("recv", ("wo", b, w), lambda: like_rest(b, w, 1))
        wait("recv", ("wq", b, w), lambda: like_main(b, w, 3, 2 if (b, w) in STEPS else 3))
        for r in range(1, F):
            p = w_half(b, w, z_peer[r])
            send(("wc", b, w), p, p, at_c())

    def w_ready(b, w):
        wait("recv", ("wc", b, w), lambda: k.wd.at[b, pl.ds(0, F - 1), :, 0] if w == "d" else whole[w].at[b, pl.ds(0, F - 1), 0])

    def cols():
        return one_hot((D, D // F), lambda r, s: r == f * (D // F) + s)

    def cond_tile():
        v = k.cd[...].astype(f32)
        a = v / (1.0 + jnp.exp(-v))
        k.cz[f] = jnp.concatenate([a] * 4, axis=0).astype(bf)

    def cond_z():
        for r in range(1, F):
            send(("cz",), k.cz.at[f], k.cz.at[f], at_z(r))

    def cond_zq():
        pick = one_hot((16, F * 16), lambda r, s: (r // 4 == s // 16) & (r % 4 == s % 16)).astype(bf)
        k.cg[q, c] = dot(pick, k.cz[...].reshape(F * 16, D)).astype(bf)
        for j in range(1, 4):
            send(("cq",), k.cg.at[q, c], k.cg.at[q, c], at_q(j))

    def cond_qc():
        wait("recv", ("cq",), lambda: k.cg.at[pl.ds(0, 3), 0])
        send(("cc",), k.cg.at[:, c], k.cg.at[:, c], at_c())

    def cond_ready():
        wait("recv", ("cc",), lambda: k.cg.at[:, 0])

    def tile_mask(n, p):
        r = lax.broadcasted_iota(jnp.int32, (n, 1), 0)
        return jnp.where((r // 4) % 4 == p, 1.0, 0.0)

    tiles = ((0, 1), (1, 3))

    def mod_partial(part):
        a = dot(k.cz[...].reshape(F * 16, D), cols().astype(bf))
        masked = [(a * tile_mask(F * 16, p)).astype(bf) for p in range(4)]
        lo, hi = tiles[part]
        for t in range(lo, hi):
            total = None
            for p in range(4):
                b, m = divmod(4 * t + p, 6)
                o = dot(masked[p], k.wa[b, :, m * D : (m + 1) * D])
                total = o if total is None else total + o
            k.ms[:, 16 * t : 16 * t + 16, :] = total.astype(bf).reshape(F, 16, D)
        some = pl.ds(16 * lo, 16 * (hi - lo))
        for r in range(1, F):
            send(("mz", part), k.ms.at[z_peer[r], some], k.mr.at[f, some], at_z(r))

    def mod_ready(part):
        lo, hi = tiles[part]
        some = slice(16 * lo, 16 * hi)
        wait("recv", ("mz", part), lambda: k.mr.at[pl.ds(0, F - 1), pl.ds(16 * lo, 16 * (hi - lo))])
        total = k.ms[f, some].astype(f32)
        for r in range(1, F):
            total = total + k.mr[z_peer[r], some].astype(f32)
        k.mod[2 * lo : 2 * hi] = total.reshape(2 * (hi - lo), 2 * I, D)

    def piece(b, i, p):
        at = p % 2 * I + i
        return k.mod[3 * b + p // 2, at : at + 1, :]

    def dm_row(b, i, p, v):
        to, at = (k.dm, (p - 2) * I + i) if p >= 2 else (k.dl, p * I + i)
        to[b, at : at + 1, :] = v

    def dm_pieces(t):
        return [(t, p + 2) for p in range(4)] if t < B else [(p // 2, p % 2) for p in range(4)]

    def dm_start(t):
        k.dg[t, q, c, f] = (k.dm[t] if t < B else k.dl[...].reshape(4 * I, D)).astype(bf)
        for r in range(1, F):
            p = k.dg.at[t, q, c, f]
            send(("dz", t), p, p, at_z(r))

    def dm_zq(t):
        wait("recv", ("dz", t), lambda: k.dg.at[t, 0, 0, pl.ds(0, F - 1)])
        for j in range(1, 4):
            p = k.dg.at[t, q, c]
            send(("dq", t), p, p, at_q(j))

    def dm_qc(t):
        wait("recv", ("dq", t), lambda: k.dg.at[t, pl.ds(0, 3), 0])
        p = k.dg.at[t, :, c]
        send(("dc", t), p, p, at_c())

    def dm_ready(t):
        wait("recv", ("dc", t), lambda: k.dg.at[t, :, 0])

    def dcond_part(t):
        tile = k.dg[t, q, c].reshape(F * 16, D).astype(f32)
        acc = None
        for p, (b, m) in enumerate(dm_pieces(t)):
            o = dot((tile * tile_mask(F * 16, p)).astype(bf), k.wa[b, :, m * D : (m + 1) * D], NT)
            acc = o if acc is None else acc + o
        return acc

    def dcond_send():
        acc = dcond_part(0) + dcond_part(1) + dcond_part(2)
        fold = one_hot((F * 8, F * 16), lambda r, s: (r // 8 == s // 16) & (r % 8 == s % 4))
        t = exact_dot(exact_dot(fold, acc), cols(), NT)
        k.cs[...] = t.reshape(F, 8, D)
        for r in range(1, F):
            send(("gz",), k.cs.at[z_peer[r]], k.cr.at[f], at_z(r))

    def dcond_finish():
        wait("recv", ("gz",), lambda: k.cr.at[pl.ds(0, F - 1)])
        total = k.cs[f]
        for r in range(1, F):
            total = total + k.cr[z_peer[r]]
        v = k.cd[...].astype(f32)
        s = 1.0 / (1.0 + jnp.exp(-v))
        k.gc[:I] = total[:I] * (s * (1.0 + v * (1.0 - s)))
        local(("grad_cond",), k.gc.at[pl.ds(0, I)], out.grad_cond).start()

    def ada_copy(b, m):
        stage = (k.xs.at[1], k.mid.at[1])[b]
        return local(("ada", b, m), stage.at[pl.ds(m * (D // F), D // F)], out.grad_ada.at[b, :, pl.ds(m * D, D)])

    def grad_ada(t):
        n = GROUP * F * 16
        a = dot(k.cg[...].reshape(n // 4, D), cols().astype(bf)).astype(bf)
        spread = one_hot((n, n // 4), lambda r, s: (r // 16 == s // 4) & (r % 4 == s % 4)).astype(bf)
        a = dot(spread, a)
        tile = k.dg[t].reshape(n, D)
        for p, (b, m) in enumerate(dm_pieces(t)):
            stage = (k.xs.at[1], k.mid.at[1])[b]
            stage[m * (D // F) : (m + 1) * (D // F), :] = dot((a * tile_mask(n, p)).astype(bf), tile, TN)
            ada_copy(b, m).start()

    def width(w):
        return W if w[0] == "q" else D

    def g_local(w):
        return k.gq.at[int(w[1])] if w[0] == "q" else {"u": k.gu, "d": k.gd}[w]

    def g_halves(b, w):
        return k.hq.at[b, int(w[1])] if w[0] == "q" else {"u": k.hu, "d": k.hd}[w].at[b]

    def g_result(b, w):
        return k.oq.at[b, int(w[1])] if w[0] == "q" else {"u": k.ou, "d": k.od}[w].at[b]

    def g_buf(b, w, kind):
        return getattr(k, f"{kind}{w}{b}")

    def quarter(w, h, qi):
        return h.at[:, qi] if w == "d" else h.at[:, :, cut(qi, width(w))]

    def one_of(w, ref, j):
        return ref.at[q_peer[j]] if w == "d" else ref.at[:, cut(q_peer[j], width(w))]

    def r_piece(b, w):
        return k.od.at[b, q, c] if w == "d" else g_result(b, w).at[c, :, cut(q, width(w))]

    def r_half(b, w):
        return k.od.at[b, :, c] if w == "d" else g_result(b, w).at[c]

    def g_c(b, w):
        half = k.gd.at[:, :, other] if w == "d" else g_local(w).at[:, other]
        send(("gc", b, w), half, g_halves(b, w), at_c())

    def g_1(b, w):
        h = g_halves(b, w)
        for kind in ("send", "recv"):
            wait(kind, ("gc", b, w), lambda: g_halves(b, w))
        for n in range(F):
            own = k.gd[n, :, c] if w == "d" else g_local(w)[n, c]
            h[n] = h[n] + own
        how = METHOD[b][w]
        if how == "direct":
            for r, j in [(r, j) for r in range(F) for j in range(4)][1:]:
                send(("g1", b, w), h.at[z_peer[r], :, cut(q_peer[j], W)], g_buf(b, w, "a").at[r * 4 + j], at_q(j, r))
        elif how == "steps":
            for n, qi in enumerate((first, across)):
                send(("gt", b, w), quarter(w, h, qi), g_buf(b, w, "t").at[n], at(first))
        elif how == "ring":
            send(("gt", b, w), h.at[z_peer[2]], g_buf(b, w, "t"), at_z(1))
        else:
            for j in range(1, 4):
                send(("g1", b, w), quarter(w, h, q_peer[j]), g_buf(b, w, "a").at[j - 1], at_q(j))

    def g_fly(b, w):
        h, t = g_halves(b, w), g_buf(b, w, "t")
        wait("recv", ("gt", b, w), lambda: t)
        for n, qi in enumerate((q, second)):
            p = quarter(w, h, qi)
            p[...] = p[...] + t[n]
        send(("g1", b, w), quarter(w, h, second), g_buf(b, w, "a"), at(second))

    def g_ring(b, w):
        h, t = g_halves(b, w), g_buf(b, w, "t")
        wait("recv", ("gt", b, w), lambda: t)
        h[z_peer[1]] = h[z_peer[1]] + t[...]
        for n, r in enumerate((1, 3)):
            send(("g1", b, w), h.at[z_peer[r]], g_buf(b, w, "a").at[n], at_z(r))

    def g_direct(b, w):
        h, a = g_halves(b, w), g_buf(b, w, "a")
        wait("recv", ("g1", b, w), lambda: a.at[pl.ds(0, 4 * F - 1)])
        total = h[f, :, cut(q, W)].astype(f32)
        for n in range(1, 4 * F):
            total = total + a[n].astype(f32)
        hand_back(b, w, total)

    def hand_back(b, w, total):
        p = r_piece(b, w)
        p[...] = total.astype(bf)
        for j in range(1, 4):
            send(("g3", b, w), p, p, at_q(j))
        if (b, w) in ONE:
            for j in range(4):
                send(("g3", b, w), p, p, at_c(j))

    def g_2(b, w):
        h, a, s = g_halves(b, w), g_buf(b, w, "a"), g_buf(b, w, "s")
        wait("recv", ("g1", b, w), lambda: a)
        if METHOD[b][w] == "ring":
            total = h[f].astype(f32) + a[0].astype(f32) + a[1].astype(f32)
            s[...] = total.astype(bf)
            for j in range(1, 4):
                send(("g2", b, w), one_of(w, s, j), g_buf(b, w, "b").at[j - 1], at_q(j))
        else:
            if METHOD[b][w] == "steps":
                s[...] = quarter(w, h, q)[...] + a[...]
            else:
                total = quarter(w, h, q)[...].astype(f32)
                for j in range(3):
                    total = total + a[j].astype(f32)
                s[...] = total.astype(bf)
            for r in range(1, F):
                send(("g2", b, w), s.at[z_peer[r]], g_buf(b, w, "b").at[f], at_z(r))

    def g_3(b, w):
        s, a = g_buf(b, w, "s"), g_buf(b, w, "b")
        if METHOD[b][w] == "ring":
            wait("recv", ("g2", b, w), lambda: a)
            total = one_of(w, s, 0)[...].astype(f32)
            for j in range(3):
                total = total + a[j].astype(f32)
        else:
            wait("recv", ("g2", b, w), lambda: a.at[pl.ds(0, F - 1)])
            total = s[f].astype(f32)
            for r in range(1, F):
                total = total + a[z_peer[r]].astype(f32)
        hand_back(b, w, total)

    def g_4(b, w):
        wait("recv", ("g3", b, w), lambda: k.od.at[b, pl.ds(0, 3), 0] if w == "d" else g_result(b, w).at[0, :, pl.ds(0, 3 * width(w))])
        send(("g4", b, w), r_half(b, w), r_half(b, w), at_c())

    def out_copy(b, w):
        to = out.grad_q.at[b, int(w[1])] if w[0] == "q" else {"u": out.grad_u, "d": out.grad_d}[w].at[b]
        return local(("out", b, w), g_result(b, w), to)

    def seven(b, w):
        return k.act.at[pl.ds(0, 7 * R), pl.ds(0, width(w))]

    def g_5(b, w):
        if (b, w) in ONE:
            wait("recv", ("g3", b, w), lambda: seven(b, w))
        else:
            wait("recv", ("g4", b, w), lambda: k.od.at[b, :, 0] if w == "d" else g_result(b, w).at[0])
        out_copy(b, w).start()

    def m_qkv(b):
        return k.wq[b, :, :, :, : 3 * D].reshape(D, 3 * D)

    def m_proj(b):
        return k.wq[b, :, :, :, 3 * D :].reshape(D, D)

    def m_up(b, at, n):
        return k.wu[b, :, :, :, at : at + n].reshape(D, n)

    def m_down(b):
        return k.wd[b].reshape(FF, D)

    def state(b, i):
        return k.xs[b, rows(i), :]

    def lane_masks():
        lane = lax.broadcasted_iota(jnp.int32, (1, 2 * HS), 1)
        lo = jnp.where(lane < HS, 1.0, 0.0)
        return lo.astype(bf), (1.0 - lo).astype(bf)

    def head_cols(p, which):
        return slice(p * D + which * W, p * D + (which + 1) * W)

    def fwd_norm(b, i):
        hat, _ = norm_hat(state(b, i))
        k.fi[b, rows(i), :] = (hat * (1.0 + piece(b, i, 1)) + piece(b, i, 0)).astype(bf)

    def fwd_qkv(b, i):
        r = rows(i)
        y = dot(k.fi[b, r, :], m_qkv(b))
        for p in range(PAIRS):
            s = head_cols(p, 0)
            k.qkv[b, r, s] = (y[:, s] * HS**-0.5).astype(bf)
            s = slice(p * D + W, (p + 1) * D)
            k.qkv[b, r, s] = y[:, s].astype(bf)

    def fwd_probs(b, i):
        masks = lane_masks()
        for h in range(HEADS):
            qs = k.qkv[b, rows(i), head_cols(h // 2, 0)]
            ks = k.qkv[b, rows(i), head_cols(h // 2, 1)]
            scores = dot(ks * masks[h % 2], qs, NT)
            ex = jnp.exp(scores - jnp.max(scores, axis=0, keepdims=True))
            k.pt[b, i * HEADS + h] = (ex * (1.0 / jnp.sum(ex, axis=0, keepdims=True))).astype(bf)

    def fwd_mix(b, i):
        mixed = []
        for p in range(PAIRS):
            vt = k.qkv[b, rows(i), head_cols(p, 2)].T
            for m in range(2):
                mixed.append(dot(vt[m * HS : (m + 1) * HS], k.pt[b, i * HEADS + 2 * p + m]))
        k.mt[b, :, rows(i)] = jnp.concatenate(mixed, axis=0).astype(bf)

    def fwd_proj(b, i):
        r = rows(i)
        att = dot(k.mt[b, :, r], m_proj(b), TN)
        k.att[b, r, :] = att.astype(bf)
        mid = state(b, i) + piece(b, i, 2) * att
        k.mid[b, r, :] = mid
        hat, _ = norm_hat(mid)
        k.si[b, r, :] = (hat * (1.0 + piece(b, i, 4)) + piece(b, i, 3)).astype(bf)

    def fwd_up(b):
        n = FF // 3
        for j in range(3):
            s = slice(j * n, (j + 1) * n)
            x = dot(k.si[b], m_up(b, j * n, n))
            k.hid[b, :, s] = x.astype(bf)
            k.act[:, s] = (x * (0.5 * jnp.tanh(x * (GELU_A + GELU_B * (x * x))) + 0.5)).astype(bf)

    def fwd_down(b):
        acc = dot(k.act[...], m_down(b))
        k.br[b] = acc.astype(bf)
        for i in images:
            r = rows(i)
            k.xs[b + 1, r, :] = k.mid[b, r, :] + piece(b, i, 5) * acc[r]

    def turn():
        for i in images:
            r = rows(i)
            k.da[r, :] = k.xs[B, r, :].astype(bf)
            k.xs[B, r, :] = k.db[r, :].astype(f32) * inp.mask[i].astype(f32)

    def bwd_hidden(b):
        for i in images:
            r = rows(i)
            g = k.xs[B, r, :]
            dm_row(b, i, 5, jnp.sum(g * k.br[b, r, :].astype(f32), axis=0, keepdims=True))
            k.db[r, :] = (g * piece(b, i, 5)).astype(bf)
        n = FF // 2
        for h in range(2):
            r = slice(h * T // 2, (h + 1) * T // 2)
            for j in range(2):
                s = slice(j * n, (j + 1) * n)
                da = dot(k.db[r, :], m_down(b)[s], NT)
                a, slope = gelu_parts(k.hid[b, r, s].astype(f32))
                k.act[r, s] = a.astype(bf)
                k.hid[b, r, s] = (slope * da).astype(bf)

    def bwd_second(b):
        acc = dot(k.hid[b], m_up(b, 0, FF), NT)
        for i in images:
            r = rows(i)
            d = acc[r]
            hat, rs = norm_hat(k.mid[b, r, :])
            dm_row(b, i, 3, jnp.sum(d, axis=0, keepdims=True))
            dm_row(b, i, 4, jnp.sum(d * hat, axis=0, keepdims=True))
            d_mid = k.xs[B, r, :] + norm_back(d * (1.0 + piece(b, i, 4)), hat, rs)
            k.xs[B, r, :] = d_mid
            dm_row(b, i, 2, jnp.sum(d_mid * k.att[b, r, :].astype(f32), axis=0, keepdims=True))
            k.da[r, :] = (d_mid * piece(b, i, 2)).astype(bf)

    def grad_down(b):
        n = FF // 2
        for h in range(2):
            x = dot(k.act[:, h * n : (h + 1) * n], k.db[...], TN)
            k.gd[h * F // 2 : (h + 1) * F // 2] = x.astype(bf).reshape(F // 2, 4, 2, R, D)

    def grad_up(b):
        n = FF // 2
        for h in range(2):
            s = slice(h * n, (h + 1) * n)
            k.gu[:, :, :, s] = dot(k.si[b], k.hid[b, :, s], TN).astype(bf).reshape(F, 2, R, n)

    def grad_proj(b):
        x = dot(k.mt[b], k.da[...]).astype(bf).reshape(F, 2, R, D)
        for p in range(PAIRS):
            k.gq[p, :, :, :, 3 * W :] = x[:, :, :, p * W : (p + 1) * W]

    def grad_qkv(b, p):
        x = dot(k.fi[b], k.qkv[b, :, p * D : (p + 1) * D], TN)
        k.gq[p, :, :, :, : 3 * W] = x.astype(bf).reshape(F, 2, R, 3 * W)

    def bwd_heads(b, p):
        masks = lane_masks()

        def ds_at(i, m):
            return slice(i * L, (i + 1) * L), slice(m * L, (m + 1) * L)

        wp = m_proj(b)[p * W : (p + 1) * W]
        for i in images:
            r = rows(i)
            do = dot(k.da[r, :], wp, NT).astype(bf)
            k.db[r, :W] = do
            vs = k.qkv[b, r, head_cols(p, 2)]
            for m in range(2):
                dp = dot(vs * masks[m], do, NT)
                pf = k.pt[b, i * HEADS + 2 * p + m].astype(f32)
                w = pf * dp
                k.act[ds_at(i, m)] = (w - pf * jnp.sum(w, axis=0, keepdims=True)).astype(bf)
        for i in images:
            r = rows(i)
            do = k.db[r, :W]
            qs = k.qkv[b, r, head_cols(p, 0)]
            ks = k.qkv[b, r, head_cols(p, 1)]
            kt = ks.T
            ds = [k.act[ds_at(i, m)] for m in range(2)]
            pt = [k.pt[b, i * HEADS + 2 * p + m] for m in range(2)]
            dk = dot(ds[0], qs * masks[0]) + dot(ds[1], qs * masks[1])
            dv = dot(pt[0], do * masks[0]) + dot(pt[1], do * masks[1])
            dq = jnp.concatenate([dot(kt[m * HS : (m + 1) * HS], ds[m]) for m in range(2)], axis=0)
            k.qkv[b, r, head_cols(p, 1)] = dk.astype(bf)
            k.qkv[b, r, head_cols(p, 2)] = dv.astype(bf)
            k.qkv[b, r, head_cols(p, 0)] = (dq * HS**-0.5).astype(bf).T

    def bwd_first(b, some):
        for i in some:
            r = rows(i)
            d = dot(k.qkv[b, r, :], m_qkv(b), NT)
            hat, rs = norm_hat(state(b, i))
            dm_row(b, i, 0, jnp.sum(d, axis=0, keepdims=True))
            dm_row(b, i, 1, jnp.sum(d * hat, axis=0, keepdims=True))
            k.xs[B, r, :] = k.xs[B, r, :] + norm_back(d * (1.0 + piece(b, i, 1)), hat, rs)

    def run(*todo):
        for fn, *args in todo:
            fn(*args)

    def each(fn, b):
        for i in images:
            fn(b, i)

    def out_wait():
        local(("os",), k.da, out.output).wait()

    def at_block(b, which, *todo):
        pl.when(b == which)(functools.partial(run, *todo))

    def phase(*todo):
        pl.when(me >= 0)(functools.partial(run, *todo))

    barrier = pltpu.get_barrier_semaphore()
    everyone = [at_q(j, r) for r in range(F) for j in range(4)][1:] + [at_c(j) for j in range(4)]
    for peer in everyone:
        pl.semaphore_signal(barrier, inc=1, device_id=peer, device_id_type=MESH)
    cond_load = local(("cd",), inp.cond, k.cd)
    cond_load.start()
    ada_load = local(("wa",), inp.ada, k.wa)
    w_loads = {"q": [], "u": [local(("wu",), inp.up_w, k.wu.at[:, f])], "d": [local(("wd",), inp.down_w, k.wd.at[:, f])]}
    for which in range(3):
        for p in range(PAIRS):
            w_loads["q"].append(
                local(
                    ("wq", which, p),
                    inp.qkv_w.at[:, :, :, pl.ds(which * D + p * W, W)],
                    k.wq.at[:, f, :, :, pl.ds(p * D + which * W, W)],
                )
            )
    w_loads["q"].append(local(("wp",), inp.proj_w, k.wq.at[:, f, :, :, pl.ds(3 * D, D)]))
    other_loads = [local(("tk",), inp.tokens, k.da), local(("db",), inp.cotangent, k.db)]
    for copy in w_loads["q"] + [ada_load] + w_loads["u"] + w_loads["d"] + other_loads:
        copy.start()
    cond_load.wait()
    cond_tile()
    for copy in w_loads["q"] + [ada_load] + w_loads["u"] + w_loads["d"] + other_loads:
        copy.wait()
    for i in images:
        k.xs[0, rows(i), :] = k.da[rows(i), :].astype(f32)
    pl.semaphore_wait(barrier, len(everyone))

    run((cond_z,), (w_z, 1, "q"), (w_z, 0, "q"), (wait, "recv", ("cz",), k.cz.at[pl.ds(0, F - 1)]), (w_z, 0, "u"), (mod_partial, 0), (w_z, 0, "d"), (w_relay, 1, "q"), (cond_zq,), (w_zq, 0, "q"), (w_zq, 0, "u"), (w_z, 1, "u"), (mod_ready, 0))

    def forward(step, _):
        b = step
        phase((each, fwd_norm, b),)
        at_block(b, 0, (w_zq, 0, "d"), (w_relay, 0, "d"), (w_qc, 0, "q"), (mod_partial, 1), (w_opposite, 1, "q"), (w_ready, 0, "q"))
        phase((each, fwd_qkv, b),)
        at_block(b, 0, (w_relay, 1, "u"), (w_z, 1, "d"))
        phase((each, fwd_probs, b), (each, fwd_mix, b))
        at_block(b, 0, (w_qc, 0, "u"), (mod_ready, 1))
        at_block(b, 1, (w_qc, 1, "u"),)
        phase((each, fwd_proj, b),)
        at_block(b, 0, (w_ready, 0, "u"), (w_qc, 0, "d"), (w_opposite, 1, "u"))
        at_block(b, 1, (w_qc, 1, "d"), (w_ready, 1, "u"))
        phase((fwd_up, b),)
        at_block(b, 0, (w_qc, 1, "q"), (w_ready, 0, "d"))
        at_block(b, 1, (w_ready, 1, "d"),)
        phase((fwd_down, b),)
        at_block(b, 0, (w_zq, 1, "d"), (w_relay, 1, "d"), (w_ready, 1, "q"))
        return 0

    lax.fori_loop(0, B, forward, 0)
    phase((turn,),)
    out_load = local(("os",), k.da, out.output)
    out_load.start()

    def backward(step, _):
        b = B - 1 - step
        phase((bwd_hidden, b),)
        at_block(b, 0, (dm_zq, 1), (g_fly, 1, "q0"), (g_2, 1, "d"))
        phase((grad_up, b),)
        at_block(b, 1, (g_c, 1, "u"),)
        at_block(b, 0, (g_c, 0, "u"), (g_3, 1, "u"))
        phase((grad_down, b),)
        at_block(b, 1, (g_c, 1, "d"), (g_1, 1, "u"))
        at_block(b, 0, (g_c, 0, "d"), (g_fly, 1, "q1"), (g_1, 0, "u"), (g_2, 1, "q0"))
        at_block(b, B - 1, (out_wait,))
        phase((bwd_second, b),)
        at_block(b, 1, (g_1, 1, "d"), (dm_start, 1))
        at_block(b, 0, (g_1, 0, "d"), (dm_start, 0), (g_4, 1, "u"), (g_2, 1, "q1"))
        phase((grad_proj, b),)
        phase((bwd_heads, b, 0),)
        at_block(b, 0, (g_5, 1, "u"), (g_3, 1, "q0"))
        phase((grad_qkv, b, 0),)
        at_block(b, 1, (g_c, 1, "q0"),)
        at_block(b, 0, (g_c, 0, "q0"),)
        phase((bwd_heads, b, 1),)
        at_block(b, 1, (g_1, 1, "q0"),)
        at_block(b, 0, (g_3, 1, "d"), (g_1, 0, "q0"))
        phase((grad_qkv, b, 1),)
        at_block(b, 1, (g_c, 1, "q1"),)
        at_block(b, 0, (g_c, 0, "q1"), (g_3, 1, "q1"), (g_2, 0, "u"))
        phase((bwd_heads, b, 2),)
        at_block(b, 1, (g_1, 1, "q1"), (g_2, 1, "u"))
        at_block(b, 0, (g_1, 0, "q1"),)
        phase((grad_qkv, b, 2),)
        at_block(b, 1, (g_c, 1, "q2"),)
        at_block(b, 0, (g_c, 0, "q2"), (g_fly, 0, "d"), (g_ring, 0, "q0"))
        phase((bwd_first, b, images[: I // 2]),)
        at_block(b, 0, (g_1, 0, "q2"),)
        phase((bwd_first, b, images[I // 2 :]),)
        at_block(b, 1, (g_1, 1, "q2"),)
        return 0

    lax.fori_loop(0, B, backward, 0)
    run((dm_start, 2),)
    g_load = local(("g",), k.xs.at[B], out.grad_tokens)
    g_load.start()
    run((g_4, 1, "d"), (g_2, 1, "q2"), (g_fly, 0, "q1"), (cond_qc,), (dm_qc, 1), (dm_zq, 0), (g_4, 1, "q0"), (g_4, 1, "q1"), (g_3, 0, "u"), (g_5, 1, "d"), (g_2, 0, "d"), (cond_ready,), (dm_ready, 1), (grad_ada, 1), (g_5, 1, "q1"), (g_5, 1, "q0"), (g_2, 0, "q0"), (g_2, 0, "q2"), (g_2, 0, "q1"), (dm_zq, 2), (dcond_send,), (g_3, 1, "q2"), (dm_qc, 0), (dm_ready, 0), (grad_ada, 0), (g_4, 0, "u"), (g_3, 0, "q0"), (g_3, 0, "d"), (g_5, 0, "u"), (g_3, 0, "q2"), (dm_qc, 2), (g_3, 0, "q1"), (g_4, 1, "q2"), (dcond_finish,), (dm_ready, 2), (grad_ada, 2), (g_4, 0, "q0"), (g_5, 1, "q2"), (g_4, 0, "d"), (g_5, 0, "q0"), (g_4, 0, "q2"), (g_5, 0, "d"), (all_sent,), (g_5, 0, "q1"), (g_5, 0, "q2"), (all_sent,))
    g_load.wait()
    local(("grad_cond",), k.gc.at[pl.ds(0, I)], out.grad_cond).wait()
    for b in range(B):
        for m in range(6):
            ada_copy(b, m).wait()
        for w in KINDS:
            out_copy(b, w).wait()
    assert len(index) <= N_SEMS and len(local_index) <= N_LOCAL


def finish(*refs):
    n = len(OUTPUTS)
    src, dst, low, high, mid, sems = refs[:n], refs[n : 2 * n + 1], refs[2 * n + 1 : 2 * n + 4], refs[2 * n + 4 : -5], refs[-5:-1], refs[-1]
    B, pairs, _, R, four = src[4].shape
    W = four // 4
    D = W * pairs
    copies = []

    def copy(a, b):
        copies.append(pltpu.make_async_copy(a, b, sems.at[len(copies)]))
        copies[-1].start()
        return copies[-1]

    loads = [copy(src[4 + m], low[m]) for m in range(3)]
    through = [copy(src[m], mid[m]) for m in range(4)]
    qkv, proj, up, down = high
    loads[0].wait()
    for b in range(B):
        for p in range(pairs):
            x = low[0][b, p].reshape(2 * R, 4 * W).astype(f32)
            for j in range(3):
                qkv[b, :, j * D + p * W : j * D + (p + 1) * W] = x[:, j * W : (j + 1) * W]
            proj[b, :, p * W : (p + 1) * W] = x[:, 3 * W :]
    copy(qkv, dst[4])
    copy(proj, dst[5])
    loads[1].wait()
    up[...] = low[1][...].reshape(up.shape).astype(f32)
    copy(up, dst[6])
    loads[2].wait()
    down[...] = low[2][...].reshape(down.shape).astype(f32)
    copy(down, dst[7])
    for m in range(4):
        through[m].wait()
        copy(mid[m], dst[m])
    for c in copies[7:]:
        c.wait()


def body(F, tokens, cond, cotangent, keep_mask, w_ada, w_qkv, w_proj, w_up, w_down):
    I, L, D = tokens.shape
    B, _, FF = w_up.shape
    R = D // F // 2
    W = D // PAIRS
    T = I * L
    shapes = scratch(F, I, L, D, FF, B)
    names = tuple(shapes)
    anywhere = pl.BlockSpec(memory_space=pl.ANY)
    results = [
        jax.ShapeDtypeStruct((T, D), bf),
        jax.ShapeDtypeStruct((T, D), f32),
        jax.ShapeDtypeStruct((I, D), f32),
        jax.ShapeDtypeStruct((B, D // F, 6 * D), f32),
        jax.ShapeDtypeStruct((B, PAIRS, 2, R, 4 * W), bf),
        jax.ShapeDtypeStruct((B, 2, R, FF), bf),
        jax.ShapeDtypeStruct((B, 4, 2, R, D), bf),
    ]
    found = pl.pallas_call(
        functools.partial(kernel, names, F, I, L, D, FF, B),
        name="blocks",
        out_shape=results,
        in_specs=[pl.BlockSpec(memory_space=pltpu.SMEM) if n == "mask" else anywhere for n in INPUTS],
        out_specs=[anywhere] * len(OUTPUTS),
        scratch_shapes=[pltpu.VMEM(*shapes[n]) for n in names]
        + [pltpu.SemaphoreType.DMA((N_SEMS,)), pltpu.SemaphoreType.DMA((N_LOCAL,))],
        compiler_params=pltpu.CompilerParams(
            collective_id=0, has_side_effects=True, vmem_limit_bytes=64 * 2**20 - 2**17
        ),
    )(
        tokens.reshape(T, D),
        cond,
        cotangent.reshape(T, D),
        keep_mask,
        w_ada,
        w_qkv.reshape(B, 2, R, 3 * D),
        w_proj.reshape(B, 2, R, D),
        w_up.reshape(B, 2, R, FF),
        w_down.reshape(B, 4, 2, R, D),
    )
    grads = [(B, 2 * R, 3 * D), (B, 2 * R, D), (B, 2 * R, FF), (B, 8 * R, D)]
    output, grad_tokens, grad_cond, *weights = pl.pallas_call(
        finish,
        name="finish",
        out_shape=results[:4] + [jax.ShapeDtypeStruct(s, f32) for s in grads],
        in_specs=[anywhere] * len(OUTPUTS),
        out_specs=[anywhere] * 8,
        scratch_shapes=[pltpu.VMEM(r.shape, bf) for r in results[4:]]
        + [pltpu.VMEM(s, f32) for s in grads]
        + [pltpu.VMEM(r.shape, r.dtype) for r in results[:4]]
        + [pltpu.SemaphoreType.DMA((16,))],
        compiler_params=pltpu.CompilerParams(vmem_limit_bytes=64 * 2**20 - 2**17),
    )(*found)
    if lax.axis_size("dp") > GROUP:
        first = lax.axis_index("dp") % GROUP == 0
        weights = lax.psum(tuple(jnp.where(first, w, 0.0) for w in weights), "dp")
    return (output.reshape(I, L, D), grad_tokens.reshape(I, L, D), grad_cond, *weights)


def solution(mesh):
    slots = P(("dp", "fsdp"), None, None)
    weight = P(None, "fsdp", None)
    return jax.shard_map(
        functools.partial(body, mesh.shape["fsdp"]),
        mesh=mesh,
        in_specs=(slots, P(("dp", "fsdp"), None), slots, P(("dp", "fsdp"))) + (weight,) * 5,
        out_specs=(slots, slots, P(("dp", "fsdp"), None)) + (weight,) * 5,
        check_vma=False,
    )
```

```python
import functools

import jax
import jax.numpy as jnp
from jax import lax
from jax.experimental import pallas as pl
from jax.experimental.pallas import tpu as pltpu
from jax.sharding import PartitionSpec as P

MESH = pl.DeviceIdType.MESH
bf, f32 = jnp.bfloat16, jnp.float32
HEADS = 6
PAIRS = HEADS // 2
GROUP = 8
NN = (((1,), (0,)), ((), ()))
NT = (((1,), (1,)), ((), ()))
TN = (((0,), (0,)), ((), ()))
GELU_A = 0.7978845608028654
GELU_B = GELU_A * 0.044715
KINDS = ("u", "d", "q0", "q1", "q2")
SPLIT = ((0, "d"), (1, "d"))
DIRECT = ((0, "d"), (0, "q"), (0, "u"), (1, "d"))
STEPS = ()
ONE = ((0, "q1"),)
METHOD = (
    {"u": "q", "d": "steps", "q0": "ring", "q1": "steps", "q2": "q"},
    {"u": "q", "d": "q", "q0": "steps", "q1": "steps", "q2": "q"},
)


def dot(a, b, dims=NN):
    return lax.dot_general(a, b, dims, preferred_element_type=f32)


def exact_dot(a, b, dims=NN):
    return lax.dot_general(a, b, dims, precision=lax.Precision.HIGHEST, preferred_element_type=f32)


def one_hot(shape, hit):
    r = lax.broadcasted_iota(jnp.int32, shape, 0)
    c = lax.broadcasted_iota(jnp.int32, shape, 1)
    return jnp.where(hit(r, c), 1.0, 0.0)


def norm_hat(v):
    c = v - jnp.mean(v, -1, keepdims=True)
    r = lax.rsqrt(jnp.mean(c * c, -1, keepdims=True) + 1e-6)
    return c * r, r


def norm_back(dx, hat, r):
    return r * (dx - jnp.mean(dx, -1, keepdims=True) - hat * jnp.mean(dx * hat, -1, keepdims=True))


def gelu_parts(x):
    x2 = x * x
    t = jnp.tanh(x * (GELU_A + GELU_B * x2))
    up = 0.5 * t + 0.5
    a = x * up
    return a, a * (1.0 - t) * (GELU_A + (3 * GELU_B) * x2) + up


class Refs:
    pass


def scratch(F, I, L, D, FF, B):
    T = I * L
    R = D // F // 2
    W = D // PAIRS
    shapes = dict(
        wq=((B, F, 2, R, FF), bf),
        wu=((B, F, 2, R, FF), bf),
        wd=((B, F, 4, 2, R, D), bf),
        wa=((B, D // F, 6 * D), bf),
        xs=((B + 1, T, D), f32),
        fi=((B, T, D), bf),
        qkv=((B, T, 3 * D), bf),
        pt=((I * HEADS, L, L), bf),
        mt=((B, D, T), bf),
        att=((B, T, D), bf),
        mid=((B, T, D), f32),
        si=((B, T, D), bf),
        hid=((T, FF), bf),
        br=((B, T, D), bf),
        db=((T, D), bf),
        act=((T, FF), bf),
        da=((T, D), bf),
        mod=((B * 3, 2 * I, D), f32),
        dm=((B, 4 * I, D), f32),
        dl=((B, 2 * I, D), f32),
        cd=((I, D), bf),
        gc=((8, D), f32),
        ms=((F, B * 6 * I, D), bf),
        mr=((F, B * 6 * I, D), bf),
        cz=((F, 16, D), bf),
        cg=((4, 2, 16, D), bf),
        dg=((B + 1, 4, 2, F, 16, D), bf),
        cs=((F, 8, D), f32),
        cr=((F, 8, D), f32),
        gq=((PAIRS, F, 2, R, 4 * W), bf),
        gu=((F, 2, R, FF), bf),
        gd=((F, 4, 2, R, D), bf),
        hq=((B, PAIRS, F, R, 4 * W), bf),
        hu=((B, F, R, FF), bf),
        hd=((B, F, 4, R, D), bf),
        oq=((B, PAIRS, 2, R, 4 * W), bf),
        ou=((B, 2, R, FF), bf),
        od=((B, 4, 2, R, D), bf),
    )
    for block in range(B):
        for w in KINDS:
            n = W if w[0] == "q" else D
            four = (4, R, n) if w == "d" else (R, 4 * n)
            at = f"{w}{block}"
            if METHOD[block][w] == "direct":
                shapes["a" + at] = ((4 * F, R, n), bf)
            elif METHOD[block][w] == "ring":
                shapes["t" + at] = (four, bf)
                shapes["a" + at] = ((2, *four), bf)
                shapes["s" + at] = (four, bf)
                shapes["b" + at] = ((3, R, n), bf)
            else:
                if METHOD[block][w] == "steps":
                    shapes["t" + at] = ((2, F, R, n), bf)
                    shapes["a" + at] = ((F, R, n), bf)
                else:
                    shapes["a" + at] = ((3, F, R, n), bf)
                shapes["s" + at] = ((F, R, n), bf)
                shapes["b" + at] = ((F, R, n), bf)
    return shapes


INPUTS = ("tokens", "cond", "cotangent", "mask", "ada", "qkv_w", "proj_w", "up_w", "down_w")
OUTPUTS = ("output", "grad_tokens", "grad_cond", "grad_ada", "grad_q", "grad_u", "grad_d")
KEPT = ("pt", "hid", "act")
N_SEMS = 256
N_LOCAL = 64


def kernel(names, F, I, L, D, FF, B, *refs):
    n_in, n_out = len(INPUTS), len(OUTPUTS) + len(KEPT)
    inp, out, k = Refs(), Refs(), Refs()
    for name, ref in zip(INPUTS, refs[:n_in]):
        setattr(inp, name, ref)
    for name, ref in zip(OUTPUTS + KEPT, refs[n_in : n_in + n_out]):
        setattr(out, name, ref)
    for name, ref in zip(names, refs[n_in + n_out :]):
        setattr(k, name, ref)
    sems, local_sems = refs[-2], refs[-1]
    T = I * L
    R = D // F // 2
    W = D // PAIRS
    HS = D // HEADS
    images = range(I)

    me, f = lax.axis_index("dp"), lax.axis_index("fsdp")
    e = me % GROUP
    base = me - e
    c, q = e % 2, e // 2
    other = 1 - c
    z_peer = [(f + r) % F for r in range(F)]
    q_peer = [(q + j) % 4 for j in range(4)]

    def at_z(r):
        return (me, z_peer[r])

    x_next, y_next = q + 1 - 2 * (q % 2), (q + 2) % 4
    first = x_next * other + y_next * c
    second = x_next * c + y_next * other
    across = 6 - q - first - second

    def at(qi):
        return (base + 2 * qi + c, f)

    def at_q(j, r=0):
        return (base + 2 * q_peer[j] + c, z_peer[r])

    def at_c(j=0):
        return (base + 2 * q_peer[j] + other, f)

    def rows(i):
        return slice(i * L, (i + 1) * L)

    def cut(j, n):
        return pl.ds(pl.multiple_of(j * n, n), n)

    index = {}

    def sem(key):
        return sems.at[index.setdefault(key, len(index))]

    def send(key, src, dst, to):
        pltpu.make_async_remote_copy(
            src_ref=src,
            dst_ref=dst,
            send_sem=sem(("send",) + key),
            recv_sem=sem(("recv",) + key),
            device_id=to,
            device_id_type=MESH,
        ).start()

    unsent = []

    def wait(kind, key, like):
        if kind == "recv" and key[0] != "gc":
            unsent.append((key, like))
        done(kind, key, like)

    def done(kind, key, like):
        ref = like() if callable(like) else like
        pltpu.make_async_copy(ref, ref, sem((kind,) + key)).wait()

    def all_sent():
        while unsent:
            done("send", *unsent.pop(0))

    local_index = {}

    def local(key, src, dst):
        n = local_index.setdefault(key, len(local_index))
        return pltpu.make_async_copy(src, dst, local_sems.at[n])

    whole = {"q": k.wq, "u": k.wu, "d": k.wd}

    def main(b, w):
        return pl.ds(0, R * 2 // 3 if (b, w) in SPLIT else R)

    rest = pl.ds(R * 2 // 3, R // 3)

    def w_main(b, w, fz, qi=q):
        some = main(b, w)
        return k.wd.at[b, fz, qi, c, some] if w == "d" else whole[w].at[b, fz, c, some, cut(qi, D)]

    def w_rest(b, w, fz):
        return k.wd.at[b, fz, :, c, rest] if w == "d" else whole[w].at[b, fz, c, rest]

    def w_half(b, w, fz):
        return k.wd.at[b, fz, :, c] if w == "d" else whole[w].at[b, fz, c]

    def like_main(b, w, n, m=1):
        some = main(b, w)
        return k.wd.at[b, pl.ds(0, n), pl.ds(0, m), 0, some] if w == "d" else whole[w].at[b, pl.ds(0, n), 0, some, pl.ds(0, m * D)]

    def like_rest(b, w, n):
        return k.wd.at[b, pl.ds(0, n), :, 0, rest] if w == "d" else whole[w].at[b, pl.ds(0, n), 0, rest]

    def w_z(b, w):
        for r in (1, 3, 2) if (b, w) in DIRECT else (1, 3):
            p = w_main(b, w, f)
            send(("wz", b, w), p, p, at_z(r))
        if (b, w) in SPLIT:
            for r in (1, 3):
                p = w_rest(b, w, f)
                send(("wr", b, w), p, p, at_z(r))

    def w_to_q(b, w, some):
        for r in some:
            for j in range(1, 4):
                p = w_main(b, w, z_peer[r])
                send(("wq", b, w), p, p, at_q(j))

    def w_zq(b, w):
        if (b, w) in DIRECT:
            wait("recv", ("wz", b, w), lambda: like_main(b, w, 3))
        else:
            wait("recv", ("wm", b, w), lambda: like_main(b, w, 1))
        if (b, w) in STEPS:
            for r in (1, 3, 2):
                p = w_main(b, w, z_peer[r])
                send(("w1", b, w), p, p, at(first))
        else:
            w_to_q(b, w, (1, 3, 2))

    def w_q2(b, w):
        wait("recv", ("w1", b, w), lambda: like_main(b, w, 3))
        for qi in (q, first):
            for r in (1, 3, 2):
                p = w_main(b, w, z_peer[r], qi)
                send(("wq", b, w), p, p, at(second))

    def w_relay(b, w):
        if (b, w) not in DIRECT:
            wait("recv", ("wz", b, w), lambda: like_main(b, w, 2))
            p = w_main(b, w, z_peer[3])
            send(("wm", b, w), p, p, at_z(1))
        if (b, w) in SPLIT:
            wait("recv", ("wr", b, w), lambda: like_rest(b, w, 2))
            p = w_rest(b, w, z_peer[3])
            send(("wo", b, w), p, p, at_z(1))
        if (b, w) not in DIRECT and (b, w) not in STEPS:
            w_to_q(b, w, (1, 3))

    def w_opposite(b, w):
        wait("recv", ("wm", b, w), lambda: like_main(b, w, 1))
        w_to_q(b, w, (2,))

    def w_qc(b, w):
        if (b, w) in SPLIT:
            wait("recv", ("wo", b, w), lambda: like_rest(b, w, 1))
        wait("recv", ("wq", b, w), lambda: like_main(b, w, 3, 2 if (b, w) in STEPS else 3))
        for r in range(1, F):
            p = w_half(b, w, z_peer[r])
            send(("wc", b, w), p, p, at_c())

    def w_ready(b, w):
        wait("recv", ("wc", b, w), lambda: k.wd.at[b, pl.ds(0, F - 1), :, 0] if w == "d" else whole[w].at[b, pl.ds(0, F - 1), 0])

    def cols():
        return one_hot((D, D // F), lambda r, s: r == f * (D // F) + s)

    def cond_tile():
        v = k.cd[...].astype(f32)
        a = v / (1.0 + jnp.exp(-v))
        k.cz[f] = jnp.concatenate([a] * 4, axis=0).astype(bf)

    def cond_z():
        for r in range(1, F):
            send(("cz",), k.cz.at[f], k.cz.at[f], at_z(r))

    def cond_zq():
        pick = one_hot((16, F * 16), lambda r, s: (r // 4 == s // 16) & (r % 4 == s % 16)).astype(bf)
        k.cg[q, c] = dot(pick, k.cz[...].reshape(F * 16, D)).astype(bf)
        for j in range(1, 4):
            send(("cq",), k.cg.at[q, c], k.cg.at[q, c], at_q(j))

    def cond_qc():
        wait("recv", ("cq",), lambda: k.cg.at[pl.ds(0, 3), 0])
        send(("cc",), k.cg.at[:, c], k.cg.at[:, c], at_c())

    def cond_ready():
        wait("recv", ("cc",), lambda: k.cg.at[:, 0])

    def tile_mask(n, p):
        r = lax.broadcasted_iota(jnp.int32, (n, 1), 0)
        return jnp.where((r // 4) % 4 == p, 1.0, 0.0)

    tiles = ((0, 1), (1, 3))

    def mod_partial(part):
        a = dot(k.cz[...].reshape(F * 16, D), cols().astype(bf))
        masked = [(a * tile_mask(F * 16, p)).astype(bf) for p in range(4)]
        lo, hi = tiles[part]
        for t in range(lo, hi):
            total = None
            for p in range(4):
                b, m = divmod(4 * t + p, 6)
                o = dot(masked[p], k.wa[b, :, m * D : (m + 1) * D])
                total = o if total is None else total + o
            k.ms[:, 16 * t : 16 * t + 16, :] = total.astype(bf).reshape(F, 16, D)
        some = pl.ds(16 * lo, 16 * (hi - lo))
        for r in range(1, F):
            send(("mz", part), k.ms.at[z_peer[r], some], k.mr.at[f, some], at_z(r))

    def mod_ready(part):
        lo, hi = tiles[part]
        some = slice(16 * lo, 16 * hi)
        wait("recv", ("mz", part), lambda: k.mr.at[pl.ds(0, F - 1), pl.ds(16 * lo, 16 * (hi - lo))])
        total = k.ms[f, some].astype(f32)
        for r in range(1, F):
            total = total + k.mr[z_peer[r], some].astype(f32)
        k.mod[2 * lo : 2 * hi] = total.reshape(2 * (hi - lo), 2 * I, D)

    def piece(b, i, p):
        at = p % 2 * I + i
        return k.mod[3 * b + p // 2, at : at + 1, :]

    def dm_row(b, i, p, v):
        to, at = (k.dm, (p - 2) * I + i) if p >= 2 else (k.dl, p * I + i)
        to[b, at : at + 1, :] = v

    def dm_pieces(t):
        return [(t, p + 2) for p in range(4)] if t < B else [(p // 2, p % 2) for p in range(4)]

    def dm_start(t):
        k.dg[t, q, c, f] = (k.dm[t] if t < B else k.dl[...].reshape(4 * I, D)).astype(bf)
        for r in range(1, F):
            p = k.dg.at[t, q, c, f]
            send(("dz", t), p, p, at_z(r))

    def dm_zq(t):
        wait("recv", ("dz", t), lambda: k.dg.at[t, 0, 0, pl.ds(0, F - 1)])
        for j in range(1, 4):
            p = k.dg.at[t, q, c]
            send(("dq", t), p, p, at_q(j))

    def dm_qc(t):
        wait("recv", ("dq", t), lambda: k.dg.at[t, pl.ds(0, 3), 0])
        p = k.dg.at[t, :, c]
        send(("dc", t), p, p, at_c())

    def dm_ready(t):
        wait("recv", ("dc", t), lambda: k.dg.at[t, :, 0])

    def dcond_part(t):
        tile = k.dg[t, q, c].reshape(F * 16, D).astype(f32)
        acc = None
        for p, (b, m) in enumerate(dm_pieces(t)):
            o = dot((tile * tile_mask(F * 16, p)).astype(bf), k.wa[b, :, m * D : (m + 1) * D], NT)
            acc = o if acc is None else acc + o
        return acc

    def dcond_send():
        acc = dcond_part(0) + dcond_part(1) + dcond_part(2)
        fold = one_hot((F * 8, F * 16), lambda r, s: (r // 8 == s // 16) & (r % 8 == s % 4))
        t = exact_dot(exact_dot(fold, acc), cols(), NT)
        k.cs[...] = t.reshape(F, 8, D)
        for r in range(1, F):
            send(("gz",), k.cs.at[z_peer[r]], k.cr.at[f], at_z(r))

    def dcond_finish():
        wait("recv", ("gz",), lambda: k.cr.at[pl.ds(0, F - 1)])
        total = k.cs[f]
        for r in range(1, F):
            total = total + k.cr[z_peer[r]]
        v = k.cd[...].astype(f32)
        s = 1.0 / (1.0 + jnp.exp(-v))
        k.gc[:I] = total[:I] * (s * (1.0 + v * (1.0 - s)))
        local(("grad_cond",), k.gc.at[pl.ds(0, I)], out.grad_cond).start()

    def ada_copy(b, m):
        stage = (k.xs.at[1], k.mid.at[1])[b]
        return local(("ada", b, m), stage.at[pl.ds(m * (D // F), D // F)], out.grad_ada.at[b, :, pl.ds(m * D, D)])

    def grad_ada(t):
        n = GROUP * F * 16
        a = dot(k.cg[...].reshape(n // 4, D), cols().astype(bf)).astype(bf)
        spread = one_hot((n, n // 4), lambda r, s: (r // 16 == s // 4) & (r % 4 == s % 4)).astype(bf)
        a = dot(spread, a)
        tile = k.dg[t].reshape(n, D)
        for p, (b, m) in enumerate(dm_pieces(t)):
            stage = (k.xs.at[1], k.mid.at[1])[b]
            stage[m * (D // F) : (m + 1) * (D // F), :] = dot((a * tile_mask(n, p)).astype(bf), tile, TN)
            ada_copy(b, m).start()

    def width(w):
        return W if w[0] == "q" else D

    def g_local(w):
        return k.gq.at[int(w[1])] if w[0] == "q" else {"u": k.gu, "d": k.gd}[w]

    def g_halves(b, w):
        return k.hq.at[b, int(w[1])] if w[0] == "q" else {"u": k.hu, "d": k.hd}[w].at[b]

    def g_result(b, w):
        return k.oq.at[b, int(w[1])] if w[0] == "q" else {"u": k.ou, "d": k.od}[w].at[b]

    def g_buf(b, w, kind):
        return getattr(k, f"{kind}{w}{b}")

    def quarter(w, h, qi):
        return h.at[:, qi] if w == "d" else h.at[:, :, cut(qi, width(w))]

    def one_of(w, ref, j):
        return ref.at[q_peer[j]] if w == "d" else ref.at[:, cut(q_peer[j], width(w))]

    def r_piece(b, w):
        return k.od.at[b, q, c] if w == "d" else g_result(b, w).at[c, :, cut(q, width(w))]

    def r_half(b, w):
        return k.od.at[b, :, c] if w == "d" else g_result(b, w).at[c]

    def g_c(b, w):
        half = k.gd.at[:, :, other] if w == "d" else g_local(w).at[:, other]
        send(("gc", b, w), half, g_halves(b, w), at_c())

    def g_1(b, w):
        h = g_halves(b, w)
        for kind in ("send", "recv"):
            wait(kind, ("gc", b, w), lambda: g_halves(b, w))
        for n in range(F):
            own = k.gd[n, :, c] if w == "d" else g_local(w)[n, c]
            h[n] = h[n] + own
        how = METHOD[b][w]
        if how == "direct":
            for r, j in [(r, j) for r in range(F) for j in range(4)][1:]:
                send(("g1", b, w), h.at[z_peer[r], :, cut(q_peer[j], W)], g_buf(b, w, "a").at[r * 4 + j], at_q(j, r))
        elif how == "steps":
            for n, qi in enumerate((first, across)):
                send(("gt", b, w), quarter(w, h, qi), g_buf(b, w, "t").at[n], at(first))
        elif how == "ring":
            send(("gt", b, w), h.at[z_peer[2]], g_buf(b, w, "t"), at_z(1))
        else:
            for j in range(1, 4):
                send(("g1", b, w), quarter(w, h, q_peer[j]), g_buf(b, w, "a").at[j - 1], at_q(j))

    def g_fly(b, w):
        h, t = g_halves(b, w), g_buf(b, w, "t")
        wait("recv", ("gt", b, w), lambda: t)
        for n, qi in enumerate((q, second)):
            p = quarter(w, h, qi)
            p[...] = p[...] + t[n]
        send(("g1", b, w), quarter(w, h, second), g_buf(b, w, "a"), at(second))

    def g_ring(b, w):
        h, t = g_halves(b, w), g_buf(b, w, "t")
        wait("recv", ("gt", b, w), lambda: t)
        h[z_peer[1]] = h[z_peer[1]] + t[...]
        for n, r in enumerate((1, 3)):
            send(("g1", b, w), h.at[z_peer[r]], g_buf(b, w, "a").at[n], at_z(r))

    def g_direct(b, w):
        h, a = g_halves(b, w), g_buf(b, w, "a")
        wait("recv", ("g1", b, w), lambda: a.at[pl.ds(0, 4 * F - 1)])
        total = h[f, :, cut(q, W)].astype(f32)
        for n in range(1, 4 * F):
            total = total + a[n].astype(f32)
        hand_back(b, w, total)

    def hand_back(b, w, total):
        p = r_piece(b, w)
        p[...] = total.astype(bf)
        for j in range(1, 4):
            send(("g3", b, w), p, p, at_q(j))
        if (b, w) in ONE:
            for j in range(4):
                send(("g3", b, w), p, p, at_c(j))

    def g_2(b, w):
        h, a, s = g_halves(b, w), g_buf(b, w, "a"), g_buf(b, w, "s")
        wait("recv", ("g1", b, w), lambda: a)
        if METHOD[b][w] == "ring":
            total = h[f].astype(f32) + a[0].astype(f32) + a[1].astype(f32)
            s[...] = total.astype(bf)
            for j in range(1, 4):
                send(("g2", b, w), one_of(w, s, j), g_buf(b, w, "b").at[j - 1], at_q(j))
        else:
            if METHOD[b][w] == "steps":
                s[...] = quarter(w, h, q)[...] + a[...]
            else:
                total = quarter(w, h, q)[...].astype(f32)
                for j in range(3):
                    total = total + a[j].astype(f32)
                s[...] = total.astype(bf)
            for r in range(1, F):
                send(("g2", b, w), s.at[z_peer[r]], g_buf(b, w, "b").at[f], at_z(r))

    def g_3(b, w):
        s, a = g_buf(b, w, "s"), g_buf(b, w, "b")
        if METHOD[b][w] == "ring":
            wait("recv", ("g2", b, w), lambda: a)
            total = one_of(w, s, 0)[...].astype(f32)
            for j in range(3):
                total = total + a[j].astype(f32)
        else:
            wait("recv", ("g2", b, w), lambda: a.at[pl.ds(0, F - 1)])
            total = s[f].astype(f32)
            for r in range(1, F):
                total = total + a[z_peer[r]].astype(f32)
        hand_back(b, w, total)

    def g_4(b, w):
        wait("recv", ("g3", b, w), lambda: k.od.at[b, pl.ds(0, 3), 0] if w == "d" else g_result(b, w).at[0, :, pl.ds(0, 3 * width(w))])
        send(("g4", b, w), r_half(b, w), r_half(b, w), at_c())

    def out_copy(b, w):
        to = out.grad_q.at[b, int(w[1])] if w[0] == "q" else {"u": out.grad_u, "d": out.grad_d}[w].at[b]
        return local(("out", b, w), g_result(b, w), to)

    def seven(b, w):
        return k.act.at[pl.ds(0, 7 * R), pl.ds(0, width(w))]

    def g_5(b, w):
        if (b, w) in ONE:
            wait("recv", ("g3", b, w), lambda: seven(b, w))
        else:
            wait("recv", ("g4", b, w), lambda: k.od.at[b, :, 0] if w == "d" else g_result(b, w).at[0])
        out_copy(b, w).start()

    def m_qkv(b):
        return k.wq[b, :, :, :, : 3 * D].reshape(D, 3 * D)

    def m_proj(b):
        return k.wq[b, :, :, :, 3 * D :].reshape(D, D)

    def m_up(b, at, n):
        return k.wu[b, :, :, :, at : at + n].reshape(D, n)

    def m_down(b):
        return k.wd[b].reshape(FF, D)

    def state(b, i):
        return k.xs[b, rows(i), :]

    def lane_masks():
        lane = lax.broadcasted_iota(jnp.int32, (1, 2 * HS), 1)
        lo = jnp.where(lane < HS, 1.0, 0.0)
        return lo.astype(bf), (1.0 - lo).astype(bf)

    def head_cols(p, which):
        return slice(p * D + which * W, p * D + (which + 1) * W)

    def fwd_norm(b, i):
        hat, _ = norm_hat(state(b, i))
        k.fi[b, rows(i), :] = (hat * (1.0 + piece(b, i, 1)) + piece(b, i, 0)).astype(bf)

    def fwd_qkv(b, i):
        r = rows(i)
        y = dot(k.fi[b, r, :], m_qkv(b))
        for p in range(PAIRS):
            s = head_cols(p, 0)
            k.qkv[b, r, s] = (y[:, s] * HS**-0.5).astype(bf)
            s = slice(p * D + W, (p + 1) * D)
            k.qkv[b, r, s] = y[:, s].astype(bf)

    def fwd_probs(b, i):
        masks = lane_masks()
        for p in range(PAIRS):
            qs = k.qkv[b, rows(i), head_cols(p, 0)]
            ks = k.qkv[b, rows(i), head_cols(p, 1)]
            both = dot(jnp.concatenate([ks * m for m in masks], axis=0), qs, NT)
            for m in range(2):
                scores = both[m * L : (m + 1) * L]
                ex = jnp.exp(scores - jnp.max(scores, axis=0, keepdims=True))
                k.pt[i * HEADS + 2 * p + m] = (ex * (1.0 / jnp.sum(ex, axis=0, keepdims=True))).astype(bf)

    def fwd_mix(b, i):
        mixed = []
        for p in range(PAIRS):
            vt = k.qkv[b, rows(i), head_cols(p, 2)].T
            for m in range(2):
                mixed.append(dot(vt[m * HS : (m + 1) * HS], k.pt[i * HEADS + 2 * p + m]))
        k.mt[b, :, rows(i)] = jnp.concatenate(mixed, axis=0).astype(bf)

    def fwd_proj(b, i):
        r = rows(i)
        att = dot(k.mt[b, :, r], m_proj(b), TN)
        k.att[b, r, :] = att.astype(bf)
        mid = state(b, i) + piece(b, i, 2) * att
        k.mid[b, r, :] = mid
        hat, _ = norm_hat(mid)
        k.si[b, r, :] = (hat * (1.0 + piece(b, i, 4)) + piece(b, i, 3)).astype(bf)

    def fwd_up(b):
        n = FF // 3
        for j in range(3):
            s = slice(j * n, (j + 1) * n)
            x = dot(k.si[b], m_up(b, j * n, n))
            a, slope = gelu_parts(x)
            k.act[:, s] = a.astype(bf)
            k.hid[:, s] = slope.astype(bf)

    def fwd_down(b):
        acc = dot(k.act[...], m_down(b))
        k.br[b] = acc.astype(bf)
        for i in images:
            r = rows(i)
            k.xs[b + 1, r, :] = k.mid[b, r, :] + piece(b, i, 5) * acc[r]

    def turn():
        for i in images:
            r = rows(i)
            k.da[r, :] = k.xs[B, r, :].astype(bf)
            k.xs[B, r, :] = k.db[r, :].astype(f32) * inp.mask[i].astype(f32)

    def bwd_hidden(b):
        for i in images:
            r = rows(i)
            g = k.xs[B, r, :]
            dm_row(b, i, 5, jnp.sum(g * k.br[b, r, :].astype(f32), axis=0, keepdims=True))
            k.db[r, :] = (g * piece(b, i, 5)).astype(bf)
        n = FF // 2
        for h in range(2):
            r = slice(h * T // 2, (h + 1) * T // 2)
            for j in range(2):
                s = slice(j * n, (j + 1) * n)
                da = dot(k.db[r, :], m_down(b)[s], NT)
                k.hid[r, s] = (k.hid[r, s].astype(f32) * da).astype(bf)

    def bwd_second(b):
        acc = dot(k.hid[...], m_up(b, 0, FF), NT)
        for i in images:
            r = rows(i)
            d = acc[r]
            hat, rs = norm_hat(k.mid[b, r, :])
            dm_row(b, i, 3, jnp.sum(d, axis=0, keepdims=True))
            dm_row(b, i, 4, jnp.sum(d * hat, axis=0, keepdims=True))
            d_mid = k.xs[B, r, :] + norm_back(d * (1.0 + piece(b, i, 4)), hat, rs)
            k.xs[B, r, :] = d_mid
            dm_row(b, i, 2, jnp.sum(d_mid * k.att[b, r, :].astype(f32), axis=0, keepdims=True))
            k.da[r, :] = (d_mid * piece(b, i, 2)).astype(bf)

    def grad_down(b):
        n = FF // 2
        for h in range(2):
            x = dot(k.act[:, h * n : (h + 1) * n], k.db[...], TN)
            k.gd[h * F // 2 : (h + 1) * F // 2] = x.astype(bf).reshape(F // 2, 4, 2, R, D)

    def grad_up(b):
        n = FF // 2
        for h in range(2):
            s = slice(h * n, (h + 1) * n)
            k.gu[:, :, :, s] = dot(k.si[b], k.hid[:, s], TN).astype(bf).reshape(F, 2, R, n)

    def grad_proj(b):
        x = dot(k.mt[b], k.da[...]).astype(bf).reshape(F, 2, R, D)
        for p in range(PAIRS):
            k.gq[p, :, :, :, 3 * W :] = x[:, :, :, p * W : (p + 1) * W]

    def grad_qkv(b, p):
        x = dot(k.fi[b], k.qkv[b, :, p * D : (p + 1) * D], TN)
        k.gq[p, :, :, :, : 3 * W] = x.astype(bf).reshape(F, 2, R, 3 * W)

    def bwd_heads(b, p):
        masks = lane_masks()

        def ds_at(i, m):
            return slice(i * L, (i + 1) * L), slice(m * L, (m + 1) * L)

        wp = m_proj(b)[p * W : (p + 1) * W]
        for i in images:
            r = rows(i)
            do = dot(k.da[r, :], wp, NT).astype(bf)
            k.db[r, :W] = do
            vs = k.qkv[b, r, head_cols(p, 2)]
            both = dot(jnp.concatenate([vs * m for m in masks], axis=0), do, NT)
            for m in range(2):
                dp = both[m * L : (m + 1) * L]
                pf = k.pt[i * HEADS + 2 * p + m].astype(f32)
                w = pf * dp
                k.act[ds_at(i, m)] = (w - pf * jnp.sum(w, axis=0, keepdims=True)).astype(bf)
        for i in images:
            r = rows(i)
            do = k.db[r, :W]
            qs = k.qkv[b, r, head_cols(p, 0)]
            ks = k.qkv[b, r, head_cols(p, 1)]
            kt = ks.T
            ds = [k.act[ds_at(i, m)] for m in range(2)]
            pt = [k.pt[i * HEADS + 2 * p + m] for m in range(2)]
            dk = dot(ds[0], qs * masks[0]) + dot(ds[1], qs * masks[1])
            dv = dot(pt[0], do * masks[0]) + dot(pt[1], do * masks[1])
            dq = jnp.concatenate([dot(kt[m * HS : (m + 1) * HS], ds[m]) for m in range(2)], axis=0)
            k.qkv[b, r, head_cols(p, 1)] = dk.astype(bf)
            k.qkv[b, r, head_cols(p, 2)] = dv.astype(bf)
            k.qkv[b, r, head_cols(p, 0)] = (dq * HS**-0.5).astype(bf).T

    def bwd_first(b, some):
        for i in some:
            r = rows(i)
            d = dot(k.qkv[b, r, :], m_qkv(b), NT)
            hat, rs = norm_hat(state(b, i))
            dm_row(b, i, 0, jnp.sum(d, axis=0, keepdims=True))
            dm_row(b, i, 1, jnp.sum(d * hat, axis=0, keepdims=True))
            k.xs[B, r, :] = k.xs[B, r, :] + norm_back(d * (1.0 + piece(b, i, 1)), hat, rs)

    def run(*todo):
        for fn, *args in todo:
            fn(*args)

    def each(fn, b):
        for i in images:
            fn(b, i)

    def keep(name):
        return local(("keep", name), getattr(k, name), getattr(out, name))

    def fetch(name):
        return local(("fetch", name), getattr(out, name), getattr(k, name))

    def keep_start(name):
        keep(name).start()

    def keep_wait(name):
        keep(name).wait()

    def fetch_start(name):
        fetch(name).start()

    def fetch_wait(name):
        fetch(name).wait()

    def out_wait():
        local(("os",), k.da, out.output).wait()

    def at_block(b, which, *todo):
        pl.when(b == which)(functools.partial(run, *todo))

    def phase(*todo):
        pl.when(me >= 0)(functools.partial(run, *todo))

    barrier = pltpu.get_barrier_semaphore()
    everyone = [at_q(j, r) for r in range(F) for j in range(4)][1:] + [at_c(j) for j in range(4)]
    for peer in everyone:
        pl.semaphore_signal(barrier, inc=1, device_id=peer, device_id_type=MESH)
    cond_load = local(("cd",), inp.cond, k.cd)
    cond_load.start()
    ada_load = local(("wa",), inp.ada, k.wa)
    w_loads = {"q": [], "u": [local(("wu",), inp.up_w, k.wu.at[:, f])], "d": [local(("wd",), inp.down_w, k.wd.at[:, f])]}
    for which in range(3):
        for p in range(PAIRS):
            w_loads["q"].append(
                local(
                    ("wq", which, p),
                    inp.qkv_w.at[:, :, :, pl.ds(which * D + p * W, W)],
                    k.wq.at[:, f, :, :, pl.ds(p * D + which * W, W)],
                )
            )
    w_loads["q"].append(local(("wp",), inp.proj_w, k.wq.at[:, f, :, :, pl.ds(3 * D, D)]))
    other_loads = [local(("tk",), inp.tokens, k.da), local(("db",), inp.cotangent, k.db)]
    for copy in w_loads["q"] + [ada_load] + w_loads["u"] + w_loads["d"] + other_loads:
        copy.start()
    cond_load.wait()
    cond_tile()
    for copy in w_loads["q"] + [ada_load] + w_loads["u"] + w_loads["d"] + other_loads:
        copy.wait()
    for i in images:
        k.xs[0, rows(i), :] = k.da[rows(i), :].astype(f32)
    pl.semaphore_wait(barrier, len(everyone))

    run((cond_z,), (w_z, 1, "q"), (w_z, 0, "q"), (wait, "recv", ("cz",), k.cz.at[pl.ds(0, F - 1)]), (w_z, 0, "u"), (mod_partial, 0), (w_z, 0, "d"), (w_relay, 1, "q"), (cond_zq,), (w_zq, 0, "q"), (w_zq, 0, "u"), (w_z, 1, "u"), (mod_ready, 0))

    def forward(step, _):
        b = step
        phase((each, fwd_norm, b),)
        at_block(b, 0, (w_zq, 0, "d"), (w_relay, 0, "d"), (w_qc, 0, "q"), (mod_partial, 1), (w_opposite, 1, "q"), (w_ready, 0, "q"))
        phase((each, fwd_qkv, b),)
        at_block(b, 0, (w_relay, 1, "u"), (w_z, 1, "d"))
        at_block(b, 1, (w_qc, 1, "u"),)
        at_block(b, 1, (keep_wait, "pt"),)
        phase((each, fwd_probs, b), (each, fwd_mix, b))
        at_block(b, 0, (keep_start, "pt"))
        at_block(b, 0, (w_qc, 0, "u"), (mod_ready, 1))
        phase((each, fwd_proj, b),)
        at_block(b, 0, (w_ready, 0, "u"), (w_qc, 0, "d"), (w_opposite, 1, "u"))
        at_block(b, 1, (w_ready, 1, "u"),)
        at_block(b, 1, (keep_wait, "hid"), (keep_wait, "act"))
        phase((fwd_up, b),)
        at_block(b, 0, (keep_start, "hid"), (keep_start, "act"))
        at_block(b, 0, (w_qc, 1, "q"), (w_ready, 0, "d"), (w_zq, 1, "d"))
        at_block(b, 1, (w_qc, 1, "d"), (w_ready, 1, "d"))
        phase((fwd_down, b),)
        at_block(b, 0, (w_relay, 1, "d"), (w_ready, 1, "q"))
        return 0

    lax.fori_loop(0, B, forward, 0)
    phase((turn,),)
    out_load = local(("os",), k.da, out.output)
    out_load.start()

    def backward(step, _):
        b = B - 1 - step
        at_block(b, 0, (fetch_wait, "hid"))
        phase((bwd_hidden, b),)
        at_block(b, 0, (dm_zq, 1),)
        phase((grad_up, b),)
        at_block(b, 1, (g_c, 1, "u"),)
        at_block(b, 0, (g_c, 0, "u"), (g_fly, 1, "q0"), (g_3, 1, "u"), (g_2, 1, "d"))
        at_block(b, 0, (fetch_wait, "act"))
        phase((grad_down, b),)
        at_block(b, 1, (g_c, 1, "d"), (g_1, 1, "u"))
        at_block(b, 0, (g_c, 0, "d"), (g_1, 0, "u"), (g_fly, 1, "q1"))
        at_block(b, B - 1, (out_wait,))
        phase((bwd_second, b),)
        at_block(b, 1, (fetch_start, "hid"))
        at_block(b, 1, (g_1, 1, "d"), (dm_start, 1))
        at_block(b, 0, (g_1, 0, "d"), (dm_start, 0), (g_2, 1, "q0"))
        phase((grad_proj, b),)
        at_block(b, 0, (fetch_wait, "pt"))
        phase((bwd_heads, b, 0),)
        at_block(b, 0, (g_4, 1, "u"),)
        phase((grad_qkv, b, 0),)
        at_block(b, 1, (g_c, 1, "q0"),)
        at_block(b, 0, (g_c, 0, "q0"),)
        phase((bwd_heads, b, 1),)
        at_block(b, 1, (g_1, 1, "q0"),)
        at_block(b, 0, (g_1, 0, "q0"), (g_5, 1, "u"))
        phase((grad_qkv, b, 1),)
        at_block(b, 1, (g_c, 1, "q1"),)
        at_block(b, 0, (g_c, 0, "q1"),)
        phase((bwd_heads, b, 2),)
        at_block(b, 1, (fetch_start, "pt"), (fetch_start, "act"))
        at_block(b, 1, (g_1, 1, "q1"), (g_2, 1, "u"))
        at_block(b, 0, (g_1, 0, "q1"), (g_3, 1, "d"), (g_2, 0, "u"), (g_3, 1, "q0"), (g_2, 1, "q1"))
        phase((grad_qkv, b, 2),)
        at_block(b, 1, (g_c, 1, "q2"),)
        at_block(b, 0, (g_c, 0, "q2"),)
        phase((bwd_first, b, images[: I // 2]),)
        at_block(b, 0, (g_fly, 0, "d"), (g_ring, 0, "q0"), (g_1, 0, "q2"))
        phase((bwd_first, b, images[I // 2 :]),)
        at_block(b, 1, (g_1, 1, "q2"),)
        return 0

    lax.fori_loop(0, B, backward, 0)
    run((dm_start, 2),)
    g_load = local(("g",), k.xs.at[B], out.grad_tokens)
    g_load.start()
    run((g_fly, 0, "q1"), (cond_qc,), (g_2, 1, "q2"), (dm_qc, 1), (dm_zq, 0), (g_4, 1, "d"), (g_4, 1, "q0"), (cond_ready,), (dm_ready, 1), (grad_ada, 1), (g_5, 1, "d"), (g_5, 1, "q0"), (g_2, 0, "d"), (g_3, 0, "u"), (g_3, 1, "q1"), (g_2, 0, "q2"), (g_2, 0, "q1"), (g_2, 0, "q0"), (dm_zq, 2), (dcond_send,), (dm_qc, 0), (g_3, 1, "q2"), (g_4, 0, "u"), (dm_ready, 0), (grad_ada, 0), (g_4, 1, "q1"), (g_3, 0, "q0"), (g_5, 0, "u"), (g_3, 0, "d"), (g_5, 1, "q1"), (g_3, 0, "q2"), (dm_qc, 2), (g_4, 1, "q2"), (g_3, 0, "q1"), (dm_ready, 2), (grad_ada, 2), (g_4, 0, "q0"), (g_5, 1, "q2"), (dcond_finish,), (g_5, 0, "q0"), (g_4, 0, "d"), (g_4, 0, "q2"), (g_5, 0, "d"), (all_sent,), (g_5, 0, "q1"), (g_5, 0, "q2"), (all_sent,))
    g_load.wait()
    local(("grad_cond",), k.gc.at[pl.ds(0, I)], out.grad_cond).wait()
    for b in range(B):
        for m in range(6):
            ada_copy(b, m).wait()
        for w in KINDS:
            out_copy(b, w).wait()
    assert len(index) <= N_SEMS and len(local_index) <= N_LOCAL


def finish(*refs):
    n = len(OUTPUTS)
    src, dst, high, sems = refs[:n], refs[n : 2 * n + 1], refs[2 * n + 1 : -1], refs[-1]
    B, pairs, _, R, four = src[4].shape
    W = four // 4
    D = W * pairs
    copies = []

    def copy(a, b):
        copies.append(pltpu.make_async_copy(a, b, sems.at[len(copies)]))
        copies[-1].start()

    for m in range(4):
        copy(src[m], dst[m])
    qkv, proj, up, down = high
    for b in range(B):
        for p in range(pairs):
            x = src[4][b, p].reshape(2 * R, 4 * W).astype(f32)
            for j in range(3):
                qkv[b, :, j * D + p * W : j * D + (p + 1) * W] = x[:, j * W : (j + 1) * W]
            proj[b, :, p * W : (p + 1) * W] = x[:, 3 * W :]
    copy(qkv, dst[4])
    copy(proj, dst[5])
    up[...] = src[5][...].reshape(up.shape).astype(f32)
    copy(up, dst[6])
    down[...] = src[6][...].reshape(down.shape).astype(f32)
    copy(down, dst[7])
    for c in copies:
        c.wait()


def body(F, tokens, cond, cotangent, keep_mask, w_ada, w_qkv, w_proj, w_up, w_down):
    I, L, D = tokens.shape
    B, _, FF = w_up.shape
    R = D // F // 2
    W = D // PAIRS
    T = I * L
    shapes = scratch(F, I, L, D, FF, B)
    names = tuple(shapes)
    anywhere = pl.BlockSpec(memory_space=pl.ANY)
    results = [
        jax.ShapeDtypeStruct((T, D), bf),
        jax.ShapeDtypeStruct((T, D), f32),
        jax.ShapeDtypeStruct((I, D), f32),
        jax.ShapeDtypeStruct((B, D // F, 6 * D), f32),
        jax.ShapeDtypeStruct((B, PAIRS, 2, R, 4 * W), bf),
        jax.ShapeDtypeStruct((B, 2, R, FF), bf),
        jax.ShapeDtypeStruct((B, 4, 2, R, D), bf),
    ]
    found = pl.pallas_call(
        functools.partial(kernel, names, F, I, L, D, FF, B),
        name="blocks",
        out_shape=[pltpu.VMEM(r.shape, r.dtype) for r in results] + [jax.ShapeDtypeStruct(*shapes[n]) for n in KEPT],
        in_specs=[pl.BlockSpec(memory_space=pltpu.SMEM) if n == "mask" else anywhere for n in INPUTS],
        out_specs=[anywhere] * len(OUTPUTS) + [pl.BlockSpec(memory_space=pltpu.HBM)] * len(KEPT),
        scratch_shapes=[pltpu.VMEM(*shapes[n]) for n in names]
        + [pltpu.SemaphoreType.DMA((N_SEMS,)), pltpu.SemaphoreType.DMA((N_LOCAL,))],
        compiler_params=pltpu.CompilerParams(
            collective_id=0, has_side_effects=True, vmem_limit_bytes=56 * 2**20 + 2**19
        ),
    )(
        tokens.reshape(T, D),
        cond,
        cotangent.reshape(T, D),
        keep_mask,
        w_ada,
        w_qkv.reshape(B, 2, R, 3 * D),
        w_proj.reshape(B, 2, R, D),
        w_up.reshape(B, 2, R, FF),
        w_down.reshape(B, 4, 2, R, D),
    )
    grads = [(B, 2 * R, 3 * D), (B, 2 * R, D), (B, 2 * R, FF), (B, 8 * R, D)]
    output, grad_tokens, grad_cond, *weights = pl.pallas_call(
        finish,
        name="finish",
        out_shape=results[:4] + [jax.ShapeDtypeStruct(s, f32) for s in grads],
        in_specs=[pl.BlockSpec(memory_space=pltpu.VMEM)] * len(OUTPUTS),
        out_specs=[anywhere] * 8,
        scratch_shapes=[pltpu.VMEM(s, f32) for s in grads] + [pltpu.SemaphoreType.DMA((8,))],
        compiler_params=pltpu.CompilerParams(vmem_limit_bytes=40 * 2**20),
    )(*found[: len(OUTPUTS)])
    if lax.axis_size("dp") > GROUP:
        first = lax.axis_index("dp") % GROUP == 0
        weights = lax.psum(tuple(jnp.where(first, w, 0.0) for w in weights), "dp")
    return (output.reshape(I, L, D), grad_tokens.reshape(I, L, D), grad_cond, *weights)


def solution(mesh):
    slots = P(("dp", "fsdp"), None, None)
    weight = P(None, "fsdp", None)
    return jax.shard_map(
        functools.partial(body, mesh.shape["fsdp"]),
        mesh=mesh,
        in_specs=(slots, P(("dp", "fsdp"), None), slots, P(("dp", "fsdp"))) + (weight,) * 5,
        out_specs=(slots, slots, P(("dp", "fsdp"), None)) + (weight,) * 5,
        check_vma=False,
    )
```

```python
import functools

import jax
import jax.numpy as jnp
from jax import lax
from jax.experimental import pallas as pl
from jax.experimental.pallas import tpu as pltpu
from jax.sharding import PartitionSpec as P

MESH = pl.DeviceIdType.MESH
bf, f32 = jnp.bfloat16, jnp.float32
HEADS = 6
PAIRS = HEADS // 2
GROUP = 8
NN = (((1,), (0,)), ((), ()))
NT = (((1,), (1,)), ((), ()))
TN = (((0,), (0,)), ((), ()))
GELU_A = 0.7978845608028654
GELU_B = GELU_A * 0.044715
KINDS = ("u", "d", "q0", "q1", "q2")
SPLIT = ((0, "q"), (1, "d"))
DIRECT = ((0, "d"), (0, "q"), (1, "d"), (1, "u"))
STEPS = ()
ONE = ((0, "q2"),)
METHOD = (
    {"u": "ring", "d": "steps", "q0": "steps", "q1": "q", "q2": "q"},
    {"u": "q", "d": "q", "q0": "q", "q1": "q", "q2": "q"},
)


def dot(a, b, dims=NN):
    return lax.dot_general(a, b, dims, preferred_element_type=f32)


def exact_dot(a, b, dims=NN):
    return lax.dot_general(a, b, dims, precision=lax.Precision.HIGHEST, preferred_element_type=f32)


def one_hot(shape, hit):
    r = lax.broadcasted_iota(jnp.int32, shape, 0)
    c = lax.broadcasted_iota(jnp.int32, shape, 1)
    return jnp.where(hit(r, c), 1.0, 0.0)


def norm_hat(v):
    c = v - jnp.mean(v, -1, keepdims=True)
    r = lax.rsqrt(jnp.mean(c * c, -1, keepdims=True) + 1e-6)
    return c * r, r


def norm_back(dx, hat, r):
    return r * (dx - jnp.mean(dx, -1, keepdims=True) - hat * jnp.mean(dx * hat, -1, keepdims=True))


def gelu_parts(x):
    x2 = x * x
    t = jnp.tanh(x * (GELU_A + GELU_B * x2))
    up = 0.5 * t + 0.5
    a = x * up
    return a, a * (1.0 - t) * (GELU_A + (3 * GELU_B) * x2) + up


class Refs:
    pass


def scratch(F, I, L, D, FF, B):
    T = I * L
    R = D // F // 2
    W = D // PAIRS
    shapes = dict(
        wq=((B, F, 2, R, FF), bf),
        wu=((B, F, 2, R, FF), bf),
        wd=((B, F, 4, 2, R, D), bf),
        wa=((B, D // F, 6 * D), bf),
        xs=((B + 1, T, D), f32),
        fi=((B, T, D), bf),
        qkv=((B, T, 3 * D), bf),
        pt=((I * HEADS, L, L), bf),
        mt=((B, D, T), bf),
        att=((B, T, D), bf),
        mid=((B, T, D), f32),
        si=((B, T, D), bf),
        hid=((T, FF), bf),
        br=((B, T, D), bf),
        db=((T, D), bf),
        act=((T, FF), bf),
        da=((T, D), bf),
        mod=((B * 3, 2 * I, D), f32),
        dm=((B, 4 * I, D), f32),
        dl=((B, 2 * I, D), f32),
        cd=((I, D), bf),
        gc=((8, D), f32),
        ms=((F, B * 6 * I, D), bf),
        mr=((F, B * 6 * I, D), bf),
        cz=((F, 16, D), bf),
        cg=((4, 2, 16, D), bf),
        dg=((B + 1, 4, 2, F, 16, D), bf),
        cs=((F, 8, D), f32),
        cr=((F, 8, D), f32),
        gq=((PAIRS, F, 2, R, 4 * W), bf),
        gu=((F, 2, R, FF), bf),
        gd=((F, 4, 2, R, D), bf),
        hq=((B, PAIRS, F, R, 4 * W), bf),
        hu=((B, F, R, FF), bf),
        hd=((B, F, 4, R, D), bf),
        oq=((B, PAIRS, 2, R, 4 * W), bf),
        ou=((B, 2, R, FF), bf),
        od=((B, 4, 2, R, D), bf),
    )
    for block in range(B):
        for w in KINDS:
            n = W if w[0] == "q" else D
            four = (4, R, n) if w == "d" else (R, 4 * n)
            at = f"{w}{block}"
            if METHOD[block][w] == "direct":
                shapes["a" + at] = ((4 * F, R, n), bf)
            elif METHOD[block][w] == "ring":
                shapes["t" + at] = (four, bf)
                shapes["a" + at] = ((2, *four), bf)
                shapes["s" + at] = (four, bf)
                shapes["b" + at] = ((3, R, n), bf)
            else:
                if METHOD[block][w] == "steps":
                    shapes["t" + at] = ((2, F, R, n), bf)
                    shapes["a" + at] = ((F, R, n), bf)
                else:
                    shapes["a" + at] = ((3, F, R, n), bf)
                shapes["s" + at] = ((F, R, n), bf)
                shapes["b" + at] = ((F, R, n), bf)
    return shapes


INPUTS = ("tokens", "cond", "cotangent", "mask", "ada", "qkv_w", "proj_w", "up_w", "down_w")
OUTPUTS = ("output", "grad_tokens", "grad_cond", "grad_ada", "grad_q", "grad_u", "grad_d")
KEPT = ("pt", "hid", "act")
N_SEMS = 256
N_LOCAL = 64


def kernel(names, F, I, L, D, FF, B, *refs):
    n_in, n_out = len(INPUTS), len(OUTPUTS) + len(KEPT)
    inp, out, k = Refs(), Refs(), Refs()
    for name, ref in zip(INPUTS, refs[:n_in]):
        setattr(inp, name, ref)
    for name, ref in zip(OUTPUTS + KEPT, refs[n_in : n_in + n_out]):
        setattr(out, name, ref)
    for name, ref in zip(names, refs[n_in + n_out :]):
        setattr(k, name, ref)
    sems, local_sems = refs[-2], refs[-1]
    T = I * L
    R = D // F // 2
    W = D // PAIRS
    HS = D // HEADS
    images = range(I)

    me, f = lax.axis_index("dp"), lax.axis_index("fsdp")
    e = me % GROUP
    base = me - e
    c, q = e % 2, e // 2
    other = 1 - c
    z_peer = [(f + r) % F for r in range(F)]
    q_peer = [(q + j) % 4 for j in range(4)]

    def at_z(r):
        return (me, z_peer[r])

    x_next, y_next = q + 1 - 2 * (q % 2), (q + 2) % 4
    first = x_next * other + y_next * c
    second = x_next * c + y_next * other
    across = 6 - q - first - second

    def at(qi):
        return (base + 2 * qi + c, f)

    def at_q(j, r=0):
        return (base + 2 * q_peer[j] + c, z_peer[r])

    def at_c(j=0):
        return (base + 2 * q_peer[j] + other, f)

    def rows(i):
        return slice(i * L, (i + 1) * L)

    def cut(j, n):
        return pl.ds(pl.multiple_of(j * n, n), n)

    index = {}

    def sem(key):
        return sems.at[index.setdefault(key, len(index))]

    def send(key, src, dst, to):
        pltpu.make_async_remote_copy(
            src_ref=src,
            dst_ref=dst,
            send_sem=sem(("send",) + key),
            recv_sem=sem(("recv",) + key),
            device_id=to,
            device_id_type=MESH,
        ).start()

    unsent = []

    def wait(kind, key, like):
        if kind == "recv" and key[0] != "gc":
            unsent.append((key, like))
        done(kind, key, like)

    def done(kind, key, like):
        ref = like() if callable(like) else like
        pltpu.make_async_copy(ref, ref, sem((kind,) + key)).wait()

    def all_sent():
        while unsent:
            done("send", *unsent.pop(0))

    local_index = {}

    def local(key, src, dst):
        n = local_index.setdefault(key, len(local_index))
        return pltpu.make_async_copy(src, dst, local_sems.at[n])

    def loads(what):
        if what == "c":
            return [local(("cd",), inp.cond, k.cd)]
        if what == "a":
            return [local(("wa",), inp.ada, k.wa)]
        if what == "u":
            return [local(("wu",), inp.up_w, k.wu.at[:, f])]
        if what == "d":
            return [local(("wd",), inp.down_w, k.wd.at[:, f])]
        if what == "t":
            return [local(("tk",), inp.tokens, k.da), local(("db",), inp.cotangent, k.db)]
        return [
            local(
                ("wq", n, p),
                inp.qkv_w.at[:, :, :, pl.ds(n * D + p * W, W)],
                k.wq.at[:, f, :, :, pl.ds(p * D + n * W, W)],
            )
            for n in range(3)
            for p in range(PAIRS)
        ] + [local(("wp",), inp.proj_w, k.wq.at[:, f, :, :, pl.ds(3 * D, D)])]

    def load(what):
        for copy in loads(what):
            copy.start()

    arrived = set()

    def loaded(what):
        if what not in arrived:
            arrived.add(what)
            for copy in loads(what):
                copy.wait()

    def tokens_ready():
        loaded("t")
        for i in images:
            k.xs[0, rows(i), :] = k.da[rows(i), :].astype(f32)

    whole = {"q": k.wq, "u": k.wu, "d": k.wd}

    def main(b, w):
        return pl.ds(0, R * 2 // 3 if (b, w) in SPLIT else R)

    rest = pl.ds(R * 2 // 3, R // 3)

    def w_main(b, w, fz, qi=q):
        some = main(b, w)
        return k.wd.at[b, fz, qi, c, some] if w == "d" else whole[w].at[b, fz, c, some, cut(qi, D)]

    def w_rest(b, w, fz):
        return k.wd.at[b, fz, :, c, rest] if w == "d" else whole[w].at[b, fz, c, rest]

    def w_half(b, w, fz):
        return k.wd.at[b, fz, :, c] if w == "d" else whole[w].at[b, fz, c]

    def like_main(b, w, n, m=1):
        some = main(b, w)
        return k.wd.at[b, pl.ds(0, n), pl.ds(0, m), 0, some] if w == "d" else whole[w].at[b, pl.ds(0, n), 0, some, pl.ds(0, m * D)]

    def like_rest(b, w, n):
        return k.wd.at[b, pl.ds(0, n), :, 0, rest] if w == "d" else whole[w].at[b, pl.ds(0, n), 0, rest]

    def w_z(b, w):
        loaded(w)
        for r in (1, 3, 2) if (b, w) in DIRECT else (1, 3):
            p = w_main(b, w, f)
            send(("wz", b, w), p, p, at_z(r))
        if (b, w) in SPLIT:
            for r in (1, 3):
                p = w_rest(b, w, f)
                send(("wr", b, w), p, p, at_z(r))

    def w_to_q(b, w, some):
        for r in some:
            for j in range(1, 4):
                p = w_main(b, w, z_peer[r])
                send(("wq", b, w), p, p, at_q(j))

    def w_zq(b, w):
        if (b, w) in DIRECT:
            wait("recv", ("wz", b, w), lambda: like_main(b, w, 3))
        else:
            wait("recv", ("wm", b, w), lambda: like_main(b, w, 1))
        if (b, w) in STEPS:
            for r in (1, 3, 2):
                p = w_main(b, w, z_peer[r])
                send(("w1", b, w), p, p, at(first))
        else:
            w_to_q(b, w, (1, 3, 2))

    def w_q2(b, w):
        wait("recv", ("w1", b, w), lambda: like_main(b, w, 3))
        for qi in (q, first):
            for r in (1, 3, 2):
                p = w_main(b, w, z_peer[r], qi)
                send(("wq", b, w), p, p, at(second))

    def w_relay(b, w):
        if (b, w) not in DIRECT:
            wait("recv", ("wz", b, w), lambda: like_main(b, w, 2))
            p = w_main(b, w, z_peer[3])
            send(("wm", b, w), p, p, at_z(1))
        if (b, w) in SPLIT:
            wait("recv", ("wr", b, w), lambda: like_rest(b, w, 2))
            p = w_rest(b, w, z_peer[3])
            send(("wo", b, w), p, p, at_z(1))
        if (b, w) not in DIRECT and (b, w) not in STEPS:
            w_to_q(b, w, (1, 3))

    def w_opposite(b, w):
        wait("recv", ("wm", b, w), lambda: like_main(b, w, 1))
        w_to_q(b, w, (2,))

    def w_qc(b, w):
        if (b, w) in SPLIT:
            wait("recv", ("wo", b, w), lambda: like_rest(b, w, 1))
        wait("recv", ("wq", b, w), lambda: like_main(b, w, 3, 2 if (b, w) in STEPS else 3))
        for r in range(1, F):
            p = w_half(b, w, z_peer[r])
            send(("wc", b, w), p, p, at_c())

    def w_ready(b, w):
        wait("recv", ("wc", b, w), lambda: k.wd.at[b, pl.ds(0, F - 1), :, 0] if w == "d" else whole[w].at[b, pl.ds(0, F - 1), 0])

    def cols():
        return one_hot((D, D // F), lambda r, s: r == f * (D // F) + s)

    def cond_tile():
        v = k.cd[...].astype(f32)
        a = v / (1.0 + jnp.exp(-v))
        k.cz[f] = jnp.concatenate([a] * 4, axis=0).astype(bf)

    def cond_z():
        for r in range(1, F):
            send(("cz",), k.cz.at[f], k.cz.at[f], at_z(r))

    def cond_zq():
        pick = one_hot((16, F * 16), lambda r, s: (r // 4 == s // 16) & (r % 4 == s % 16)).astype(bf)
        k.cg[q, c] = dot(pick, k.cz[...].reshape(F * 16, D)).astype(bf)
        for j in range(1, 4):
            send(("cq",), k.cg.at[q, c], k.cg.at[q, c], at_q(j))

    def cond_qc():
        wait("recv", ("cq",), lambda: k.cg.at[pl.ds(0, 3), 0])
        send(("cc",), k.cg.at[:, c], k.cg.at[:, c], at_c())

    def cond_ready():
        wait("recv", ("cc",), lambda: k.cg.at[:, 0])

    def tile_mask(n, p):
        r = lax.broadcasted_iota(jnp.int32, (n, 1), 0)
        return jnp.where((r // 4) % 4 == p, 1.0, 0.0)

    tiles = ((0, 1), (1, 3))

    def mod_partial(part):
        loaded("a")
        a = dot(k.cz[...].reshape(F * 16, D), cols().astype(bf))
        masked = [(a * tile_mask(F * 16, p)).astype(bf) for p in range(4)]
        lo, hi = tiles[part]
        for t in range(lo, hi):
            total = None
            for p in range(4):
                b, m = divmod(4 * t + p, 6)
                o = dot(masked[p], k.wa[b, :, m * D : (m + 1) * D])
                total = o if total is None else total + o
            k.ms[:, 16 * t : 16 * t + 16, :] = total.astype(bf).reshape(F, 16, D)
        some = pl.ds(16 * lo, 16 * (hi - lo))
        for r in range(1, F):
            send(("mz", part), k.ms.at[z_peer[r], some], k.mr.at[f, some], at_z(r))

    def mod_ready(part):
        lo, hi = tiles[part]
        some = slice(16 * lo, 16 * hi)
        wait("recv", ("mz", part), lambda: k.mr.at[pl.ds(0, F - 1), pl.ds(16 * lo, 16 * (hi - lo))])
        total = k.ms[f, some].astype(f32)
        for r in range(1, F):
            total = total + k.mr[z_peer[r], some].astype(f32)
        k.mod[2 * lo : 2 * hi] = total.reshape(2 * (hi - lo), 2 * I, D)

    def piece(b, i, p):
        at = p % 2 * I + i
        return k.mod[3 * b + p // 2, at : at + 1, :]

    def dm_row(b, i, p, v):
        to, at = (k.dm, (p - 2) * I + i) if p >= 2 else (k.dl, p * I + i)
        to[b, at : at + 1, :] = v

    def dm_pieces(t):
        return [(t, p + 2) for p in range(4)] if t < B else [(p // 2, p % 2) for p in range(4)]

    def dm_start(t):
        k.dg[t, q, c, f] = (k.dm[t] if t < B else k.dl[...].reshape(4 * I, D)).astype(bf)
        for r in range(1, F):
            p = k.dg.at[t, q, c, f]
            send(("dz", t), p, p, at_z(r))

    def dm_zq(t):
        wait("recv", ("dz", t), lambda: k.dg.at[t, 0, 0, pl.ds(0, F - 1)])
        for j in range(1, 4):
            p = k.dg.at[t, q, c]
            send(("dq", t), p, p, at_q(j))

    def dm_qc(t):
        wait("recv", ("dq", t), lambda: k.dg.at[t, pl.ds(0, 3), 0])
        p = k.dg.at[t, :, c]
        send(("dc", t), p, p, at_c())

    def dm_ready(t):
        wait("recv", ("dc", t), lambda: k.dg.at[t, :, 0])

    def dcond_part(t):
        tile = k.dg[t, q, c].reshape(F * 16, D).astype(f32)
        acc = None
        for p, (b, m) in enumerate(dm_pieces(t)):
            o = dot((tile * tile_mask(F * 16, p)).astype(bf), k.wa[b, :, m * D : (m + 1) * D], NT)
            acc = o if acc is None else acc + o
        return acc

    def dcond_send():
        acc = dcond_part(0) + dcond_part(1) + dcond_part(2)
        fold = one_hot((F * 8, F * 16), lambda r, s: (r // 8 == s // 16) & (r % 8 == s % 4))
        t = exact_dot(exact_dot(fold, acc), cols(), NT)
        k.cs[...] = t.reshape(F, 8, D)
        for r in range(1, F):
            send(("gz",), k.cs.at[z_peer[r]], k.cr.at[f], at_z(r))

    def dcond_finish():
        wait("recv", ("gz",), lambda: k.cr.at[pl.ds(0, F - 1)])
        total = k.cs[f]
        for r in range(1, F):
            total = total + k.cr[z_peer[r]]
        v = k.cd[...].astype(f32)
        s = 1.0 / (1.0 + jnp.exp(-v))
        k.gc[:I] = total[:I] * (s * (1.0 + v * (1.0 - s)))
        local(("grad_cond",), k.gc.at[pl.ds(0, I)], out.grad_cond).start()

    def ada_copy(b, m):
        stage = (k.xs.at[1], k.mid.at[1])[b]
        return local(("ada", b, m), stage.at[pl.ds(m * (D // F), D // F)], out.grad_ada.at[b, :, pl.ds(m * D, D)])

    def grad_ada(t):
        n = GROUP * F * 16
        a = dot(k.cg[...].reshape(n // 4, D), cols().astype(bf)).astype(bf)
        spread = one_hot((n, n // 4), lambda r, s: (r // 16 == s // 4) & (r % 4 == s % 4)).astype(bf)
        a = dot(spread, a)
        tile = k.dg[t].reshape(n, D)
        for p, (b, m) in enumerate(dm_pieces(t)):
            stage = (k.xs.at[1], k.mid.at[1])[b]
            stage[m * (D // F) : (m + 1) * (D // F), :] = dot((a * tile_mask(n, p)).astype(bf), tile, TN)
            ada_copy(b, m).start()

    def width(w):
        return W if w[0] == "q" else D

    def g_local(w):
        return k.gq.at[int(w[1])] if w[0] == "q" else {"u": k.gu, "d": k.gd}[w]

    def g_halves(b, w):
        return k.hq.at[b, int(w[1])] if w[0] == "q" else {"u": k.hu, "d": k.hd}[w].at[b]

    def g_result(b, w):
        return k.oq.at[b, int(w[1])] if w[0] == "q" else {"u": k.ou, "d": k.od}[w].at[b]

    def g_buf(b, w, kind):
        return getattr(k, f"{kind}{w}{b}")

    def quarter(w, h, qi):
        return h.at[:, qi] if w == "d" else h.at[:, :, cut(qi, width(w))]

    def one_of(w, ref, j):
        return ref.at[q_peer[j]] if w == "d" else ref.at[:, cut(q_peer[j], width(w))]

    def r_piece(b, w):
        return k.od.at[b, q, c] if w == "d" else g_result(b, w).at[c, :, cut(q, width(w))]

    def r_half(b, w):
        return k.od.at[b, :, c] if w == "d" else g_result(b, w).at[c]

    def g_c(b, w):
        half = k.gd.at[:, :, other] if w == "d" else g_local(w).at[:, other]
        send(("gc", b, w), half, g_halves(b, w), at_c())

    def g_1(b, w):
        h = g_halves(b, w)
        for kind in ("send", "recv"):
            wait(kind, ("gc", b, w), lambda: g_halves(b, w))
        for n in range(F):
            own = k.gd[n, :, c] if w == "d" else g_local(w)[n, c]
            h[n] = h[n] + own
        how = METHOD[b][w]
        if how == "direct":
            for r, j in [(r, j) for r in range(F) for j in range(4)][1:]:
                send(("g1", b, w), h.at[z_peer[r], :, cut(q_peer[j], W)], g_buf(b, w, "a").at[r * 4 + j], at_q(j, r))
        elif how == "steps":
            for n, qi in enumerate((first, across)):
                send(("gt", b, w), quarter(w, h, qi), g_buf(b, w, "t").at[n], at(first))
        elif how == "ring":
            send(("gt", b, w), h.at[z_peer[2]], g_buf(b, w, "t"), at_z(1))
        else:
            for j in range(1, 4):
                send(("g1", b, w), quarter(w, h, q_peer[j]), g_buf(b, w, "a").at[j - 1], at_q(j))

    def g_fly(b, w):
        h, t = g_halves(b, w), g_buf(b, w, "t")
        wait("recv", ("gt", b, w), lambda: t)
        for n, qi in enumerate((q, second)):
            p = quarter(w, h, qi)
            p[...] = p[...] + t[n]
        send(("g1", b, w), quarter(w, h, second), g_buf(b, w, "a"), at(second))

    def g_ring(b, w):
        h, t = g_halves(b, w), g_buf(b, w, "t")
        wait("recv", ("gt", b, w), lambda: t)
        h[z_peer[1]] = h[z_peer[1]] + t[...]
        for n, r in enumerate((1, 3)):
            send(("g1", b, w), h.at[z_peer[r]], g_buf(b, w, "a").at[n], at_z(r))

    def g_direct(b, w):
        h, a = g_halves(b, w), g_buf(b, w, "a")
        wait("recv", ("g1", b, w), lambda: a.at[pl.ds(0, 4 * F - 1)])
        total = h[f, :, cut(q, W)].astype(f32)
        for n in range(1, 4 * F):
            total = total + a[n].astype(f32)
        hand_back(b, w, total)

    def hand_back(b, w, total):
        p = r_piece(b, w)
        p[...] = total.astype(bf)
        for j in range(1, 4):
            send(("g3", b, w), p, p, at_q(j))
        if (b, w) in ONE:
            for j in range(4):
                send(("g3", b, w), p, p, at_c(j))

    def g_2(b, w):
        h, a, s = g_halves(b, w), g_buf(b, w, "a"), g_buf(b, w, "s")
        wait("recv", ("g1", b, w), lambda: a)
        if METHOD[b][w] == "ring":
            total = h[f].astype(f32) + a[0].astype(f32) + a[1].astype(f32)
            s[...] = total.astype(bf)
            for j in range(1, 4):
                send(("g2", b, w), one_of(w, s, j), g_buf(b, w, "b").at[j - 1], at_q(j))
        else:
            if METHOD[b][w] == "steps":
                s[...] = quarter(w, h, q)[...] + a[...]
            else:
                total = quarter(w, h, q)[...].astype(f32)
                for j in range(3):
                    total = total + a[j].astype(f32)
                s[...] = total.astype(bf)
            for r in range(1, F):
                send(("g2", b, w), s.at[z_peer[r]], g_buf(b, w, "b").at[f], at_z(r))

    def g_3(b, w):
        s, a = g_buf(b, w, "s"), g_buf(b, w, "b")
        if METHOD[b][w] == "ring":
            wait("recv", ("g2", b, w), lambda: a)
            total = one_of(w, s, 0)[...].astype(f32)
            for j in range(3):
                total = total + a[j].astype(f32)
        else:
            wait("recv", ("g2", b, w), lambda: a.at[pl.ds(0, F - 1)])
            total = s[f].astype(f32)
            for r in range(1, F):
                total = total + a[z_peer[r]].astype(f32)
        hand_back(b, w, total)

    def g_4(b, w):
        wait("recv", ("g3", b, w), lambda: k.od.at[b, pl.ds(0, 3), 0] if w == "d" else g_result(b, w).at[0, :, pl.ds(0, 3 * width(w))])
        send(("g4", b, w), r_half(b, w), r_half(b, w), at_c())

    def out_copy(b, w):
        to = out.grad_q.at[b, int(w[1])] if w[0] == "q" else {"u": out.grad_u, "d": out.grad_d}[w].at[b]
        return local(("out", b, w), g_result(b, w), to)

    def seven(b, w):
        return k.act.at[pl.ds(0, 7 * R), pl.ds(0, width(w))]

    def g_5(b, w):
        if (b, w) in ONE:
            wait("recv", ("g3", b, w), lambda: seven(b, w))
        else:
            wait("recv", ("g4", b, w), lambda: k.od.at[b, :, 0] if w == "d" else g_result(b, w).at[0])
        out_copy(b, w).start()

    def m_qkv(b):
        return k.wq[b, :, :, :, : 3 * D].reshape(D, 3 * D)

    def m_proj(b):
        return k.wq[b, :, :, :, 3 * D :].reshape(D, D)

    def m_up(b, at, n):
        return k.wu[b, :, :, :, at : at + n].reshape(D, n)

    def m_down(b):
        return k.wd[b].reshape(FF, D)

    def state(b, i):
        return k.xs[b, rows(i), :]

    def lane_masks():
        lane = lax.broadcasted_iota(jnp.int32, (1, 2 * HS), 1)
        lo = jnp.where(lane < HS, 1.0, 0.0)
        return lo.astype(bf), (1.0 - lo).astype(bf)

    def head_cols(p, which):
        return slice(p * D + which * W, p * D + (which + 1) * W)

    def fwd_norm(b, i):
        hat, _ = norm_hat(state(b, i))
        k.fi[b, rows(i), :] = (hat * (1.0 + piece(b, i, 1)) + piece(b, i, 0)).astype(bf)

    def fwd_qkv(b, i):
        r = rows(i)
        y = dot(k.fi[b, r, :], m_qkv(b))
        for p in range(PAIRS):
            s = head_cols(p, 0)
            k.qkv[b, r, s] = (y[:, s] * HS**-0.5).astype(bf)
            s = slice(p * D + W, (p + 1) * D)
            k.qkv[b, r, s] = y[:, s].astype(bf)

    def fwd_probs(b, i):
        masks = lane_masks()
        for p in range(PAIRS):
            qs = k.qkv[b, rows(i), head_cols(p, 0)]
            ks = k.qkv[b, rows(i), head_cols(p, 1)]
            both = dot(jnp.concatenate([ks * m for m in masks], axis=0), qs, NT)
            for m in range(2):
                scores = both[m * L : (m + 1) * L]
                ex = jnp.exp(scores - jnp.max(scores, axis=0, keepdims=True))
                k.pt[i * HEADS + 2 * p + m] = (ex * (1.0 / jnp.sum(ex, axis=0, keepdims=True))).astype(bf)

    def fwd_mix(b, i):
        mixed = []
        for p in range(PAIRS):
            vt = k.qkv[b, rows(i), head_cols(p, 2)].T
            for m in range(2):
                mixed.append(dot(vt[m * HS : (m + 1) * HS], k.pt[i * HEADS + 2 * p + m]))
        k.mt[b, :, rows(i)] = jnp.concatenate(mixed, axis=0).astype(bf)

    def fwd_proj(b, i):
        r = rows(i)
        att = dot(k.mt[b, :, r], m_proj(b), TN)
        k.att[b, r, :] = att.astype(bf)
        mid = state(b, i) + piece(b, i, 2) * att
        k.mid[b, r, :] = mid
        hat, _ = norm_hat(mid)
        k.si[b, r, :] = (hat * (1.0 + piece(b, i, 4)) + piece(b, i, 3)).astype(bf)

    def fwd_up(b):
        n = FF // 3
        for j in range(3):
            s = slice(j * n, (j + 1) * n)
            x = dot(k.si[b], m_up(b, j * n, n))
            a, slope = gelu_parts(x)
            k.act[:, s] = a.astype(bf)
            k.hid[:, s] = slope.astype(bf)

    def fwd_down(b):
        acc = dot(k.act[...], m_down(b))
        k.br[b] = acc.astype(bf)
        for i in images:
            r = rows(i)
            k.xs[b + 1, r, :] = k.mid[b, r, :] + piece(b, i, 5) * acc[r]

    def turn():
        for i in images:
            r = rows(i)
            k.da[r, :] = k.xs[B, r, :].astype(bf)
            k.xs[B, r, :] = k.db[r, :].astype(f32) * inp.mask[i].astype(f32)

    def bwd_hidden(b):
        for i in images:
            r = rows(i)
            g = k.xs[B, r, :]
            dm_row(b, i, 5, jnp.sum(g * k.br[b, r, :].astype(f32), axis=0, keepdims=True))
            k.db[r, :] = (g * piece(b, i, 5)).astype(bf)
        n = FF // 2
        for h in range(2):
            r = slice(h * T // 2, (h + 1) * T // 2)
            for j in range(2):
                s = slice(j * n, (j + 1) * n)
                da = dot(k.db[r, :], m_down(b)[s], NT)
                k.hid[r, s] = (k.hid[r, s].astype(f32) * da).astype(bf)

    def bwd_second(b):
        acc = dot(k.hid[...], m_up(b, 0, FF), NT)
        for i in images:
            r = rows(i)
            d = acc[r]
            hat, rs = norm_hat(k.mid[b, r, :])
            dm_row(b, i, 3, jnp.sum(d, axis=0, keepdims=True))
            dm_row(b, i, 4, jnp.sum(d * hat, axis=0, keepdims=True))
            d_mid = k.xs[B, r, :] + norm_back(d * (1.0 + piece(b, i, 4)), hat, rs)
            k.xs[B, r, :] = d_mid
            dm_row(b, i, 2, jnp.sum(d_mid * k.att[b, r, :].astype(f32), axis=0, keepdims=True))
            k.da[r, :] = (d_mid * piece(b, i, 2)).astype(bf)

    def grad_down(b):
        n = FF // 2
        for h in range(2):
            x = dot(k.act[:, h * n : (h + 1) * n], k.db[...], TN)
            k.gd[h * F // 2 : (h + 1) * F // 2] = x.astype(bf).reshape(F // 2, 4, 2, R, D)

    def grad_up(b):
        n = FF // 2
        for h in range(2):
            s = slice(h * n, (h + 1) * n)
            k.gu[:, :, :, s] = dot(k.si[b], k.hid[:, s], TN).astype(bf).reshape(F, 2, R, n)

    def grad_proj(b):
        x = dot(k.mt[b], k.da[...]).astype(bf).reshape(F, 2, R, D)
        for p in range(PAIRS):
            k.gq[p, :, :, :, 3 * W :] = x[:, :, :, p * W : (p + 1) * W]

    def grad_qkv(b, p):
        x = dot(k.fi[b], k.qkv[b, :, p * D : (p + 1) * D], TN)
        k.gq[p, :, :, :, : 3 * W] = x.astype(bf).reshape(F, 2, R, 3 * W)

    def bwd_heads(b, p):
        masks = lane_masks()

        def ds_at(i, m):
            return slice(i * L, (i + 1) * L), slice(m * L, (m + 1) * L)

        wp = m_proj(b)[p * W : (p + 1) * W]
        for i in images:
            r = rows(i)
            do = dot(k.da[r, :], wp, NT).astype(bf)
            k.db[r, :W] = do
            vs = k.qkv[b, r, head_cols(p, 2)]
            both = dot(jnp.concatenate([vs * m for m in masks], axis=0), do, NT)
            for m in range(2):
                dp = both[m * L : (m + 1) * L]
                pf = k.pt[i * HEADS + 2 * p + m].astype(f32)
                w = pf * dp
                k.act[ds_at(i, m)] = (w - pf * jnp.sum(w, axis=0, keepdims=True)).astype(bf)
        for i in images:
            r = rows(i)
            do = k.db[r, :W]
            qs = k.qkv[b, r, head_cols(p, 0)]
            ks = k.qkv[b, r, head_cols(p, 1)]
            kt = ks.T
            ds = [k.act[ds_at(i, m)] for m in range(2)]
            pt = [k.pt[i * HEADS + 2 * p + m] for m in range(2)]
            dk = dot(ds[0], qs * masks[0]) + dot(ds[1], qs * masks[1])
            dv = dot(pt[0], do * masks[0]) + dot(pt[1], do * masks[1])
            dq = jnp.concatenate([dot(kt[m * HS : (m + 1) * HS], ds[m]) for m in range(2)], axis=0)
            k.qkv[b, r, head_cols(p, 1)] = dk.astype(bf)
            k.qkv[b, r, head_cols(p, 2)] = dv.astype(bf)
            k.qkv[b, r, head_cols(p, 0)] = (dq * HS**-0.5).astype(bf).T

    def bwd_first(b, some):
        for i in some:
            r = rows(i)
            d = dot(k.qkv[b, r, :], m_qkv(b), NT)
            hat, rs = norm_hat(state(b, i))
            dm_row(b, i, 0, jnp.sum(d, axis=0, keepdims=True))
            dm_row(b, i, 1, jnp.sum(d * hat, axis=0, keepdims=True))
            k.xs[B, r, :] = k.xs[B, r, :] + norm_back(d * (1.0 + piece(b, i, 1)), hat, rs)

    def run(*todo):
        for fn, *args in todo:
            fn(*args)

    def each(fn, b):
        for i in images:
            fn(b, i)

    def keep(name):
        return local(("keep", name), getattr(k, name), getattr(out, name))

    def fetch(name):
        return local(("fetch", name), getattr(out, name), getattr(k, name))

    def keep_start(name):
        keep(name).start()

    def keep_wait(name):
        keep(name).wait()

    def fetch_start(name):
        fetch(name).start()

    def fetch_wait(name):
        fetch(name).wait()

    def out_wait():
        local(("os",), k.da, out.output).wait()

    def at_block(b, which, *todo):
        pl.when(b == which)(functools.partial(run, *todo))

    def phase(*todo):
        pl.when(me >= 0)(functools.partial(run, *todo))

    barrier = pltpu.get_barrier_semaphore()
    everyone = [at_z(r) for r in range(1, F)] + [at_q(j) for j in range(1, 4)] + [at_c(j) for j in range(4)]
    for peer in everyone:
        pl.semaphore_signal(barrier, inc=1, device_id=peer, device_id_type=MESH)
    load("c")
    load("q")
    load("a")
    load("u")
    load("d")
    load("t")
    loaded("c")
    cond_tile()
    loaded("q")
    pl.semaphore_wait(barrier, len(everyone))

    run((cond_z,), (w_z, 0, "u"), (w_z, 0, "q"), (wait, "recv", ("cz",), k.cz.at[pl.ds(0, F - 1)]), (w_z, 1, "q"), (cond_zq,), (w_relay, 0, "u"), (w_z, 0, "d"), (w_zq, 0, "q"), (w_relay, 0, "q"), (mod_partial, 0), (w_relay, 1, "q"), (w_opposite, 0, "u"), (w_z, 1, "u"), (mod_partial, 1), (w_qc, 0, "q"), (w_zq, 0, "d"), (w_z, 1, "d"), (mod_ready, 0))
    tokens_ready()

    def forward(step, _):
        b = step
        phase((each, fwd_norm, b),)
        at_block(b, 0, (w_opposite, 1, "q"), (w_ready, 0, "q"))
        phase((each, fwd_qkv, b),)
        at_block(b, 0, (cond_qc,), (w_qc, 0, "u"))
        at_block(b, 1, (w_qc, 1, "u"),)
        at_block(b, 1, (keep_wait, "pt"),)
        phase((each, fwd_probs, b), (each, fwd_mix, b))
        at_block(b, 0, (keep_start, "pt"))
        at_block(b, 0, (w_zq, 1, "u"), (cond_ready,), (w_ready, 0, "u"), (mod_ready, 1))
        phase((each, fwd_proj, b),)
        at_block(b, 0, (w_qc, 0, "d"),)
        at_block(b, 1, (w_ready, 1, "u"), (w_qc, 1, "d"))
        at_block(b, 1, (keep_wait, "hid"), (keep_wait, "act"))
        phase((fwd_up, b),)
        at_block(b, 0, (keep_start, "hid"), (keep_start, "act"))
        at_block(b, 0, (w_qc, 1, "q"), (w_ready, 0, "d"), (w_zq, 1, "d"), (w_relay, 1, "d"))
        at_block(b, 1, (w_ready, 1, "d"),)
        phase((fwd_down, b),)
        at_block(b, 0, (w_ready, 1, "q"),)
        return 0

    lax.fori_loop(0, B, forward, 0)
    phase((turn,),)
    out_load = local(("os",), k.da, out.output)
    out_load.start()

    def backward(step, _):
        b = B - 1 - step
        at_block(b, 0, (fetch_wait, "hid"))
        phase((bwd_hidden, b),)
        phase((grad_up, b),)
        at_block(b, 1, (g_c, 1, "u"),)
        at_block(b, 0, (g_c, 0, "u"), (g_2, 1, "d"), (g_3, 1, "u"), (g_2, 1, "q0"))
        at_block(b, 0, (fetch_wait, "act"))
        phase((grad_down, b),)
        at_block(b, 1, (g_c, 1, "d"), (g_1, 1, "u"))
        at_block(b, 0, (g_c, 0, "d"), (g_1, 0, "u"), (dm_qc, 1))
        at_block(b, B - 1, (out_wait,))
        phase((bwd_second, b),)
        at_block(b, 1, (fetch_start, "hid"))
        at_block(b, 1, (g_1, 1, "d"), (dm_start, 1))
        at_block(b, 0, (g_2, 1, "q1"), (g_1, 0, "d"), (dm_start, 0), (dm_ready, 1))
        phase((grad_proj, b),)
        at_block(b, 0, (fetch_wait, "pt"))
        phase((bwd_heads, b, 0),)
        at_block(b, 0, (g_3, 1, "d"), (g_2, 1, "q2"), (g_3, 1, "q0"))
        phase((grad_qkv, b, 0),)
        at_block(b, 1, (g_c, 1, "q0"),)
        at_block(b, 0, (g_c, 0, "q0"),)
        phase((bwd_heads, b, 1),)
        at_block(b, 1, (g_1, 1, "q0"),)
        at_block(b, 0, (g_ring, 0, "u"), (g_1, 0, "q0"))
        phase((grad_qkv, b, 1),)
        at_block(b, 1, (g_c, 1, "q1"), (dm_zq, 1))
        at_block(b, 0, (g_c, 0, "q1"), (g_fly, 0, "d"), (g_3, 1, "q1"))
        phase((bwd_heads, b, 2),)
        at_block(b, 1, (fetch_start, "pt"), (fetch_start, "act"))
        at_block(b, 1, (g_1, 1, "q1"), (g_2, 1, "u"))
        at_block(b, 0, (g_4, 1, "d"), (g_1, 0, "q1"), (g_4, 1, "q0"), (dm_zq, 0))
        phase((grad_qkv, b, 2),)
        at_block(b, 1, (g_c, 1, "q2"),)
        at_block(b, 0, (g_c, 0, "q2"),)
        phase((bwd_first, b, images[: I // 2]),)
        at_block(b, 0, (g_fly, 0, "q0"), (g_5, 1, "d"), (g_5, 1, "q0"))
        phase((bwd_first, b, images[I // 2 :]),)
        at_block(b, 1, (g_1, 1, "q2"),)
        return 0

    lax.fori_loop(0, B, backward, 0)
    run((dm_start, 2),)
    g_load = local(("g",), k.xs.at[B], out.grad_tokens)
    g_load.start()
    run((g_1, 0, "q2"), (g_4, 1, "q1"), (g_2, 0, "d"), (grad_ada, 1), (g_4, 1, "u"), (g_3, 1, "q2"), (g_5, 1, "q1"), (g_2, 0, "q1"), (g_5, 1, "u"), (g_2, 0, "u"), (dm_qc, 0), (g_2, 0, "q0"), (dm_zq, 2), (dcond_send,), (dm_ready, 0), (grad_ada, 0), (g_2, 0, "q2"), (g_4, 1, "q2"), (g_3, 0, "d"), (g_5, 1, "q2"), (g_3, 0, "u"), (g_3, 0, "q1"), (g_3, 0, "q0"), (dm_qc, 2), (dcond_finish,), (g_3, 0, "q2"), (dm_ready, 2), (grad_ada, 2), (g_4, 0, "d"), (g_4, 0, "u"), (g_5, 0, "d"), (g_4, 0, "q1"), (g_4, 0, "q0"), (g_5, 0, "u"), (g_5, 0, "q1"), (all_sent,), (g_5, 0, "q2"), (g_5, 0, "q0"), (all_sent,))
    g_load.wait()
    local(("grad_cond",), k.gc.at[pl.ds(0, I)], out.grad_cond).wait()
    for b in range(B):
        for m in range(6):
            ada_copy(b, m).wait()
        for w in KINDS:
            out_copy(b, w).wait()
    assert len(index) <= N_SEMS and len(local_index) <= N_LOCAL


def finish(*refs):
    n = len(OUTPUTS)
    src, dst, high, sems = refs[:n], refs[n : 2 * n + 1], refs[2 * n + 1 : -1], refs[-1]
    B, pairs, _, R, four = src[4].shape
    W = four // 4
    D = W * pairs
    copies = []

    def copy(a, b):
        copies.append(pltpu.make_async_copy(a, b, sems.at[len(copies)]))
        copies[-1].start()

    for m in range(4):
        copy(src[m], dst[m])
    qkv, proj, up, down = high
    for b in range(B):
        for p in range(pairs):
            x = src[4][b, p].reshape(2 * R, 4 * W).astype(f32)
            for j in range(3):
                qkv[b, :, j * D + p * W : j * D + (p + 1) * W] = x[:, j * W : (j + 1) * W]
            proj[b, :, p * W : (p + 1) * W] = x[:, 3 * W :]
    copy(qkv, dst[4])
    copy(proj, dst[5])
    up[...] = src[5][...].reshape(up.shape).astype(f32)
    copy(up, dst[6])
    down[...] = src[6][...].reshape(down.shape).astype(f32)
    copy(down, dst[7])
    for c in copies:
        c.wait()


def body(F, tokens, cond, cotangent, keep_mask, w_ada, w_qkv, w_proj, w_up, w_down):
    I, L, D = tokens.shape
    B, _, FF = w_up.shape
    R = D // F // 2
    W = D // PAIRS
    T = I * L
    shapes = scratch(F, I, L, D, FF, B)
    names = tuple(shapes)
    anywhere = pl.BlockSpec(memory_space=pl.ANY)
    results = [
        jax.ShapeDtypeStruct((T, D), bf),
        jax.ShapeDtypeStruct((T, D), f32),
        jax.ShapeDtypeStruct((I, D), f32),
        jax.ShapeDtypeStruct((B, D // F, 6 * D), f32),
        jax.ShapeDtypeStruct((B, PAIRS, 2, R, 4 * W), bf),
        jax.ShapeDtypeStruct((B, 2, R, FF), bf),
        jax.ShapeDtypeStruct((B, 4, 2, R, D), bf),
    ]
    found = pl.pallas_call(
        functools.partial(kernel, names, F, I, L, D, FF, B),
        name="blocks",
        out_shape=[pltpu.VMEM(r.shape, r.dtype) for r in results] + [jax.ShapeDtypeStruct(*shapes[n]) for n in KEPT],
        in_specs=[pl.BlockSpec(memory_space=pltpu.SMEM) if n == "mask" else anywhere for n in INPUTS],
        out_specs=[anywhere] * len(OUTPUTS) + [pl.BlockSpec(memory_space=pltpu.HBM)] * len(KEPT),
        scratch_shapes=[pltpu.VMEM(*shapes[n]) for n in names]
        + [pltpu.SemaphoreType.DMA((N_SEMS,)), pltpu.SemaphoreType.DMA((N_LOCAL,))],
        compiler_params=pltpu.CompilerParams(
            collective_id=0, has_side_effects=True, vmem_limit_bytes=56 * 2**20 + 2**19
        ),
    )(
        tokens.reshape(T, D),
        cond,
        cotangent.reshape(T, D),
        keep_mask,
        w_ada,
        w_qkv.reshape(B, 2, R, 3 * D),
        w_proj.reshape(B, 2, R, D),
        w_up.reshape(B, 2, R, FF),
        w_down.reshape(B, 4, 2, R, D),
    )
    grads = [(B, 2 * R, 3 * D), (B, 2 * R, D), (B, 2 * R, FF), (B, 8 * R, D)]
    output, grad_tokens, grad_cond, *weights = pl.pallas_call(
        finish,
        name="finish",
        out_shape=results[:4] + [jax.ShapeDtypeStruct(s, f32) for s in grads],
        in_specs=[pl.BlockSpec(memory_space=pltpu.VMEM)] * len(OUTPUTS),
        out_specs=[anywhere] * 8,
        scratch_shapes=[pltpu.VMEM(s, f32) for s in grads] + [pltpu.SemaphoreType.DMA((8,))],
        compiler_params=pltpu.CompilerParams(vmem_limit_bytes=40 * 2**20),
    )(*found[: len(OUTPUTS)])
    if lax.axis_size("dp") > GROUP:
        first = lax.axis_index("dp") % GROUP == 0
        weights = lax.psum(tuple(jnp.where(first, w, 0.0) for w in weights), "dp")
    return (output.reshape(I, L, D), grad_tokens.reshape(I, L, D), grad_cond, *weights)


def solution(mesh):
    slots = P(("dp", "fsdp"), None, None)
    weight = P(None, "fsdp", None)
    return jax.shard_map(
        functools.partial(body, mesh.shape["fsdp"]),
        mesh=mesh,
        in_specs=(slots, P(("dp", "fsdp"), None), slots, P(("dp", "fsdp"))) + (weight,) * 5,
        out_specs=(slots, slots, P(("dp", "fsdp"), None)) + (weight,) * 5,
        check_vma=False,
    )
```

```python
import functools

import jax
import jax.numpy as jnp
from jax import lax
from jax.experimental import pallas as pl
from jax.experimental.pallas import tpu as pltpu
from jax.sharding import PartitionSpec as P

MESH = pl.DeviceIdType.MESH
bf, f32 = jnp.bfloat16, jnp.float32
HEADS = 6
PAIRS = HEADS // 2
GROUP = 8
NN = (((1,), (0,)), ((), ()))
NT = (((1,), (1,)), ((), ()))
TN = (((0,), (0,)), ((), ()))
GELU_A = 0.7978845608028654
GELU_B = GELU_A * 0.044715
KINDS = ("u", "d", "q0", "q1", "q2")
SPLIT = ((0, "q"), (1, "d"))
DIRECT = ((0, "d"), (0, "q"), (1, "d"), (1, "u"))
STEPS = ()
ONE = ((0, "q2"),)
METHOD = (
    {"u": "ring", "d": "steps", "q0": "steps", "q1": "q", "q2": "q"},
    {"u": "q", "d": "q", "q0": "q", "q1": "q", "q2": "q"},
)


def dot(a, b, dims=NN):
    return lax.dot_general(a, b, dims, preferred_element_type=f32)


def exact_dot(a, b, dims=NN):
    return lax.dot_general(a, b, dims, precision=lax.Precision.HIGHEST, preferred_element_type=f32)


def one_hot(shape, hit):
    r = lax.broadcasted_iota(jnp.int32, shape, 0)
    c = lax.broadcasted_iota(jnp.int32, shape, 1)
    return jnp.where(hit(r, c), 1.0, 0.0)


def norm_hat(v):
    c = v - jnp.mean(v, -1, keepdims=True)
    r = lax.rsqrt(jnp.mean(c * c, -1, keepdims=True) + 1e-6)
    return c * r, r


def norm_back(dx, hat, r):
    return r * (dx - jnp.mean(dx, -1, keepdims=True) - hat * jnp.mean(dx * hat, -1, keepdims=True))


def gelu_parts(x):
    x2 = x * x
    t = jnp.tanh(x * (GELU_A + GELU_B * x2))
    up = 0.5 * t + 0.5
    a = x * up
    return a, a * (1.0 - t) * (GELU_A + (3 * GELU_B) * x2) + up


class Refs:
    pass


def scratch(F, I, L, D, FF, B):
    T = I * L
    R = D // F // 2
    W = D // PAIRS
    shapes = dict(
        wq=((B, F, 2, R, FF), bf),
        wu=((B, F, 2, R, FF), bf),
        wd=((B, F, 4, 2, R, D), bf),
        wa=((B, D // F, 6 * D), bf),
        xs=((B + 1, T, D), f32),
        fi=((B, T, D), bf),
        qkv=((B, T, 3 * D), bf),
        pt=((I * HEADS, L, L), bf),
        mt=((B, D, T), bf),
        att=((B, T, D), bf),
        mid=((B, T, D), f32),
        r1=((B, T, 1), f32),
        r2=((B, T, 1), f32),
        si=((B, T, D), bf),
        hid=((T, FF), bf),
        br=((B, T, D), bf),
        db=((T, D), bf),
        act=((T, FF), bf),
        da=((T, D), bf),
        mod=((B * 3, 2 * I, D), f32),
        dm=((B, 4 * I, D), f32),
        dl=((B, 2 * I, D), f32),
        cd=((I, D), bf),
        gc=((8, D), f32),
        ms=((F, B * 6 * I, D), bf),
        mr=((F, B * 6 * I, D), bf),
        cz=((F, 16, D), bf),
        cg=((4, 2, 16, D), bf),
        dg=((B + 1, 4, 2, F, 16, D), bf),
        cs=((F, 8, D), f32),
        cr=((F, 8, D), f32),
        gq=((PAIRS, F, 2, R, 4 * W), bf),
        gu=((F, 2, R, FF), bf),
        gd=((F, 4, 2, R, D), bf),
        hq=((B, PAIRS, F, R, 4 * W), bf),
        hu=((B, F, R, FF), bf),
        hd=((B, F, 4, R, D), bf),
        oq=((B, PAIRS, 2, R, 4 * W), bf),
        ou=((B, 2, R, FF), bf),
        od=((B, 4, 2, R, D), bf),
    )
    for block in range(B):
        for w in KINDS:
            n = W if w[0] == "q" else D
            four = (4, R, n) if w == "d" else (R, 4 * n)
            at = f"{w}{block}"
            if METHOD[block][w] == "direct":
                shapes["a" + at] = ((4 * F, R, n), bf)
            elif METHOD[block][w] == "ring":
                shapes["t" + at] = (four, bf)
                shapes["a" + at] = ((2, *four), bf)
                shapes["s" + at] = (four, bf)
                shapes["b" + at] = ((3, R, n), bf)
            else:
                if METHOD[block][w] == "steps":
                    shapes["t" + at] = ((2, F, R, n), bf)
                    shapes["a" + at] = ((F, R, n), bf)
                else:
                    shapes["a" + at] = ((3, F, R, n), bf)
                shapes["s" + at] = ((F, R, n), bf)
                shapes["b" + at] = ((F, R, n), bf)
    return shapes


INPUTS = ("tokens", "cond", "cotangent", "mask", "ada", "qkv_w", "proj_w", "up_w", "down_w")
OUTPUTS = ("output", "grad_tokens", "grad_cond", "grad_ada", "grad_q", "grad_u", "grad_d")
KEPT = ("pt", "hid", "act")
N_SEMS = 256
N_LOCAL = 64


def kernel(names, F, I, L, D, FF, B, *refs):
    n_in, n_out = len(INPUTS), len(OUTPUTS) + len(KEPT)
    inp, out, k = Refs(), Refs(), Refs()
    for name, ref in zip(INPUTS, refs[:n_in]):
        setattr(inp, name, ref)
    for name, ref in zip(OUTPUTS + KEPT, refs[n_in : n_in + n_out]):
        setattr(out, name, ref)
    for name, ref in zip(names, refs[n_in + n_out :]):
        setattr(k, name, ref)
    sems, local_sems = refs[-2], refs[-1]
    T = I * L
    R = D // F // 2
    W = D // PAIRS
    HS = D // HEADS
    images = range(I)

    me, f = lax.axis_index("dp"), lax.axis_index("fsdp")
    e = me % GROUP
    base = me - e
    c, q = e % 2, e // 2
    other = 1 - c
    z_peer = [(f + r) % F for r in range(F)]
    q_peer = [(q + j) % 4 for j in range(4)]

    def at_z(r):
        return (me, z_peer[r])

    x_next, y_next = q + 1 - 2 * (q % 2), (q + 2) % 4
    first = x_next * other + y_next * c
    second = x_next * c + y_next * other
    across = 6 - q - first - second

    def at(qi):
        return (base + 2 * qi + c, f)

    def at_q(j, r=0):
        return (base + 2 * q_peer[j] + c, z_peer[r])

    def at_c(j=0):
        return (base + 2 * q_peer[j] + other, f)

    def rows(i):
        return slice(i * L, (i + 1) * L)

    def cut(j, n):
        return pl.ds(pl.multiple_of(j * n, n), n)

    index = {}

    def sem(key):
        return sems.at[index.setdefault(key, len(index))]

    def send(key, src, dst, to):
        pltpu.make_async_remote_copy(
            src_ref=src,
            dst_ref=dst,
            send_sem=sem(("send",) + key),
            recv_sem=sem(("recv",) + key),
            device_id=to,
            device_id_type=MESH,
        ).start()

    unsent = []

    def wait(kind, key, like):
        if kind == "recv" and key[0] != "gc":
            unsent.append((key, like))
        done(kind, key, like)

    def done(kind, key, like):
        ref = like() if callable(like) else like
        pltpu.make_async_copy(ref, ref, sem((kind,) + key)).wait()

    def all_sent():
        while unsent:
            done("send", *unsent.pop(0))

    local_index = {}

    def local(key, src, dst):
        n = local_index.setdefault(key, len(local_index))
        return pltpu.make_async_copy(src, dst, local_sems.at[n])

    def loads(what):
        if what == "c":
            return [local(("cd",), inp.cond, k.cd)]
        if what == "a":
            return [local(("wa",), inp.ada, k.wa)]
        if what == "u":
            return [local(("wu",), inp.up_w, k.wu.at[:, f])]
        if what == "d":
            return [local(("wd",), inp.down_w, k.wd.at[:, f])]
        if what == "t":
            return [local(("tk",), inp.tokens, k.da), local(("db",), inp.cotangent, k.db)]
        return [
            local(
                ("wq", n, p),
                inp.qkv_w.at[:, :, :, pl.ds(n * D + p * W, W)],
                k.wq.at[:, f, :, :, pl.ds(p * D + n * W, W)],
            )
            for n in range(3)
            for p in range(PAIRS)
        ] + [local(("wp",), inp.proj_w, k.wq.at[:, f, :, :, pl.ds(3 * D, D)])]

    def load(what):
        for copy in loads(what):
            copy.start()

    arrived = set()

    def loaded(what):
        if what not in arrived:
            arrived.add(what)
            for copy in loads(what):
                copy.wait()

    def tokens_ready():
        loaded("t")
        for i in images:
            k.xs[0, rows(i), :] = k.da[rows(i), :].astype(f32)

    whole = {"q": k.wq, "u": k.wu, "d": k.wd}

    def main(b, w):
        return pl.ds(0, R * 2 // 3 if (b, w) in SPLIT else R)

    rest = pl.ds(R * 2 // 3, R // 3)

    def w_main(b, w, fz, qi=q):
        some = main(b, w)
        return k.wd.at[b, fz, qi, c, some] if w == "d" else whole[w].at[b, fz, c, some, cut(qi, D)]

    def w_rest(b, w, fz):
        return k.wd.at[b, fz, :, c, rest] if w == "d" else whole[w].at[b, fz, c, rest]

    def w_half(b, w, fz):
        return k.wd.at[b, fz, :, c] if w == "d" else whole[w].at[b, fz, c]

    def like_main(b, w, n, m=1):
        some = main(b, w)
        return k.wd.at[b, pl.ds(0, n), pl.ds(0, m), 0, some] if w == "d" else whole[w].at[b, pl.ds(0, n), 0, some, pl.ds(0, m * D)]

    def like_rest(b, w, n):
        return k.wd.at[b, pl.ds(0, n), :, 0, rest] if w == "d" else whole[w].at[b, pl.ds(0, n), 0, rest]

    def w_z(b, w):
        loaded(w)
        for r in (1, 3, 2) if (b, w) in DIRECT else (1, 3):
            p = w_main(b, w, f)
            send(("wz", b, w), p, p, at_z(r))
        if (b, w) in SPLIT:
            for r in (1, 3):
                p = w_rest(b, w, f)
                send(("wr", b, w), p, p, at_z(r))

    def w_to_q(b, w, some):
        for r in some:
            for j in range(1, 4):
                p = w_main(b, w, z_peer[r])
                send(("wq", b, w), p, p, at_q(j))

    def w_zq(b, w):
        if (b, w) in DIRECT:
            wait("recv", ("wz", b, w), lambda: like_main(b, w, 3))
        else:
            wait("recv", ("wm", b, w), lambda: like_main(b, w, 1))
        if (b, w) in STEPS:
            for r in (1, 3, 2):
                p = w_main(b, w, z_peer[r])
                send(("w1", b, w), p, p, at(first))
        else:
            w_to_q(b, w, (1, 3, 2))

    def w_q2(b, w):
        wait("recv", ("w1", b, w), lambda: like_main(b, w, 3))
        for qi in (q, first):
            for r in (1, 3, 2):
                p = w_main(b, w, z_peer[r], qi)
                send(("wq", b, w), p, p, at(second))

    def w_relay(b, w):
        if (b, w) not in DIRECT:
            wait("recv", ("wz", b, w), lambda: like_main(b, w, 2))
            p = w_main(b, w, z_peer[3])
            send(("wm", b, w), p, p, at_z(1))
        if (b, w) in SPLIT:
            wait("recv", ("wr", b, w), lambda: like_rest(b, w, 2))
            p = w_rest(b, w, z_peer[3])
            send(("wo", b, w), p, p, at_z(1))
        if (b, w) not in DIRECT and (b, w) not in STEPS:
            w_to_q(b, w, (1, 3))

    def w_opposite(b, w):
        wait("recv", ("wm", b, w), lambda: like_main(b, w, 1))
        w_to_q(b, w, (2,))

    def w_qc(b, w):
        if (b, w) in SPLIT:
            wait("recv", ("wo", b, w), lambda: like_rest(b, w, 1))
        wait("recv", ("wq", b, w), lambda: like_main(b, w, 3, 2 if (b, w) in STEPS else 3))
        for r in range(1, F):
            p = w_half(b, w, z_peer[r])
            send(("wc", b, w), p, p, at_c())

    def w_ready(b, w):
        wait("recv", ("wc", b, w), lambda: k.wd.at[b, pl.ds(0, F - 1), :, 0] if w == "d" else whole[w].at[b, pl.ds(0, F - 1), 0])

    def cols():
        return one_hot((D, D // F), lambda r, s: r == f * (D // F) + s)

    def cond_tile():
        v = k.cd[...].astype(f32)
        a = v / (1.0 + jnp.exp(-v))
        k.cz[f] = jnp.concatenate([a] * 4, axis=0).astype(bf)

    def cond_z():
        for r in range(1, F):
            send(("cz",), k.cz.at[f], k.cz.at[f], at_z(r))

    def cond_zq():
        pick = one_hot((16, F * 16), lambda r, s: (r // 4 == s // 16) & (r % 4 == s % 16)).astype(bf)
        k.cg[q, c] = dot(pick, k.cz[...].reshape(F * 16, D)).astype(bf)
        for j in range(1, 4):
            send(("cq",), k.cg.at[q, c], k.cg.at[q, c], at_q(j))

    def cond_qc():
        wait("recv", ("cq",), lambda: k.cg.at[pl.ds(0, 3), 0])
        send(("cc",), k.cg.at[:, c], k.cg.at[:, c], at_c())

    def cond_ready():
        wait("recv", ("cc",), lambda: k.cg.at[:, 0])

    def tile_mask(n, p):
        r = lax.broadcasted_iota(jnp.int32, (n, 1), 0)
        return jnp.where((r // 4) % 4 == p, 1.0, 0.0)

    tiles = ((0, 1), (1, 3))

    def mod_partial(part):
        loaded("a")
        a = dot(k.cz[...].reshape(F * 16, D), cols().astype(bf))
        masked = [(a * tile_mask(F * 16, p)).astype(bf) for p in range(4)]
        lo, hi = tiles[part]
        for t in range(lo, hi):
            total = None
            for p in range(4):
                b, m = divmod(4 * t + p, 6)
                o = dot(masked[p], k.wa[b, :, m * D : (m + 1) * D])
                total = o if total is None else total + o
            k.ms[:, 16 * t : 16 * t + 16, :] = total.astype(bf).reshape(F, 16, D)
        some = pl.ds(16 * lo, 16 * (hi - lo))
        for r in range(1, F):
            send(("mz", part), k.ms.at[z_peer[r], some], k.mr.at[f, some], at_z(r))

    def mod_ready(part):
        lo, hi = tiles[part]
        some = slice(16 * lo, 16 * hi)
        wait("recv", ("mz", part), lambda: k.mr.at[pl.ds(0, F - 1), pl.ds(16 * lo, 16 * (hi - lo))])
        total = k.ms[f, some].astype(f32)
        for r in range(1, F):
            total = total + k.mr[z_peer[r], some].astype(f32)
        k.mod[2 * lo : 2 * hi] = total.reshape(2 * (hi - lo), 2 * I, D)

    def piece(b, i, p):
        at = p % 2 * I + i
        return k.mod[3 * b + p // 2, at : at + 1, :]

    def dm_row(b, i, p, v):
        to, at = (k.dm, (p - 2) * I + i) if p >= 2 else (k.dl, p * I + i)
        to[b, at : at + 1, :] = v

    def dm_pieces(t):
        return [(t, p + 2) for p in range(4)] if t < B else [(p // 2, p % 2) for p in range(4)]

    def dm_start(t):
        k.dg[t, q, c, f] = (k.dm[t] if t < B else k.dl[...].reshape(4 * I, D)).astype(bf)
        for r in range(1, F):
            p = k.dg.at[t, q, c, f]
            send(("dz", t), p, p, at_z(r))

    def dm_zq(t):
        wait("recv", ("dz", t), lambda: k.dg.at[t, 0, 0, pl.ds(0, F - 1)])
        for j in range(1, 4):
            p = k.dg.at[t, q, c]
            send(("dq", t), p, p, at_q(j))

    def dm_qc(t):
        wait("recv", ("dq", t), lambda: k.dg.at[t, pl.ds(0, 3), 0])
        p = k.dg.at[t, :, c]
        send(("dc", t), p, p, at_c())

    def dm_ready(t):
        wait("recv", ("dc", t), lambda: k.dg.at[t, :, 0])

    def dcond_part(t):
        tile = k.dg[t, q, c].reshape(F * 16, D).astype(f32)
        acc = None
        for p, (b, m) in enumerate(dm_pieces(t)):
            o = dot((tile * tile_mask(F * 16, p)).astype(bf), k.wa[b, :, m * D : (m + 1) * D], NT)
            acc = o if acc is None else acc + o
        return acc

    def dcond_send():
        acc = dcond_part(0) + dcond_part(1) + dcond_part(2)
        fold = one_hot((F * 8, F * 16), lambda r, s: (r // 8 == s // 16) & (r % 8 == s % 4))
        t = exact_dot(exact_dot(fold, acc), cols(), NT)
        k.cs[...] = t.reshape(F, 8, D)
        for r in range(1, F):
            send(("gz",), k.cs.at[z_peer[r]], k.cr.at[f], at_z(r))

    def dcond_finish():
        wait("recv", ("gz",), lambda: k.cr.at[pl.ds(0, F - 1)])
        total = k.cs[f]
        for r in range(1, F):
            total = total + k.cr[z_peer[r]]
        v = k.cd[...].astype(f32)
        s = 1.0 / (1.0 + jnp.exp(-v))
        k.gc[:I] = total[:I] * (s * (1.0 + v * (1.0 - s)))
        local(("grad_cond",), k.gc.at[pl.ds(0, I)], out.grad_cond).start()

    def ada_copy(b, m):
        stage = (k.xs.at[1], k.mid.at[1])[b]
        return local(("ada", b, m), stage.at[pl.ds(m * (D // F), D // F)], out.grad_ada.at[b, :, pl.ds(m * D, D)])

    def grad_ada(t):
        n = GROUP * F * 16
        a = dot(k.cg[...].reshape(n // 4, D), cols().astype(bf)).astype(bf)
        spread = one_hot((n, n // 4), lambda r, s: (r // 16 == s // 4) & (r % 4 == s % 4)).astype(bf)
        a = dot(spread, a)
        tile = k.dg[t].reshape(n, D)
        for p, (b, m) in enumerate(dm_pieces(t)):
            stage = (k.xs.at[1], k.mid.at[1])[b]
            stage[m * (D // F) : (m + 1) * (D // F), :] = dot((a * tile_mask(n, p)).astype(bf), tile, TN)
            ada_copy(b, m).start()

    def width(w):
        return W if w[0] == "q" else D

    def g_local(w):
        return k.gq.at[int(w[1])] if w[0] == "q" else {"u": k.gu, "d": k.gd}[w]

    def g_halves(b, w):
        return k.hq.at[b, int(w[1])] if w[0] == "q" else {"u": k.hu, "d": k.hd}[w].at[b]

    def g_result(b, w):
        return k.oq.at[b, int(w[1])] if w[0] == "q" else {"u": k.ou, "d": k.od}[w].at[b]

    def g_buf(b, w, kind):
        return getattr(k, f"{kind}{w}{b}")

    def quarter(w, h, qi):
        return h.at[:, qi] if w == "d" else h.at[:, :, cut(qi, width(w))]

    def one_of(w, ref, j):
        return ref.at[q_peer[j]] if w == "d" else ref.at[:, cut(q_peer[j], width(w))]

    def r_piece(b, w):
        return k.od.at[b, q, c] if w == "d" else g_result(b, w).at[c, :, cut(q, width(w))]

    def r_half(b, w):
        return k.od.at[b, :, c] if w == "d" else g_result(b, w).at[c]

    def g_c(b, w):
        half = k.gd.at[:, :, other] if w == "d" else g_local(w).at[:, other]
        send(("gc", b, w), half, g_halves(b, w), at_c())

    def g_1(b, w):
        h = g_halves(b, w)
        for kind in ("send", "recv"):
            wait(kind, ("gc", b, w), lambda: g_halves(b, w))
        for n in range(F):
            own = k.gd[n, :, c] if w == "d" else g_local(w)[n, c]
            h[n] = h[n] + own
        how = METHOD[b][w]
        if how == "direct":
            for r, j in [(r, j) for r in range(F) for j in range(4)][1:]:
                send(("g1", b, w), h.at[z_peer[r], :, cut(q_peer[j], W)], g_buf(b, w, "a").at[r * 4 + j], at_q(j, r))
        elif how == "steps":
            for n, qi in enumerate((first, across)):
                send(("gt", b, w), quarter(w, h, qi), g_buf(b, w, "t").at[n], at(first))
        elif how == "ring":
            send(("gt", b, w), h.at[z_peer[2]], g_buf(b, w, "t"), at_z(1))
        else:
            for j in range(1, 4):
                send(("g1", b, w), quarter(w, h, q_peer[j]), g_buf(b, w, "a").at[j - 1], at_q(j))

    def g_fly(b, w):
        h, t = g_halves(b, w), g_buf(b, w, "t")
        wait("recv", ("gt", b, w), lambda: t)
        for n, qi in enumerate((q, second)):
            p = quarter(w, h, qi)
            p[...] = p[...] + t[n]
        send(("g1", b, w), quarter(w, h, second), g_buf(b, w, "a"), at(second))

    def g_ring(b, w):
        h, t = g_halves(b, w), g_buf(b, w, "t")
        wait("recv", ("gt", b, w), lambda: t)
        h[z_peer[1]] = h[z_peer[1]] + t[...]
        for n, r in enumerate((1, 3)):
            send(("g1", b, w), h.at[z_peer[r]], g_buf(b, w, "a").at[n], at_z(r))

    def g_direct(b, w):
        h, a = g_halves(b, w), g_buf(b, w, "a")
        wait("recv", ("g1", b, w), lambda: a.at[pl.ds(0, 4 * F - 1)])
        total = h[f, :, cut(q, W)].astype(f32)
        for n in range(1, 4 * F):
            total = total + a[n].astype(f32)
        hand_back(b, w, total)

    def hand_back(b, w, total):
        p = r_piece(b, w)
        p[...] = total.astype(bf)
        for j in range(1, 4):
            send(("g3", b, w), p, p, at_q(j))
        if (b, w) in ONE:
            for j in range(4):
                send(("g3", b, w), p, p, at_c(j))

    def g_2(b, w):
        h, a, s = g_halves(b, w), g_buf(b, w, "a"), g_buf(b, w, "s")
        wait("recv", ("g1", b, w), lambda: a)
        if METHOD[b][w] == "ring":
            total = h[f].astype(f32) + a[0].astype(f32) + a[1].astype(f32)
            s[...] = total.astype(bf)
            for j in range(1, 4):
                send(("g2", b, w), one_of(w, s, j), g_buf(b, w, "b").at[j - 1], at_q(j))
        else:
            if METHOD[b][w] == "steps":
                s[...] = quarter(w, h, q)[...] + a[...]
            else:
                total = quarter(w, h, q)[...].astype(f32)
                for j in range(3):
                    total = total + a[j].astype(f32)
                s[...] = total.astype(bf)
            for r in range(1, F):
                send(("g2", b, w), s.at[z_peer[r]], g_buf(b, w, "b").at[f], at_z(r))

    def g_3(b, w):
        s, a = g_buf(b, w, "s"), g_buf(b, w, "b")
        if METHOD[b][w] == "ring":
            wait("recv", ("g2", b, w), lambda: a)
            total = one_of(w, s, 0)[...].astype(f32)
            for j in range(3):
                total = total + a[j].astype(f32)
        else:
            wait("recv", ("g2", b, w), lambda: a.at[pl.ds(0, F - 1)])
            total = s[f].astype(f32)
            for r in range(1, F):
                total = total + a[z_peer[r]].astype(f32)
        hand_back(b, w, total)

    def g_4(b, w):
        wait("recv", ("g3", b, w), lambda: k.od.at[b, pl.ds(0, 3), 0] if w == "d" else g_result(b, w).at[0, :, pl.ds(0, 3 * width(w))])
        send(("g4", b, w), r_half(b, w), r_half(b, w), at_c())

    def out_copy(b, w):
        to = out.grad_q.at[b, int(w[1])] if w[0] == "q" else {"u": out.grad_u, "d": out.grad_d}[w].at[b]
        return local(("out", b, w), g_result(b, w), to)

    def seven(b, w):
        return k.act.at[pl.ds(0, 7 * R), pl.ds(0, width(w))]

    def g_5(b, w):
        if (b, w) in ONE:
            wait("recv", ("g3", b, w), lambda: seven(b, w))
        else:
            wait("recv", ("g4", b, w), lambda: k.od.at[b, :, 0] if w == "d" else g_result(b, w).at[0])
        out_copy(b, w).start()

    def m_qkv(b):
        return k.wq[b, :, :, :, : 3 * D].reshape(D, 3 * D)

    def m_proj(b):
        return k.wq[b, :, :, :, 3 * D :].reshape(D, D)

    def m_up(b, at, n):
        return k.wu[b, :, :, :, at : at + n].reshape(D, n)

    def m_down(b):
        return k.wd[b].reshape(FF, D)

    def state(b, i):
        return k.xs[b, rows(i), :]

    def lane_masks():
        lane = lax.broadcasted_iota(jnp.int32, (1, 2 * HS), 1)
        lo = jnp.where(lane < HS, 1.0, 0.0)
        return lo.astype(bf), (1.0 - lo).astype(bf)

    def head_cols(p, which):
        return slice(p * D + which * W, p * D + (which + 1) * W)

    def fwd_norm(b, i):
        x = state(b, i)
        hat, k.r1[b, rows(i), :] = norm_hat(x)
        k.xs[b, rows(i), :] = hat
        k.xs[b + 1, rows(i), :] = x
        k.fi[b, rows(i), :] = (hat * (1.0 + piece(b, i, 1)) + piece(b, i, 0)).astype(bf)

    def fwd_qkv(b, i):
        r = rows(i)
        y = dot(k.fi[b, r, :], m_qkv(b))
        for p in range(PAIRS):
            s = head_cols(p, 0)
            k.qkv[b, r, s] = (y[:, s] * HS**-0.5).astype(bf)
            s = slice(p * D + W, (p + 1) * D)
            k.qkv[b, r, s] = y[:, s].astype(bf)

    def fwd_probs(b, i):
        masks = lane_masks()
        for p in range(PAIRS):
            qs = k.qkv[b, rows(i), head_cols(p, 0)]
            ks = k.qkv[b, rows(i), head_cols(p, 1)]
            both = dot(jnp.concatenate([ks * m for m in masks], axis=0), qs, NT)
            for m in range(2):
                scores = both[m * L : (m + 1) * L]
                ex = jnp.exp(scores - jnp.max(scores, axis=0, keepdims=True))
                k.pt[i * HEADS + 2 * p + m] = (ex * (1.0 / jnp.sum(ex, axis=0, keepdims=True))).astype(bf)

    def fwd_mix(b, i):
        mixed = []
        for p in range(PAIRS):
            vt = k.qkv[b, rows(i), head_cols(p, 2)].T
            for m in range(2):
                mixed.append(dot(vt[m * HS : (m + 1) * HS], k.pt[i * HEADS + 2 * p + m]))
        k.mt[b, :, rows(i)] = jnp.concatenate(mixed, axis=0).astype(bf)

    def fwd_proj(b, i):
        r = rows(i)
        att = dot(k.mt[b, :, r], m_proj(b), TN)
        k.att[b, r, :] = att.astype(bf)
        mid = state(b + 1, i) + piece(b, i, 2) * att
        k.xs[b + 1, r, :] = mid
        hat, k.r2[b, r, :] = norm_hat(mid)
        k.mid[b, r, :] = hat
        k.si[b, r, :] = (hat * (1.0 + piece(b, i, 4)) + piece(b, i, 3)).astype(bf)

    def fwd_up(b):
        n = FF // 3
        for j in range(3):
            s = slice(j * n, (j + 1) * n)
            x = dot(k.si[b], m_up(b, j * n, n))
            a, slope = gelu_parts(x)
            k.act[:, s] = a.astype(bf)
            k.hid[:, s] = slope.astype(bf)

    def fwd_down(b):
        acc = dot(k.act[...], m_down(b))
        k.br[b] = acc.astype(bf)
        for i in images:
            r = rows(i)
            k.xs[b + 1, r, :] = k.xs[b + 1, r, :] + piece(b, i, 5) * acc[r]

    def turn():
        for i in images:
            r = rows(i)
            k.da[r, :] = k.xs[B, r, :].astype(bf)
            k.xs[B, r, :] = k.db[r, :].astype(f32) * inp.mask[i].astype(f32)

    def bwd_hidden(b):
        for i in images:
            r = rows(i)
            g = k.xs[B, r, :]
            dm_row(b, i, 5, jnp.sum(g * k.br[b, r, :].astype(f32), axis=0, keepdims=True))
            k.db[r, :] = (g * piece(b, i, 5)).astype(bf)
        n = FF // 2
        for h in range(2):
            r = slice(h * T // 2, (h + 1) * T // 2)
            for j in range(2):
                s = slice(j * n, (j + 1) * n)
                da = dot(k.db[r, :], m_down(b)[s], NT)
                k.hid[r, s] = (k.hid[r, s].astype(f32) * da).astype(bf)

    def bwd_second(b):
        acc = dot(k.hid[...], m_up(b, 0, FF), NT)
        for i in images:
            r = rows(i)
            d = acc[r]
            hat, rs = k.mid[b, r, :], k.r2[b, r, :]
            dm_row(b, i, 3, jnp.sum(d, axis=0, keepdims=True))
            dm_row(b, i, 4, jnp.sum(d * hat, axis=0, keepdims=True))
            d_mid = k.xs[B, r, :] + norm_back(d * (1.0 + piece(b, i, 4)), hat, rs)
            k.xs[B, r, :] = d_mid
            dm_row(b, i, 2, jnp.sum(d_mid * k.att[b, r, :].astype(f32), axis=0, keepdims=True))
            k.da[r, :] = (d_mid * piece(b, i, 2)).astype(bf)

    def grad_down(b):
        n = FF // 2
        for h in range(2):
            x = dot(k.act[:, h * n : (h + 1) * n], k.db[...], TN)
            k.gd[h * F // 2 : (h + 1) * F // 2] = x.astype(bf).reshape(F // 2, 4, 2, R, D)

    def grad_up(b):
        n = FF // 2
        for h in range(2):
            s = slice(h * n, (h + 1) * n)
            k.gu[:, :, :, s] = dot(k.si[b], k.hid[:, s], TN).astype(bf).reshape(F, 2, R, n)

    def grad_proj(b):
        x = dot(k.mt[b], k.da[...]).astype(bf).reshape(F, 2, R, D)
        for p in range(PAIRS):
            k.gq[p, :, :, :, 3 * W :] = x[:, :, :, p * W : (p + 1) * W]

    def grad_qkv(b, p):
        x = dot(k.fi[b], k.qkv[b, :, p * D : (p + 1) * D], TN)
        k.gq[p, :, :, :, : 3 * W] = x.astype(bf).reshape(F, 2, R, 3 * W)

    def bwd_heads(b, p):
        masks = lane_masks()

        def ds_at(i, m):
            return slice(i * L, (i + 1) * L), slice(m * L, (m + 1) * L)

        wp = m_proj(b)[p * W : (p + 1) * W]
        for i in images:
            r = rows(i)
            do = dot(k.da[r, :], wp, NT).astype(bf)
            k.db[r, :W] = do
            vs = k.qkv[b, r, head_cols(p, 2)]
            both = dot(jnp.concatenate([vs * m for m in masks], axis=0), do, NT)
            for m in range(2):
                dp = both[m * L : (m + 1) * L]
                pf = k.pt[i * HEADS + 2 * p + m].astype(f32)
                w = pf * dp
                k.act[ds_at(i, m)] = (w - pf * jnp.sum(w, axis=0, keepdims=True)).astype(bf)
        for i in images:
            r = rows(i)
            do = k.db[r, :W]
            qs = k.qkv[b, r, head_cols(p, 0)]
            ks = k.qkv[b, r, head_cols(p, 1)]
            kt = ks.T
            ds = [k.act[ds_at(i, m)] for m in range(2)]
            pt = [k.pt[i * HEADS + 2 * p + m] for m in range(2)]
            dk = dot(ds[0], qs * masks[0]) + dot(ds[1], qs * masks[1])
            dv = dot(pt[0], do * masks[0]) + dot(pt[1], do * masks[1])
            dq = jnp.concatenate([dot(kt[m * HS : (m + 1) * HS], ds[m]) for m in range(2)], axis=0)
            k.qkv[b, r, head_cols(p, 1)] = dk.astype(bf)
            k.qkv[b, r, head_cols(p, 2)] = dv.astype(bf)
            k.qkv[b, r, head_cols(p, 0)] = (dq * HS**-0.5).astype(bf).T

    def bwd_first(b, some):
        for i in some:
            r = rows(i)
            d = dot(k.qkv[b, r, :], m_qkv(b), NT)
            hat, rs = state(b, i), k.r1[b, r, :]
            dm_row(b, i, 0, jnp.sum(d, axis=0, keepdims=True))
            dm_row(b, i, 1, jnp.sum(d * hat, axis=0, keepdims=True))
            k.xs[B, r, :] = k.xs[B, r, :] + norm_back(d * (1.0 + piece(b, i, 1)), hat, rs)

    def run(*todo):
        for fn, *args in todo:
            fn(*args)

    def each(fn, b):
        for i in images:
            fn(b, i)

    def keep(name):
        return local(("keep", name), getattr(k, name), getattr(out, name))

    def fetch(name):
        return local(("fetch", name), getattr(out, name), getattr(k, name))

    def keep_start(name):
        keep(name).start()

    def keep_wait(name):
        keep(name).wait()

    def fetch_start(name):
        fetch(name).start()

    def fetch_wait(name):
        fetch(name).wait()

    def out_wait():
        local(("os",), k.da, out.output).wait()

    def at_block(b, which, *todo):
        pl.when(b == which)(functools.partial(run, *todo))

    def phase(*todo):
        pl.when(me >= 0)(functools.partial(run, *todo))

    barrier = pltpu.get_barrier_semaphore()
    everyone = [at_z(r) for r in range(1, F)] + [at_q(j) for j in range(1, 4)] + [at_c(j) for j in range(4)]
    for peer in everyone:
        pl.semaphore_signal(barrier, inc=1, device_id=peer, device_id_type=MESH)
    load("c")
    load("q")
    load("a")
    load("u")
    load("d")
    load("t")
    loaded("c")
    cond_tile()
    loaded("q")
    pl.semaphore_wait(barrier, len(everyone))

    run((cond_z,), (w_z, 0, "u"), (w_z, 0, "q"), (wait, "recv", ("cz",), k.cz.at[pl.ds(0, F - 1)]), (w_z, 1, "q"), (cond_zq,), (w_relay, 0, "u"), (w_z, 0, "d"), (w_zq, 0, "q"), (w_relay, 0, "q"), (mod_partial, 0), (w_relay, 1, "q"), (w_opposite, 0, "u"), (w_z, 1, "u"), (mod_partial, 1), (w_qc, 0, "q"), (w_zq, 0, "d"), (w_z, 1, "d"), (mod_ready, 0))
    tokens_ready()

    def forward(step, _):
        b = step
        phase((each, fwd_norm, b),)
        at_block(b, 0, (w_opposite, 1, "q"), (w_ready, 0, "q"))
        phase((each, fwd_qkv, b),)
        at_block(b, 0, (cond_qc,), (w_qc, 0, "u"))
        at_block(b, 1, (w_qc, 1, "u"),)
        at_block(b, 1, (keep_wait, "pt"),)
        phase((each, fwd_probs, b), (each, fwd_mix, b))
        at_block(b, 0, (keep_start, "pt"))
        at_block(b, 0, (w_zq, 1, "u"), (cond_ready,), (w_ready, 0, "u"), (mod_ready, 1))
        phase((each, fwd_proj, b),)
        at_block(b, 0, (w_qc, 0, "d"),)
        at_block(b, 1, (w_ready, 1, "u"), (w_qc, 1, "d"))
        at_block(b, 1, (keep_wait, "hid"), (keep_wait, "act"))
        phase((fwd_up, b),)
        at_block(b, 0, (keep_start, "hid"), (keep_start, "act"))
        at_block(b, 0, (w_qc, 1, "q"), (w_ready, 0, "d"), (w_zq, 1, "d"), (w_relay, 1, "d"))
        at_block(b, 1, (w_ready, 1, "d"),)
        phase((fwd_down, b),)
        at_block(b, 0, (w_ready, 1, "q"),)
        return 0

    lax.fori_loop(0, B, forward, 0)
    phase((turn,),)
    out_load = local(("os",), k.da, out.output)
    out_load.start()

    def backward(step, _):
        b = B - 1 - step
        at_block(b, 0, (fetch_wait, "hid"))
        phase((bwd_hidden, b),)
        phase((grad_up, b),)
        at_block(b, 1, (g_c, 1, "u"),)
        at_block(b, 0, (g_c, 0, "u"), (g_2, 1, "d"), (g_3, 1, "u"), (g_2, 1, "q0"))
        at_block(b, 0, (fetch_wait, "act"))
        phase((grad_down, b),)
        at_block(b, 1, (g_c, 1, "d"), (g_1, 1, "u"))
        at_block(b, 0, (g_c, 0, "d"), (g_1, 0, "u"), (dm_qc, 1))
        at_block(b, B - 1, (out_wait,))
        phase((bwd_second, b),)
        at_block(b, 1, (fetch_start, "hid"))
        at_block(b, 1, (g_1, 1, "d"), (dm_start, 1))
        at_block(b, 0, (g_2, 1, "q1"), (g_1, 0, "d"), (dm_start, 0), (dm_ready, 1))
        phase((grad_proj, b),)
        at_block(b, 0, (fetch_wait, "pt"))
        phase((bwd_heads, b, 0),)
        at_block(b, 0, (g_3, 1, "d"), (g_2, 1, "q2"), (g_3, 1, "q0"))
        phase((grad_qkv, b, 0),)
        at_block(b, 1, (g_c, 1, "q0"),)
        at_block(b, 0, (g_c, 0, "q0"),)
        phase((bwd_heads, b, 1),)
        at_block(b, 1, (g_1, 1, "q0"),)
        at_block(b, 0, (g_ring, 0, "u"), (g_1, 0, "q0"))
        phase((grad_qkv, b, 1),)
        at_block(b, 1, (g_c, 1, "q1"), (dm_zq, 1))
        at_block(b, 0, (g_c, 0, "q1"), (g_fly, 0, "d"), (g_3, 1, "q1"))
        phase((bwd_heads, b, 2),)
        at_block(b, 1, (fetch_start, "pt"), (fetch_start, "act"))
        at_block(b, 1, (g_1, 1, "q1"), (g_2, 1, "u"))
        at_block(b, 0, (g_4, 1, "d"), (g_1, 0, "q1"), (g_4, 1, "q0"), (dm_zq, 0))
        phase((grad_qkv, b, 2),)
        at_block(b, 1, (g_c, 1, "q2"),)
        at_block(b, 0, (g_c, 0, "q2"),)
        phase((bwd_first, b, images[: I // 2]),)
        at_block(b, 0, (g_fly, 0, "q0"), (g_5, 1, "d"), (g_5, 1, "q0"))
        phase((bwd_first, b, images[I // 2 :]),)
        at_block(b, 1, (g_1, 1, "q2"),)
        return 0

    lax.fori_loop(0, B, backward, 0)
    run((dm_start, 2),)
    g_load = local(("g",), k.xs.at[B], out.grad_tokens)
    g_load.start()
    run((g_1, 0, "q2"), (g_4, 1, "q1"), (g_2, 0, "d"), (grad_ada, 1), (g_4, 1, "u"), (g_3, 1, "q2"), (g_5, 1, "q1"), (g_2, 0, "q1"), (g_5, 1, "u"), (g_2, 0, "u"), (dm_qc, 0), (g_2, 0, "q0"), (dm_zq, 2), (dcond_send,), (dm_ready, 0), (grad_ada, 0), (g_2, 0, "q2"), (g_4, 1, "q2"), (g_3, 0, "d"), (g_5, 1, "q2"), (g_3, 0, "u"), (g_3, 0, "q1"), (g_3, 0, "q0"), (dm_qc, 2), (dcond_finish,), (g_3, 0, "q2"), (dm_ready, 2), (grad_ada, 2), (g_4, 0, "d"), (g_4, 0, "u"), (g_5, 0, "d"), (g_4, 0, "q1"), (g_4, 0, "q0"), (g_5, 0, "u"), (g_5, 0, "q1"), (all_sent,), (g_5, 0, "q2"), (g_5, 0, "q0"), (all_sent,))
    g_load.wait()
    local(("grad_cond",), k.gc.at[pl.ds(0, I)], out.grad_cond).wait()
    for b in range(B):
        for m in range(6):
            ada_copy(b, m).wait()
        for w in KINDS:
            out_copy(b, w).wait()
    assert len(index) <= N_SEMS and len(local_index) <= N_LOCAL


def finish(*refs):
    n = len(OUTPUTS)
    src, dst, high, sems = refs[:n], refs[n : 2 * n + 1], refs[2 * n + 1 : -1], refs[-1]
    B, pairs, _, R, four = src[4].shape
    W = four // 4
    D = W * pairs
    copies = []

    def copy(a, b):
        copies.append(pltpu.make_async_copy(a, b, sems.at[len(copies)]))
        copies[-1].start()

    for m in range(4):
        copy(src[m], dst[m])
    qkv, proj, up, down = high
    for b in range(B):
        for p in range(pairs):
            x = src[4][b, p].reshape(2 * R, 4 * W).astype(f32)
            for j in range(3):
                qkv[b, :, j * D + p * W : j * D + (p + 1) * W] = x[:, j * W : (j + 1) * W]
            proj[b, :, p * W : (p + 1) * W] = x[:, 3 * W :]
    copy(qkv, dst[4])
    copy(proj, dst[5])
    up[...] = src[5][...].reshape(up.shape).astype(f32)
    copy(up, dst[6])
    down[...] = src[6][...].reshape(down.shape).astype(f32)
    copy(down, dst[7])
    for c in copies:
        c.wait()


def body(F, tokens, cond, cotangent, keep_mask, w_ada, w_qkv, w_proj, w_up, w_down):
    I, L, D = tokens.shape
    B, _, FF = w_up.shape
    R = D // F // 2
    W = D // PAIRS
    T = I * L
    shapes = scratch(F, I, L, D, FF, B)
    names = tuple(shapes)
    anywhere = pl.BlockSpec(memory_space=pl.ANY)
    results = [
        jax.ShapeDtypeStruct((T, D), bf),
        jax.ShapeDtypeStruct((T, D), f32),
        jax.ShapeDtypeStruct((I, D), f32),
        jax.ShapeDtypeStruct((B, D // F, 6 * D), f32),
        jax.ShapeDtypeStruct((B, PAIRS, 2, R, 4 * W), bf),
        jax.ShapeDtypeStruct((B, 2, R, FF), bf),
        jax.ShapeDtypeStruct((B, 4, 2, R, D), bf),
    ]
    found = pl.pallas_call(
        functools.partial(kernel, names, F, I, L, D, FF, B),
        name="blocks",
        out_shape=[pltpu.VMEM(r.shape, r.dtype) for r in results] + [jax.ShapeDtypeStruct(*shapes[n]) for n in KEPT],
        in_specs=[pl.BlockSpec(memory_space=pltpu.SMEM) if n == "mask" else anywhere for n in INPUTS],
        out_specs=[anywhere] * len(OUTPUTS) + [pl.BlockSpec(memory_space=pltpu.HBM)] * len(KEPT),
        scratch_shapes=[pltpu.VMEM(*shapes[n]) for n in names]
        + [pltpu.SemaphoreType.DMA((N_SEMS,)), pltpu.SemaphoreType.DMA((N_LOCAL,))],
        compiler_params=pltpu.CompilerParams(
            collective_id=0, has_side_effects=True, vmem_limit_bytes=57 * 2**20
        ),
    )(
        tokens.reshape(T, D),
        cond,
        cotangent.reshape(T, D),
        keep_mask,
        w_ada,
        w_qkv.reshape(B, 2, R, 3 * D),
        w_proj.reshape(B, 2, R, D),
        w_up.reshape(B, 2, R, FF),
        w_down.reshape(B, 4, 2, R, D),
    )
    grads = [(B, 2 * R, 3 * D), (B, 2 * R, D), (B, 2 * R, FF), (B, 8 * R, D)]
    output, grad_tokens, grad_cond, *weights = pl.pallas_call(
        finish,
        name="finish",
        out_shape=results[:4] + [jax.ShapeDtypeStruct(s, f32) for s in grads],
        in_specs=[pl.BlockSpec(memory_space=pltpu.VMEM)] * len(OUTPUTS),
        out_specs=[anywhere] * 8,
        scratch_shapes=[pltpu.VMEM(s, f32) for s in grads] + [pltpu.SemaphoreType.DMA((8,))],
        compiler_params=pltpu.CompilerParams(vmem_limit_bytes=40 * 2**20),
    )(*found[: len(OUTPUTS)])
    if lax.axis_size("dp") > GROUP:
        first = lax.axis_index("dp") % GROUP == 0
        weights = lax.psum(tuple(jnp.where(first, w, 0.0) for w in weights), "dp")
    return (output.reshape(I, L, D), grad_tokens.reshape(I, L, D), grad_cond, *weights)


def solution(mesh):
    slots = P(("dp", "fsdp"), None, None)
    weight = P(None, "fsdp", None)
    return jax.shard_map(
        functools.partial(body, mesh.shape["fsdp"]),
        mesh=mesh,
        in_specs=(slots, P(("dp", "fsdp"), None), slots, P(("dp", "fsdp"))) + (weight,) * 5,
        out_specs=(slots, slots, P(("dp", "fsdp"), None)) + (weight,) * 5,
        check_vma=False,
    )
```
